32 devices in a mesh: ctx: 8 (over y, x, core), wsh: 4 (over z).
Axes of the slice: x: 2, y: 2, z: 4, core: 2. Of those that a mesh axis runs over, the one named last changes fastest.
Arguments:
- block_in: bfloat16 [4, 8192, 800], P('wsh', 'ctx'), may hold values from -6 to 6
- out_grad: bfloat16 [4, 8192, 800], P('wsh', 'ctx'), may hold values from -6 to 6
- segments: int32 [4, 8192], P('wsh', 'ctx'), may hold values from 0 to 127, as said below
- block_deal: int32 [64], replicated, may hold values from 0 to 63, as said below
- weight_in: bfloat16 [800, 400], P(None, 'wsh'), may hold values from -0.21875 to 0.21875
- weight_conv: bfloat16 [3, 400, 400], P(None, None, 'wsh'), may hold values from -0.1875 to 0.1875
- weight_out: bfloat16 [400, 800], P(None, 'wsh'), may hold values from -0.3125 to 0.3125
- gain_first: bfloat16 [800], P('wsh'), may hold values from 0.25 to 1.75
- shift_first: bfloat16 [800], P('wsh'), may hold values from -3 to 3
- gain_second: bfloat16 [400], P('wsh'), may hold values from 0.25 to 1.75
- shift_second: bfloat16 [400], P('wsh'), may hold values from -3 to 3
- gain_third: bfloat16 [400], P('wsh'), may hold values from 0.25 to 1.75
- shift_third: bfloat16 [400], P('wsh'), may hold values from -3 to 3
- bias_first: bfloat16 [400], P('wsh'), may hold values from -3 to 3
- bias_conv: bfloat16 [400], P('wsh'), may hold values from -3 to 3
- bias_out: bfloat16 [800], P('wsh'), may hold values from -3 to 3
Outputs:
- block_out: bfloat16 [4, 8192, 800], P('wsh', 'ctx')
- input_grad: float32 [4, 8192, 800], P('wsh', 'ctx')
- grad_weight_in: float32 [800, 400], P(None, 'wsh')
- grad_weight_conv: float32 [3, 400, 400], P(None, None, 'wsh')
- grad_weight_out: float32 [400, 800], P(None, 'wsh')
- grad_gain_first: float32 [800], P('wsh')
- grad_shift_first: float32 [800], P('wsh')
- grad_gain_second: float32 [400], P('wsh')
- grad_shift_second: float32 [400], P('wsh')
- grad_gain_third: float32 [400], P('wsh')
- grad_shift_third: float32 [400], P('wsh')
- grad_bias_first: float32 [400], P('wsh')
- grad_bias_conv: float32 [400], P('wsh')
- grad_bias_out: float32 [800], P('wsh')
The draws below stay inside these ranges and needn't reach their ends.
Inputs may be any that keep to these rules, and one draw needn't show every extreme that they name: `block_deal`: A permutation of the 64 blocks of a sequence; the slots of one device along ctx come in pairs 2q, 2q + 1 that hold blocks j and 63 - j. `segments`: read in the natural order of blocks given by block_deal, the numbers of a sequence start at 0, never fall, rise by at most one from a position to the next, and end at 127; a document may cross block and device boundaries.
All inputs are finite; a program needn't handle non-finite values.
Results may differ from the reference program's by a relative error of at most 0.0066.
Values may be sent and summed in bfloat16 or wider, within the bound.
A program may use at most 256 MiB of HBM per device.

```python
import jax
import jax.numpy as jnp
from jax import lax

D = 800
H = 400
KERNEL_TAPS = 3
DILATION_STEP = 16
BLK = 128
BPD = 8
NB = 64
LEN = 8192
SEQS = 4


def block_dealer(key):
    pair_count = NB // 2
    order = jax.random.permutation(jax.random.fold_in(key, 11), pair_count).astype(jnp.int32)
    layout = order.reshape(NB // BPD, BPD // 2)
    early = layout
    later = NB - 1 - layout
    return jnp.stack([early, later], axis=-1).reshape(NB).astype(jnp.int32)


def draw_block_deal(key, part):
    return block_dealer(key)


def draw_segments(key, part):
    dealing = block_dealer(key)
    total_len = NB * BLK
    levels = jax.random.randint(jax.random.fold_in(key, 12), (SEQS, NB), 0, 4).astype(jnp.int32)
    level_rows = jnp.repeat(levels, BLK, axis=1)
    raw_ints = jax.random.randint(jax.random.fold_in(key, 13), (SEQS, total_len), 0, 4096).astype(jnp.int32)
    place = jnp.arange(total_len, dtype=jnp.int32)[None, :]
    scores = jnp.right_shift(raw_ints, 2 * level_rows) * total_len + place
    scores = jnp.where(place == 0, 4096 * total_len, scores).astype(jnp.int32)
    unused, cuts = lax.top_k(-scores, 2 * NB - 1)
    row_ids = jnp.arange(SEQS, dtype=jnp.int32)[:, None]
    starting = jnp.zeros((SEQS, total_len), jnp.int32).at[row_ids, cuts].set(1)
    starting = starting.at[:, 0].set(1)
    natural = jnp.cumsum(starting, axis=1).astype(jnp.int32) - 1
    return natural.reshape(SEQS, NB, BLK)[:, dealing].reshape(SEQS, total_len).astype(jnp.int32)


def shard_levels(stream_key, extent, split, smallest, top_value):
    level = 1.0
    for position, shards_of in split:
        draws = jax.random.uniform(jax.random.fold_in(jax.random.fold_in(stream_key, 6), position), (shards_of,), jnp.float32, smallest / len(split), top_value / len(split))
        level = level * jnp.repeat(jnp.exp(draws), extent[position] // shards_of).reshape((-1,) + (1,) * (len(extent) - 1 - position))
    return level


def normal_values(key, shape, scale, limit, cuts=(), held_as=jnp.bfloat16):
    loudness = shard_levels(key, shape, cuts, -0.22, 0.18) if cuts else 1.0
    entries = jax.random.normal(key, shape, jnp.float32) * scale * loudness
    return jnp.minimum(jnp.maximum(entries, -limit), limit).astype(held_as)


def setup_inputs(seed: int = 0) -> dict:
    seeds = jax.random.split(jax.random.key(seed), 17)
    block_in = normal_values(seeds[0], (SEQS, LEN, D), 1.0, 6.0, ((0, 4), (1, 8)))
    out_grad = normal_values(seeds[1], (SEQS, LEN, D), 1.0, 6.0, ((0, 4), (1, 8)))
    segments = draw_segments(jax.random.fold_in(seeds[16], 71), 0)
    block_deal = draw_block_deal(jax.random.fold_in(seeds[16], 71), 0)
    weight_in = normal_values(seeds[4], (D, H), D ** -0.5, 0.21875, ((1, 4),))
    weight_conv = normal_values(seeds[5], (KERNEL_TAPS, H, H), (KERNEL_TAPS * H) ** -0.5, 0.1875, ((2, 4),))
    weight_out = normal_values(seeds[6], (H, D), H ** -0.5, 0.3125, ((1, 4),))
    gain_first = jnp.clip(1.0 + 0.15 * jax.random.normal(seeds[7], (D,), jnp.float32), 0.25, 1.75).astype(jnp.bfloat16)
    shift_first = normal_values(seeds[8], (D,), 0.5, 3.0, ((0, 4),))
    gain_second = jnp.clip(1.0 + 0.15 * jax.random.normal(seeds[9], (H,), jnp.float32), 0.25, 1.75).astype(jnp.bfloat16)
    shift_second = normal_values(seeds[10], (H,), 0.5, 3.0, ((0, 4),))
    gain_third = jnp.clip(1.0 + 0.15 * jax.random.normal(seeds[11], (H,), jnp.float32), 0.25, 1.75).astype(jnp.bfloat16)
    shift_third = normal_values(seeds[12], (H,), 0.5, 3.0, ((0, 4),))
    bias_first = normal_values(seeds[13], (H,), 0.5, 3.0, ((0, 4),))
    bias_conv = normal_values(seeds[14], (H,), 0.5, 3.0, ((0, 4),))
    bias_out = normal_values(seeds[15], (D,), 0.5, 3.0, ((0, 4),))
    return {"block_in": block_in, "out_grad": out_grad, "segments": segments, "block_deal": block_deal, "weight_in": weight_in, "weight_conv": weight_conv, "weight_out": weight_out, "gain_first": gain_first, "shift_first": shift_first, "gain_second": gain_second, "shift_second": shift_second, "gain_third": gain_third, "shift_third": shift_third, "bias_first": bias_first, "bias_conv": bias_conv, "bias_out": bias_out}


EPS = 1e-05
HIGHEST = lax.Precision.HIGHEST

@jax.custom_vjp
def low(v):
    return lax.optimization_barrier(v.astype(jnp.bfloat16)).astype(jnp.float32)

@jax.custom_vjp
def low_back(v):
    return v

def low_keep(v):
    return (low(v), None)

def low_pass(kept, grad):
    return (grad,)

def back_keep(v):
    return (v, None)

def back_low(kept, grad):
    return (low(grad),)
low.defvjp(low_keep, low_pass)
low_back.defvjp(back_keep, back_low)

def layer_norm(values, gain, shift):
    centre = lax.optimization_barrier(jnp.mean(values, -1, keepdims=True))
    centred = values - centre
    scaled = lax.rsqrt(lax.optimization_barrier(jnp.mean(centred * centred, -1, keepdims=True)) + EPS)
    return centred * scaled * gain + shift

def forward(params, inputs, seg_natural):
    weight_in, weight_conv, weight_out, gain_first, shift_first, gain_second, shift_second, gain_third, shift_third, bias_first, bias_conv, bias_out = params
    act_first = low(jax.nn.silu(layer_norm(inputs, gain_first, shift_first)))
    hidden = low_back(jnp.dot(act_first, weight_in, precision=HIGHEST) + bias_first)
    act_second = low(jax.nn.silu(layer_norm(hidden, gain_second, shift_second)))
    length = inputs.shape[0]
    positions = jnp.arange(length, dtype=jnp.int32)
    conv_sum = bias_conv
    for kernel_tap_index in range(KERNEL_TAPS):
        tap_delay = kernel_tap_index * DILATION_STEP
        shifted = jnp.pad(act_second, ((tap_delay, 0), (0, 0)))[:length]
        seg_shifted = jnp.pad(seg_natural, (tap_delay, 0))[:length]
        keeping = jnp.logical_and(seg_shifted == seg_natural, positions >= tap_delay).astype(jnp.float32)
        conv_sum = conv_sum + jnp.dot(keeping[:, None] * shifted, weight_conv[kernel_tap_index], precision=HIGHEST)
    conv_out = low_back(conv_sum)
    act_third = low(jax.nn.silu(layer_norm(conv_out, gain_third, shift_third)))
    return inputs + jnp.dot(act_third, weight_out, precision=HIGHEST) + bias_out

def reference(block_in, out_grad, segments, block_deal, weight_in, weight_conv, weight_out, gain_first, shift_first, gain_second, shift_second, gain_third, shift_third, bias_first, bias_conv, bias_out):
    params = tuple((item.astype(jnp.float32) for item in (weight_in, weight_conv, weight_out, gain_first, shift_first, gain_second, shift_second, gain_third, shift_third, bias_first, bias_conv, bias_out)))
    block_ids = jnp.arange(NB, dtype=jnp.int32)
    slot_of = jnp.zeros((NB,), jnp.int32).at[block_deal].set(block_ids)

    def to_natural(values):
        width = values.shape[-1]
        return values.reshape(NB, BLK, width)[slot_of].reshape(NB * BLK, width)

    def to_dealt(values):
        width = values.shape[-1]
        return values.reshape(NB, BLK, width)[block_deal].reshape(NB * BLK, width)

    def one_sequence(totals, item):
        seq_in, seq_grad, seq_seg = item
        inputs = to_natural(seq_in.astype(jnp.float32))
        upstream = to_natural(seq_grad.astype(jnp.float32))
        seg_natural = to_natural(seq_seg[:, None])[:, 0]

        def running(param_set, values):
            return forward(param_set, values, seg_natural)
        result, pull = jax.vjp(running, params, inputs)
        grad_params, grad_inputs = pull(upstream)
        totals = jax.tree.map(jnp.add, totals, grad_params)
        return (totals, (to_dealt(result).astype(jnp.bfloat16), to_dealt(grad_inputs)))
    zeros = tuple((jnp.zeros_like(item) for item in params))
    grads, (outputs, input_grads) = lax.scan(one_sequence, zeros, (block_in, out_grad, segments))
    return (outputs, input_grads, grads[0], grads[1], grads[2], grads[3], grads[4], grads[5], grads[6], grads[7], grads[8], grads[9], grads[10], grads[11])
```

```python
import jax
import jax.numpy as jnp
from jax import lax
from jax.experimental import pallas as pl
from jax.experimental.pallas import tpu as pltpu
from jax.sharding import PartitionSpec as P

TAPS = 3
STEP = 16
BLK = 128
EDGE = (TAPS - 1) * STEP
EPS = 1e-05
LANES = 128
MESH = pl.DeviceIdType.MESH
F32 = jnp.float32
BF16 = jnp.bfloat16


def up(value, unit):
    return -(-value // unit) * unit


class Packed:
    def __init__(self, rows, panels, width, devices):
        self.rows, self.panels, self.width = rows, panels, width
        total = rows * panels
        if width % 4 == 0 and width > 64 and LANES - width >= width // 4 and total % 80 == 0:
            main, rest, quarter = total * 4 // 5, total // 5, width // 4
            self.parts = [(0, main, 0, width, 0, 0)]
            self.parts += [(main, rest, quarter * i, quarter, rest * i, width) for i in range(4)]
            used = main
        else:
            count = max(LANES // width, 1)
            used = up(-(-total // count), 16)
            self.parts = [
                (used * i, min(used, total - used * i), 0, width, 0, width * i)
                for i in range(count)
                if used * i < total
            ]
        self.used = used
        self.size = up(used, 16 * devices)

    def packed_spans(self):
        cuts = {0, self.used}
        for row, count, _, _, at, _ in self.parts:
            cuts |= {at, at + count}
            cuts |= {at + self.rows * h - row for h in range(self.panels) if row < self.rows * h < row + count}
        cuts = sorted(cuts)
        for start, end in zip(cuts, cuts[1:]):
            inside = []
            for row, count, column, columns, at, lane in self.parts:
                if at <= start and end <= at + count:
                    source = row + start - at
                    inside.append((source % self.rows, source // self.rows, column, columns, lane))
            yield start, end - start, sorted(inside, key=lambda item: item[-1])

    def plain_spans(self):
        cuts = {0, self.rows}
        for row, count, _, _, _, _ in self.parts:
            cuts |= {edge - self.rows * h for edge in (row, row + count) for h in range(self.panels)}
        cuts = sorted(cut for cut in cuts if 0 <= cut <= self.rows)
        for start, end in zip(cuts, cuts[1:]):
            panels = []
            for h in range(self.panels):
                first = self.rows * h + start
                inside = [
                    (column, at + first - row, lane, columns)
                    for row, count, column, columns, at, lane in self.parts
                    if row <= first < row + count
                ]
                panels.append([item[1:] for item in sorted(inside)])
            yield start, end - start, panels


def chunk_of(count):
    return next(size for size in (80, 64, 48, 32, 16) if count % size == 0)


def flip(value, mask):
    bit = 1
    out = value
    while bit <= mask:
        if mask & bit:
            out = out + bit - 2 * bit * ((value // bit) % 2)
        bit *= 2
    return out


def dot(a, b, contract=(1, 0)):
    return lax.dot_general(
        a, b, (((contract[0],), (contract[1],)), ((), ())), preferred_element_type=F32
    )


def dup(v, lanes):
    return jnp.concatenate([v] * (lanes // LANES), axis=1)


def fold_rows(v):
    out = v[0:8]
    for i in range(8, v.shape[0], 8):
        out = out + v[i : i + 8]
    return out


def fold_lanes(v):
    out = v[:, 0:LANES]
    for i in range(LANES, v.shape[1], LANES):
        out = out + v[:, i : i + LANES]
    return out


def total_rows(v):
    return jnp.sum(v, 0, keepdims=True)


class Copies:
    def __init__(self, send, recv):
        self.send, self.recv, self.count, self.open = send, recv, 0, []

    def start(self, source, target, device):
        copy = pltpu.make_async_remote_copy(
            src_ref=source,
            dst_ref=target,
            send_sem=self.send.at[self.count],
            recv_sem=self.recv.at[self.count],
            device_id=device,
            device_id_type=MESH,
        )
        self.count += 1
        self.open.append(copy)
        copy.start()
        return copy


LG = 256
FB = 80
CHUNKS = 2


def kernel(cfg, *refs):
    C, W, J, D, H = cfg["C"], cfg["W"], cfg["J"], cfg["D"], cfg["H"]
    forms, bases = cfg["forms"], cfg["bases"]
    width, vec_at = cfg["width"], cfg["vec_at"]
    half_chips = C // 2
    R = J * BLK
    CW = R // CHUNKS
    CJ = J // CHUNKS
    EW = CJ * EDGE
    (slots, tgt_ref, x_hbm, og_hbm, seg_ref, vec_ref, wi_ref, wc_ref, wo_ref) = refs[:9]
    (bo_hbm, ig_hbm, gi_ref, gc_ref, go_ref, vo_ref) = refs[9:15]
    (
        x_v, og_v, mu1, sc1, a1, h2, mu2, sc2, a2, b1, b2, a3, gv, gh, big, c3, g3,
        m1, m2, k1, k2, w_in, w_inT, w_cv, w_cvT, w_out, wps, vecb, sa, ta, ha, pt, nh,
        psg, rx1, rx2, s2, rx3, fo, p8, p4, acc8, acc4, vx, vr, vs, vz,
        lsem, ssem, rsem,
    ) = refs[15:]

    c = lax.axis_index("ctx")
    z = lax.axis_index("wsh")
    k = c % 2
    p = c // 2
    slot_in_order = k * half_chips + p
    sibling = (flip(c, 1), z)
    chips = [(flip(c, 2 * e), z) for e in range(1, half_chips)]
    planes = [(c, flip(z, d)) for d in range(1, W)]
    copies = Copies(ssem, rsem)
    shards = range(W)

    def local(i, source, target):
        copy = pltpu.make_async_copy(source, target, lsem.at[i])
        copy.start()
        return copy

    def loop(count, body):
        lax.fori_loop(0, count, lambda i, carry: (body(i), carry)[1], 0)

    bar = pltpu.get_barrier_semaphore()
    for m in range(1, C):
        pl.semaphore_signal(bar, inc=1, device_id=(flip(c, m), z), device_id_type=MESH)
    for device in planes:
        pl.semaphore_signal(bar, inc=1, device_id=device, device_id_type=MESH)
    x_copy = local(0, x_hbm, x_v)
    og_copy = local(1, og_hbm, og_v)
    sa[pl.ds(pl.multiple_of(c * J, 8), J)] = seg_ref[...]
    vecb[0] = vec_ref[...]
    acc8[...] = jnp.zeros_like(acc8)
    acc4[...] = jnp.zeros_like(acc4)
    vx[...] = jnp.zeros_like(vx)

    def pack(name, take, put, copies_of, dtype):
        form, base = forms[name], bases[name]
        for start, count, inside in form.packed_spans():
            size = chunk_of(count)

            def step(i, start=start, inside=inside, size=size):
                shift = i * size
                to = pl.ds(pl.multiple_of(base + start + shift, 16), size)
                for s in copies_of:
                    parts, lane = [], 0
                    for row, panel, column, columns, at in inside:
                        rows = pl.ds(pl.multiple_of(row + shift, 16), size)
                        parts.append(take(s, panel, rows, slice(column, column + columns)))
                        lane = at + columns
                    if lane < LANES:
                        parts.append(jnp.zeros((size, LANES - lane), dtype))
                    put(s, to, jnp.concatenate(parts, axis=1))

            loop(count // size, step)
        if form.size > form.used:
            for s in copies_of:
                rest = pl.ds(base + form.used, form.size - form.used)
                put(s, rest, jnp.zeros((form.size - form.used, LANES), dtype))

    def moved(columns, by):
        return slice(columns.start + by, columns.stop + by)

    def put_own(s, rows, value):
        wps[0, rows, :] = value

    own_shard = {
        "in": lambda s, panel, rows, columns: w_in[rows, columns],
        "conv": lambda s, panel, rows, columns: wc_ref[panel, rows, columns],
        "out": lambda s, panel, rows, columns: wo_ref[rows, moved(columns, width * panel)],
    }
    w_in[:, 0:width] = wi_ref[...].T
    for name, take in own_shard.items():
        pack(name, take, put_own, (0,), BF16)
    pl.semaphore_wait(bar, C - 1 + W - 1)

    vec_sends = [copies.start(vecb.at[0], vecb.at[d + 1], planes[d]) for d in range(W - 1)]

    def part(name, order):
        share = forms[name].size // C
        return pl.ds(pl.multiple_of(bases[name] + order * share, 16), share)

    def half(name, which):
        share = forms[name].size // 2
        return pl.ds(pl.multiple_of(bases[name] + which * share, 16), share)

    def z_send(name):
        rows = part(name, slot_in_order)
        return [copies.start(wps.at[0, rows], wps.at[d + 1, rows], planes[d]) for d in range(W - 1)]

    def plane_send(name, before):
        for copy in before:
            copy.wait_recv()
        there = wps.at[pl.ds(1, W - 1), part(name, slot_in_order)]
        return [copies.start(there, there, device) for device in chips]

    def sibling_send(name, before):
        for copy in before:
            copy.wait_recv()
        there = wps.at[pl.ds(1, W - 1), half(name, k)]
        return copies.start(there, there, sibling)

    w_z = {name: z_send(name) for name in forms}
    own_seg = sa.at[pl.ds(pl.multiple_of(c * J, 8), J)]
    seg_sends = [copies.start(own_seg, own_seg, (flip(c, m), z)) for m in range(1, C)]

    def unpack(name, target, stacked=False):
        form, base = forms[name], bases[name]
        for start, count, panels in form.plain_spans():
            size = chunk_of(count)
            groups = [[panel] for panel in panels] if stacked else [panels]
            for g, group in enumerate(groups):

                def step(i, first=g * form.rows + start, group=group, size=size):
                    shift = i * size
                    parts = [
                        wps[flip(z, s), pl.ds(pl.multiple_of(base + row + shift, 16), size), lane : lane + columns]
                        for s in shards
                        for panel in group
                        for row, lane, columns in panel
                    ]
                    target[pl.ds(pl.multiple_of(first + shift, 16), size), :] = jnp.concatenate(parts, axis=1)

                loop(count // size, step)

    def lanes_at(start):
        return pl.ds(pl.multiple_of(start, LG), LG)

    def blocks(n):
        return [slice(f, f + FB) for f in range(0, n, FB)]

    x_copy.wait()
    og_copy.wait()

    def first_stats(i):
        lanes = lanes_at(i * LG)
        acc = jnp.zeros((8, LG), F32)
        for f in blocks(D):
            acc += fold_rows(x_v[f, lanes].astype(F32))
            acc8[2, f] += fold_lanes(og_v[f, lanes].astype(F32))
        mean = total_rows(acc) * (1.0 / D)
        acc = jnp.zeros((8, LG), F32)
        for f in blocks(D):
            centred = x_v[f, lanes].astype(F32) - mean
            acc += fold_rows(centred * centred)
        mu1[:, lanes] = mean
        sc1[:, lanes] = lax.rsqrt(total_rows(acc) * (1.0 / D) + EPS)

    loop(R // LG, first_stats)

    for copy in vec_sends:
        copy.wait_recv()
    vecs = [vecb[flip(z, s)].astype(F32) for s in shards]
    narrow = jnp.concatenate([v[:, :width] for v in vecs], axis=1).T
    for i in range(6):
        scale = 0.5 if i < 4 else 1.0
        p4[i] = jnp.broadcast_to(narrow[:, 4 + i : 5 + i] * scale, (H, LANES))
    broad = jnp.concatenate(
        [
            jnp.concatenate([v[at + h : at + h + 1, :width] for v in vecs for h in range(2)], axis=1)
            for at in (0, 2, 10)
        ]
        + [jnp.zeros((5, D), F32)],
        axis=0,
    ).T
    for i in range(3):
        scale = 0.5 if i < 2 else 1.0
        p8[i] = jnp.broadcast_to(broad[:, i : i + 1] * scale, (D, LANES))

    def first_act(i):
        lanes = lanes_at(i * LG)
        mean, scaled = mu1[:, lanes], sc1[:, lanes]
        for f in blocks(D):
            normed = (x_v[f, lanes].astype(F32) - mean) * scaled
            pre = normed * dup(p8[0, f], LG) + dup(p8[1, f], LG)
            a1[f, lanes] = (pre * jnp.tanh(pre) + pre).astype(BF16)

    w_plane = {"in": plane_send("in", w_z["in"])}
    loop(R // LG // 2, first_act)
    w_plane["conv"] = plane_send("conv", w_z["conv"])
    loop(R // LG // 2, lambda i: first_act(i + R // LG // 2))
    w_plane["out"] = plane_send("out", w_z["out"])
    w_sib = {"in": sibling_send("in", w_plane["in"])}
    w_sib["in"].wait_recv()
    unpack("in", w_in)
    w_inT[...] = w_in[...].T

    def second(chunk):
        here = slice(chunk * CW, (chunk + 1) * CW)
        h2[:, here] = dot(w_inT[...], a1[:, here])

        def step(i):
            lanes = lanes_at(chunk * CW + i * LG)
            acc = jnp.zeros((8, LG), F32)
            for f in blocks(H):
                value = h2[f, lanes] + dup(p4[4, f], LG)
                h2[f, lanes] = value
                acc += fold_rows(value)
            mean = total_rows(acc) * (1.0 / H)
            acc = jnp.zeros((8, LG), F32)
            for f in blocks(H):
                centred = h2[f, lanes] - mean
                acc += fold_rows(centred * centred)
            scaled = lax.rsqrt(total_rows(acc) * (1.0 / H) + EPS)
            mu2[:, lanes] = mean
            sc2[:, lanes] = scaled
            for f in blocks(H):
                normed = (h2[f, lanes] - mean) * scaled
                pre = normed * dup(p4[0, f], LG) + dup(p4[1, f], LG)
                a2[f, lanes] = (pre * jnp.tanh(pre) + pre).astype(BF16)

        loop(CW // LG, step)

    def edge_send(store, source, chunk, first):
        lanes = slice(chunk * EW, (chunk + 1) * EW)
        store[c, :, lanes] = jnp.concatenate(
            [source[:, j * BLK + first : j * BLK + first + EDGE] for j in range(chunk * CJ, (chunk + 1) * CJ)], axis=1
        )
        there = store.at[c, :, lanes]
        return [copies.start(there, there, device) for device in chips], copies.start(there, there, sibling)

    def edge_forward(store, sends, chunk):
        lanes = slice(chunk * EW, (chunk + 1) * EW)
        passed = []
        for e in range(1, half_chips):
            there = store.at[flip(c, 2 * e), :, lanes]
            sends[e - 1].wait_recv()
            passed.append(copies.start(there, there, sibling))
        return passed

    def edge_take(store, waits, row, target):
        for copy in waits:
            copy.wait_recv()
        wanted = tgt_ref[row : row + 1, :]
        total = jnp.zeros((H, J * EDGE), F32)
        for device in range(C):
            ids = lax.broadcasted_iota(jnp.int32, (J * EDGE, J * EDGE), 0) + device * J * EDGE
            chosen = jnp.where(ids == wanted, 1.0, 0.0).astype(BF16)
            total += dot(store[device], chosen)
        target[...] = total.astype(BF16)

    t_first, t_near, t_passed = [], [], []
    for chunk in range(CHUNKS):
        second(chunk)
        sends, near = edge_send(ta, a2, chunk, BLK - EDGE)
        t_first.append(sends)
        t_near.append(near)
    w_sib["conv"] = sibling_send("conv", w_plane["conv"])
    w_sib["out"] = sibling_send("out", w_plane["out"])

    for copy in seg_sends:
        copy.wait_recv()
    own = sa[pl.ds(pl.multiple_of(c * J, 8), J)].astype(F32)

    def neighbour(first):
        out = []
        for j in range(J):
            row = sa[pl.ds(slots[first + j], 1), :].astype(F32)
            out.append(jnp.where(slots[first + 2 * J + j] > 0, row, -1.0))
        return jnp.concatenate(out, axis=0)

    before, behind = neighbour(0), neighbour(J)
    cut = BLK - STEP

    def same(a, b):
        return jnp.where(a == b, 1.0, 0.0)

    keep_1 = same(own, jnp.concatenate([before[:, cut:], own[:, :cut]], axis=1))
    keep_2 = same(own, jnp.concatenate([before[:, BLK - EDGE :], own[:, : BLK - EDGE]], axis=1))
    next_1 = same(behind[:, :EDGE], jnp.concatenate([own[:, cut:], behind[:, :STEP]], axis=1))
    next_2 = same(behind[:, :EDGE], own[:, BLK - EDGE :])
    for target, mask, size in ((m1, keep_1, BLK), (m2, keep_2, BLK), (k1, next_1, EDGE), (k2, next_2, EDGE)):
        for j in range(J):
            target[:, j * size : (j + 1) * size] = jnp.broadcast_to(mask[j : j + 1], (16, size)).astype(BF16)

    def tall(mask):
        return jnp.concatenate([mask] * (H // 16), axis=0)

    w_sib["conv"].wait_recv()
    unpack("conv", w_cv, stacked=True)
    for tap in range(TAPS):
        w_cvT[tap] = w_cv[tap * H : (tap + 1) * H].T
    w_sib["out"].wait_recv()
    unpack("out", w_out)
    for chunk in range(CHUNKS):
        t_passed += edge_forward(ta, t_first[chunk], chunk)
    for chunk in range(CHUNKS):
        here = slice(chunk * CW, (chunk + 1) * CW)
        g3[:, here] = dot(w_out[...], og_v[:, here])
    edge_take(ta, t_near + t_passed, 0, pt)

    def third(chunk):
        here = slice(chunk * CW, (chunk + 1) * CW)
        for j in range(chunk * CJ, (chunk + 1) * CJ):
            tile, edge = slice(j * BLK, (j + 1) * BLK), slice(j * EDGE, (j + 1) * EDGE)
            own, prev = a2[:, tile], pt[:, edge]
            b1[:, tile] = jnp.concatenate([prev[:, STEP:], own[:, :cut]], axis=1) * tall(m1[:, tile])
            b2[:, tile] = jnp.concatenate([prev, own[:, : BLK - EDGE]], axis=1) * tall(m2[:, tile])
        c3[:, here] = dot(w_cvT[0], a2[:, here]) + dot(w_cvT[1], b1[:, here]) + dot(w_cvT[2], b2[:, here])

        def step(i):
            lanes = lanes_at(chunk * CW + i * LG)
            acc = jnp.zeros((8, LG), F32)
            for f in blocks(H):
                value = c3[f, lanes] + dup(p4[5, f], LG)
                c3[f, lanes] = value
                acc += fold_rows(value)
            mean = total_rows(acc) * (1.0 / H)
            acc = jnp.zeros((8, LG), F32)
            for f in blocks(H):
                centred = c3[f, lanes] - mean
                acc += fold_rows(centred * centred)
            scaled = lax.rsqrt(total_rows(acc) * (1.0 / H) + EPS)
            first, second = jnp.zeros((8, LG), F32), jnp.zeros((8, LG), F32)
            for f in blocks(H):
                normed = (c3[f, lanes] - mean) * scaled
                gain = dup(p4[2, f], LG)
                pre = normed * gain + dup(p4[3, f], LG)
                t = jnp.tanh(pre)
                a3[f, lanes] = (pre * t + pre).astype(BF16)
                upstream = g3[f, lanes] * ((1.0 + t) * (1.0 + pre * (1.0 - t)))
                acc4[2, f] += fold_lanes(upstream * normed)
                acc4[3, f] += fold_lanes(upstream)
                upstream = upstream * gain
                g3[f, lanes] = upstream
                first += fold_rows(upstream)
                second += fold_rows(upstream * normed)
            first, second = total_rows(first) * (1.0 / H), total_rows(second) * (1.0 / H)
            for f in blocks(H):
                normed = (c3[f, lanes] - mean) * scaled
                grad = (scaled * (g3[f, lanes] - first - normed * second)).astype(BF16)
                gv[f, lanes] = grad
                acc4[5, f] += fold_lanes(grad.astype(F32))

        loop(CW // LG, step)

    h_first, h_near, h_passed = [], [], []
    for chunk in range(CHUNKS):
        third(chunk)
        sends, near = edge_send(ha, gv, chunk, 0)
        h_first.append(sends)
        h_near.append(near)

    taps_at = (c3, g3, big)
    whole_grad = {
        "in": lambda s, panel, rows, columns: big[rows, moved(columns, width * s)],
        "conv": lambda s, panel, rows, columns: taps_at[panel][rows, moved(columns, width * s)],
        "out": lambda s, panel, rows, columns: big[rows, moved(columns, width * (forms["out"].panels * s + panel))],
    }

    def put_grad(s, rows, value):
        psg[flip(z, s), rows, :] = value.astype(BF16)

    def pack_grad(name):
        pack(name, whole_grad[name], put_grad, shards, F32)

    def halved(name):
        return pl.ds(bases[name] // 2, forms[name].size // 2)

    def shared(name):
        return pl.ds(bases[name] // C, forms[name].size // C)

    def reduce_1(name):
        return copies.start(psg.at[:, half(name, 1 - k)], rx1.at[:, halved(name)], sibling)

    def tiles(rows, body):
        size = chunk_of(rows)
        loop(rows // size, lambda i: body(pl.multiple_of(i * size, 16), size))

    def reduce_2(name, before):
        before.wait_recv()
        form = forms[name]
        first, mine = bases[name] // 2, bases[name] + k * (form.size // 2)

        def add(at, size):
            to = pl.ds(pl.multiple_of(first + at, 16), size)
            here = pl.ds(pl.multiple_of(mine + at, 16), size)
            for d in range(W):
                psg[d, here] = (psg[d, here].astype(F32) + rx1[d, to].astype(F32)).astype(BF16)

        tiles(form.size // 2, add)
        share = form.size // C
        sends = []
        for e, device in enumerate(chips):
            rows = pl.ds(pl.multiple_of(mine + flip(p, e + 1) * share, 16), share)
            sends.append(copies.start(psg.at[:, rows], rx2.at[e, :, shared(name)], device))
        return sends

    def reduce_3(name, before):
        for copy in before:
            copy.wait_recv()
        share = forms[name].size // C
        first, mine = bases[name] // C, bases[name] + slot_in_order * share

        def add(at, size):
            to = pl.ds(pl.multiple_of(first + at, 16), size)
            here = pl.ds(pl.multiple_of(mine + at, 16), size)
            for d in range(W):
                total = psg[d, here].astype(F32)
                for e in range(half_chips - 1):
                    total = total + rx2[e, d, to].astype(F32)
                s2[d, to] = total.astype(BF16)

        tiles(share, add)
        return [copies.start(s2.at[d + 1, shared(name)], rx3.at[d, shared(name)], planes[d]) for d in range(W - 1)]

    def reduce_4(name, before):
        for copy in before:
            copy.wait_recv()
        share = forms[name].size // C
        first, mine = bases[name] // C, bases[name] + slot_in_order * share

        def add(at, size):
            to = pl.ds(pl.multiple_of(first + at, 16), size)
            total = s2[0, to].astype(F32)
            for d in range(W - 1):
                total = total + rx3[d, to].astype(F32)
            fo[pl.ds(pl.multiple_of(mine + at, 16), size)] = total

        tiles(share, add)
        there = fo.at[part(name, slot_in_order)]
        return [copies.start(there, there, device) for device in chips]

    def reduce_5(name, before):
        for copy in before:
            copy.wait_recv()
        there = fo.at[half(name, k)]
        return copies.start(there, there, sibling)

    def finish(name, before, target):
        before.wait_recv()
        form, base = forms[name], bases[name]
        pieces = []
        for start, count, panels in form.plain_spans():
            values = [
                [fo[base + row : base + row + count, lane : lane + columns] for row, lane, columns in panel]
                for panel in panels
            ]
            if name == "conv":
                for tap, parts in enumerate(values):
                    target[tap, start : start + count] = jnp.concatenate(parts, axis=1)
            else:
                pieces.append(jnp.concatenate(sum(values, []), axis=1))
                if name == "out":
                    target[start : start + count] = pieces[-1]
        if name == "in":
            target[...] = jnp.concatenate(pieces, axis=0).T

    big[0:H, 0:D] = dot(a3[...], og_v[...], (1, 1))
    pack_grad("out")
    g_out = reduce_1("out")
    for tap, source in enumerate((a2, b1, b2)):
        taps_at[tap][0:H, 0:H] = dot(source[...], gv[...], (1, 1))
    pack_grad("conv")
    g_conv = reduce_1("conv")
    for chunk in range(CHUNKS):
        h_passed += edge_forward(ha, h_first[chunk], chunk)
    g_out = reduce_2("out", g_out)
    g_conv = reduce_2("conv", g_conv)
    edge_take(ha, h_near + h_passed, 1, nh)

    def second_back(chunk):
        here = slice(chunk * CW, (chunk + 1) * CW)
        for j in range(chunk * CJ, (chunk + 1) * CJ):
            tile, edge = slice(j * BLK, (j + 1) * BLK), slice(j * EDGE, (j + 1) * EDGE)
            own, late = gv[:, tile], nh[:, edge]
            shifted = (late * tall(k1[:, edge]))[:, :STEP]
            b1[:, tile] = jnp.concatenate([(own * tall(m1[:, tile]))[:, STEP:], shifted], axis=1)
            shifted = late * tall(k2[:, edge])
            b2[:, tile] = jnp.concatenate([(own * tall(m2[:, tile]))[:, EDGE:], shifted], axis=1)
        c3[:, here] = (
            dot(w_cv[0:H], gv[:, here]) + dot(w_cv[H : 2 * H], b1[:, here]) + dot(w_cv[2 * H : 3 * H], b2[:, here])
        )

        def step(i):
            lanes = lanes_at(chunk * CW + i * LG)
            mean, scaled = mu2[:, lanes], sc2[:, lanes]
            first, second = jnp.zeros((8, LG), F32), jnp.zeros((8, LG), F32)
            for f in blocks(H):
                normed = (h2[f, lanes] - mean) * scaled
                gain = dup(p4[0, f], LG)
                pre = normed * gain + dup(p4[1, f], LG)
                t = jnp.tanh(pre)
                upstream = c3[f, lanes] * ((1.0 + t) * (1.0 + pre * (1.0 - t)))
                acc4[0, f] += fold_lanes(upstream * normed)
                acc4[1, f] += fold_lanes(upstream)
                upstream = upstream * gain
                c3[f, lanes] = upstream
                first += fold_rows(upstream)
                second += fold_rows(upstream * normed)
            first, second = total_rows(first) * (1.0 / H), total_rows(second) * (1.0 / H)
            for f in blocks(H):
                normed = (h2[f, lanes] - mean) * scaled
                grad = (scaled * (c3[f, lanes] - first - normed * second)).astype(BF16)
                gh[f, lanes] = grad
                acc4[4, f] += fold_lanes(grad.astype(F32))

        loop(CW // LG, step)

    for chunk in range(CHUNKS):
        second_back(chunk)
    big[:, 0:H] = dot(a1[...], gh[...], (1, 1))
    pack_grad("in")
    g_in = reduce_1("in")
    g_out = reduce_3("out", g_out)
    for side in range(D // H):
        w_cvT[side] = w_out[:, side * H : (side + 1) * H].T

    def first_back(chunk):
        here = slice(chunk * CW, (chunk + 1) * CW)
        big[:, here] = dot(w_in[...], gh[:, here])

        def step(i):
            lanes = lanes_at(chunk * CW + i * LG)
            mean, scaled = mu1[:, lanes], sc1[:, lanes]
            first, second = jnp.zeros((8, LG), F32), jnp.zeros((8, LG), F32)
            for f in blocks(D):
                normed = (x_v[f, lanes].astype(F32) - mean) * scaled
                gain = dup(p8[0, f], LG)
                pre = normed * gain + dup(p8[1, f], LG)
                t = jnp.tanh(pre)
                upstream = big[f, lanes] * ((1.0 + t) * (1.0 + pre * (1.0 - t)))
                acc8[0, f] += fold_lanes(upstream * normed)
                acc8[1, f] += fold_lanes(upstream)
                upstream = upstream * gain
                big[f, lanes] = upstream
                first += fold_rows(upstream)
                second += fold_rows(upstream * normed)
            first, second = total_rows(first) * (1.0 / D), total_rows(second) * (1.0 / D)
            for f in blocks(D):
                normed = (x_v[f, lanes].astype(F32) - mean) * scaled
                grad = scaled * (big[f, lanes] - first - normed * second)
                big[f, lanes] = og_v[f, lanes].astype(F32) + grad

        loop(CW // LG, step)
        return local(2 + chunk, big.at[:, here], ig_hbm.at[:, here])

    def last(chunk):
        here = slice(chunk * CW, (chunk + 1) * CW)
        for side, store in enumerate((c3, g3)):
            store[:, 0:CW] = dot(w_cvT[side], a3[:, here])

            def step(i, side=side, store=store):
                lanes, at = lanes_at(chunk * CW + i * LG), lanes_at(i * LG)
                for f in blocks(H):
                    to = slice(side * H + f.start, side * H + f.stop)
                    value = store[f, at] + dup(p8[2, to], LG)
                    x_v[to, lanes] = (x_v[to, lanes].astype(F32) + value).astype(BF16)

            loop(CW // LG, step)
        return local(4 + chunk, x_v.at[:, here], bo_hbm.at[:, here])

    out_copies = [first_back(0)]
    g_in = reduce_2("in", g_in)
    g_conv = reduce_3("conv", g_conv)
    out_copies.append(first_back(1))

    def row_sums(group, i, scale):
        return jnp.sum((acc8 if group == 8 else acc4)[i].T, 0, keepdims=True) * scale

    for (group, i, count, scale), at in vec_at:
        value = row_sums(group, i, scale)
        for t in range(-(-count // LANES)):
            size = min(LANES, count - t * LANES)
            vx[at + t : at + t + 1, 0:size] = value[:, t * LANES : t * LANES + size]
    vr[c] = vx[...]
    v_sends = [copies.start(vr.at[c], vr.at[c], (flip(c, m), z)) for m in range(1, C)]
    g_in = reduce_3("in", g_in)
    g_out = reduce_4("out", g_out)
    g_conv = reduce_4("conv", g_conv)
    out_copies.append(last(0))
    for copy in v_sends:
        copy.wait_recv()
    total = vr[0]
    for m in range(1, C):
        total = total + vr[m]
    vs[...] = total
    z_sends = [copies.start(vs, vz.at[d], planes[d]) for d in range(W - 1)]
    g_in = reduce_4("in", g_in)
    out_copies.append(last(1))
    g_out = reduce_5("out", g_out)
    g_conv = reduce_5("conv", g_conv)
    g_in = reduce_5("in", g_in)
    finish("out", g_out, go_ref)
    finish("conv", g_conv, gc_ref)
    for copy in z_sends:
        copy.wait_recv()
    total = vs[...]
    for d in range(W - 1):
        total = total + vz[d]
    vx[...] = total
    for row, ((_, _, count, _), at) in enumerate(vec_at):
        whole = jnp.concatenate([vx[at + t : at + t + 1] for t in range(-(-count // LANES))], axis=1)
        share = count // W
        mine = jnp.zeros((1, share), F32)
        for s in shards:
            mine = jnp.where(z == s, whole[:, s * share : (s + 1) * share], mine)
        vo_ref[row : row + 1, 0:share] = mine
    finish("in", g_in, gi_ref)
    for copy in copies.open:
        copy.wait_send()
    for copy in out_copies:
        copy.wait()


def on_device(
    block_in, out_grad, segments, block_deal, weight_in, weight_conv, weight_out,
    gain_first, shift_first, gain_second, shift_second, gain_third, shift_third, bias_first, bias_conv, bias_out,
):
    C, W = lax.axis_size("ctx"), lax.axis_size("wsh")
    _, rows, D = block_in.shape
    width = weight_in.shape[1]
    H = width * W
    panels = weight_out.shape[1] // width
    J = rows // BLK
    blocks = J * C
    forms = {
        "in": Packed(D, 1, width, C),
        "conv": Packed(H, TAPS, width, C),
        "out": Packed(H, panels, width, C),
    }
    bases, total = {}, 0
    for name, form in forms.items():
        bases[name] = total
        total += form.size

    device = lax.axis_index("ctx")
    mine = lax.dynamic_slice_in_dim(block_deal, device * J, J)
    wanted = jnp.concatenate([mine - 1, mine + 1])
    ids = jnp.arange(blocks, dtype=jnp.int32)
    found = jnp.sum(jnp.where(block_deal[None, :] == wanted[:, None], ids[None, :], 0), axis=1)
    there = jnp.logical_and(wanted >= 0, wanted < blocks)
    slots = jnp.concatenate([found, there.astype(jnp.int32)]).astype(jnp.int32)
    places = found.reshape(2, J, 1) * EDGE + jnp.arange(EDGE, dtype=jnp.int32)
    places = jnp.where(there.reshape(2, J, 1), places, -1).reshape(2, J * EDGE)

    vectors = [
        gain_first, shift_first, gain_second, shift_second, gain_third, shift_third, bias_first, bias_conv, bias_out,
    ]
    vec = jnp.concatenate([v.reshape(-1, width) for v in vectors], axis=0)
    vec = jnp.pad(vec, ((0, 16 - vec.shape[0]), (0, LANES - width)))

    vec_at, at = [], 0
    for item in [(8, 0, D, 0.5), (8, 1, D, 0.5), (8, 2, D, 1.0)] + [
        (4, i, H, 0.5 if i < 4 else 1.0) for i in range(6)
    ]:
        vec_at.append((item, at))
        at += -(-item[2] // LANES)
    v_rows = up(at, 8)
    cfg = {
        "C": C, "W": W, "J": J, "D": D, "H": H, "forms": forms, "bases": bases, "width": width, "vec_at": vec_at,
    }
    R = rows
    others = max(C // 2 - 1, 1)
    n_copies = (
        3 * ((W - 1) + (C // 2 - 1) + 1) + (W - 1) + (C - 1) + 2 * CHUNKS * (2 * (C // 2 - 1) + 1)
        + 3 * (2 * (C // 2 - 1) + (W - 1) + 2) + (C - 1) + (W - 1)
    )
    vmem = pltpu.VMEM
    scratch = [
        vmem((D, R), BF16),
        vmem((D, R), BF16),
        vmem((1, R), F32),
        vmem((1, R), F32),
        vmem((D, R), BF16),
        vmem((H, R), F32),
        vmem((1, R), F32),
        vmem((1, R), F32),
        vmem((H, R), BF16),
        vmem((H, R), BF16),
        vmem((H, R), BF16),
        vmem((H, R), BF16),
        vmem((H, R), BF16),
        vmem((H, R), BF16),
        vmem((D, R), F32),
        vmem((H, R), F32),
        vmem((H, R), F32),
        vmem((16, R), BF16),
        vmem((16, R), BF16),
        vmem((16, J * EDGE), BF16),
        vmem((16, J * EDGE), BF16),
        vmem((D, H), BF16),
        vmem((H, D), BF16),
        vmem((TAPS * H, H), BF16),
        vmem((TAPS, H, H), BF16),
        vmem((H, D), BF16),
        vmem((W, total, LANES), BF16),
        vmem((W, 16, LANES), BF16),
        vmem((blocks, BLK), jnp.int32),
        vmem((C, H, J * EDGE), BF16),
        vmem((C, H, J * EDGE), BF16),
        vmem((H, J * EDGE), BF16),
        vmem((H, J * EDGE), BF16),
        vmem((W, total, LANES), BF16),
        vmem((W, total // 2, LANES), BF16),
        vmem((others, W, total // C, LANES), BF16),
        vmem((W, total // C, LANES), BF16),
        vmem((W - 1, total // C, LANES), BF16),
        vmem((total, LANES), F32),
        vmem((3, D, LANES), F32),
        vmem((6, H, LANES), F32),
        vmem((3, D, LANES), F32),
        vmem((6, H, LANES), F32),
        vmem((v_rows, LANES), F32),
        vmem((C, v_rows, LANES), F32),
        vmem((v_rows, LANES), F32),
        vmem((W - 1, v_rows, LANES), F32),
        pltpu.SemaphoreType.DMA((6,)),
        pltpu.SemaphoreType.DMA((n_copies,)),
        pltpu.SemaphoreType.DMA((n_copies,)),
    ]
    any_spec = pl.BlockSpec(memory_space=pl.ANY)
    vmem_spec = pl.BlockSpec(memory_space=pltpu.VMEM)
    flat, tree = jax.tree.flatten(scratch)

    def run(*refs):
        kernel(cfg, *refs[:15], *jax.tree.unflatten(tree, refs[15:]))

    macs = R * (2 * D * H + TAPS * H * H) * 3
    bo, ig, gi, gc, go, vo = pl.pallas_call(
        run,
        out_shape=(
            jax.ShapeDtypeStruct((D, R), BF16),
            jax.ShapeDtypeStruct((D, R), F32),
            jax.ShapeDtypeStruct((width, D), F32),
            jax.ShapeDtypeStruct((TAPS, H, width), F32),
            jax.ShapeDtypeStruct((H, panels * width), F32),
            jax.ShapeDtypeStruct((16, up(panels * width, LANES)), F32),
        ),
        in_specs=[pl.BlockSpec(memory_space=pltpu.SMEM), vmem_spec, any_spec, any_spec] + [vmem_spec] * 5,
        out_specs=(any_spec, any_spec, vmem_spec, vmem_spec, vmem_spec, vmem_spec),
        scratch_shapes=flat,
        compiler_params=pltpu.CompilerParams(
            collective_id=0, has_side_effects=True, vmem_limit_bytes=62 * 2**20
        ),
        cost_estimate=pl.CostEstimate(
            flops=2 * macs, bytes_accessed=10 * R * D, transcendentals=2 * R * (D + 2 * H)
        ),
        name="block",
    )(
        slots,
        places,
        block_in[0].T,
        out_grad[0].T,
        segments.reshape(J, BLK),
        vec,
        weight_in.T,
        weight_conv,
        weight_out,
    )

    def own_share(index):
        return vo[index, : vec_at[index][0][2] // W]

    return (
        bo.T[None],
        ig.T[None],
        gi.T,
        gc,
        go,
        own_share(0), own_share(1), own_share(3), own_share(4), own_share(5), own_share(6),
        own_share(7), own_share(8), own_share(2),
    )


def solution(mesh):
    in_specs = (
        P("wsh", "ctx", None), P("wsh", "ctx", None), P("wsh", "ctx"), P(),
        P(None, "wsh"), P(None, None, "wsh"), P(None, "wsh"),
    ) + (P("wsh"),) * 9
    out_specs = (
        P("wsh", "ctx", None), P("wsh", "ctx", None),
        P(None, "wsh"), P(None, None, "wsh"), P(None, "wsh"),
    ) + (P("wsh"),) * 9
    return jax.shard_map(
        on_device, mesh=mesh, in_specs=in_specs, out_specs=out_specs, check_vma=False
    )
```

```python
import jax
import jax.numpy as jnp
from jax import lax
from jax.experimental import pallas as pl
from jax.experimental.pallas import tpu as pltpu
from jax.sharding import PartitionSpec as P

TAPS = 3
STEP = 16
BLK = 128
EDGE = (TAPS - 1) * STEP
EPS = 1e-05
LANES = 128
MESH = pl.DeviceIdType.MESH
F32 = jnp.float32
BF16 = jnp.bfloat16


def up(value, unit):
    return -(-value // unit) * unit


class Packed:
    def __init__(self, rows, panels, width, devices):
        self.rows, self.panels, self.width = rows, panels, width
        total = rows * panels
        if width % 4 == 0 and width > 64 and LANES - width >= width // 4 and total % 80 == 0:
            main, rest, quarter = total * 4 // 5, total // 5, width // 4
            self.parts = [(0, main, 0, width, 0, 0)]
            self.parts += [(main, rest, quarter * i, quarter, rest * i, width) for i in range(4)]
            used = main
        else:
            count = max(LANES // width, 1)
            used = up(-(-total // count), 16)
            self.parts = [
                (used * i, min(used, total - used * i), 0, width, 0, width * i)
                for i in range(count)
                if used * i < total
            ]
        self.used = used
        self.size = up(used, 16 * devices)

    def packed_spans(self):
        cuts = {0, self.used}
        for row, count, _, _, at, _ in self.parts:
            cuts |= {at, at + count}
            cuts |= {at + self.rows * h - row for h in range(self.panels) if row < self.rows * h < row + count}
        cuts = sorted(cuts)
        for start, end in zip(cuts, cuts[1:]):
            inside = []
            for row, count, column, columns, at, lane in self.parts:
                if at <= start and end <= at + count:
                    source = row + start - at
                    inside.append((source % self.rows, source // self.rows, column, columns, lane))
            yield start, end - start, sorted(inside, key=lambda item: item[-1])

    def plain_spans(self):
        cuts = {0, self.rows}
        for row, count, _, _, _, _ in self.parts:
            cuts |= {edge - self.rows * h for edge in (row, row + count) for h in range(self.panels)}
        cuts = sorted(cut for cut in cuts if 0 <= cut <= self.rows)
        for start, end in zip(cuts, cuts[1:]):
            panels = []
            for h in range(self.panels):
                first = self.rows * h + start
                inside = [
                    (column, at + first - row, lane, columns)
                    for row, count, column, columns, at, lane in self.parts
                    if row <= first < row + count
                ]
                panels.append([item[1:] for item in sorted(inside)])
            yield start, end - start, panels


def chunk_of(count):
    return next(size for size in (80, 64, 48, 32, 16) if count % size == 0)


def flip(value, mask):
    bit = 1
    out = value
    while bit <= mask:
        if mask & bit:
            out = out + bit - 2 * bit * ((value // bit) % 2)
        bit *= 2
    return out


def dot(a, b, contract=(1, 0)):
    return lax.dot_general(
        a, b, (((contract[0],), (contract[1],)), ((), ())), preferred_element_type=F32
    )


def dup(v, lanes):
    return jnp.concatenate([v] * (lanes // LANES), axis=1)


def fold_rows(v):
    out = v[0:8]
    for i in range(8, v.shape[0], 8):
        out = out + v[i : i + 8]
    return out


def fold_lanes(v):
    out = v[:, 0:LANES]
    for i in range(LANES, v.shape[1], LANES):
        out = out + v[:, i : i + LANES]
    return out


def total_rows(v):
    return jnp.sum(v, 0, keepdims=True)


class Copies:
    def __init__(self, send, recv):
        self.send, self.recv, self.count, self.open = send, recv, 0, []

    def start(self, source, target, device):
        copy = pltpu.make_async_remote_copy(
            src_ref=source,
            dst_ref=target,
            send_sem=self.send.at[self.count],
            recv_sem=self.recv.at[self.count],
            device_id=device,
            device_id_type=MESH,
        )
        self.count += 1
        self.open.append(copy)
        copy.start()
        return copy


LG = 256
FB = 80
CHUNKS = 2
SPREAD = 5


def kernel(cfg, *refs):
    C, W, J, D, H = cfg["C"], cfg["W"], cfg["J"], cfg["D"], cfg["H"]
    forms, bases = cfg["forms"], cfg["bases"]
    width, vec_at = cfg["width"], cfg["vec_at"]
    half_chips = C // 2
    R = J * BLK
    CW = R // CHUNKS
    CJ = J // CHUNKS
    EW = CJ * EDGE
    (deal, x_hbm, og_hbm, seg_ref, wi_ref, wc_ref, wo_ref) = refs[:7]
    vec_refs = refs[7:16]
    (bo_hbm, ig_hbm, fo_hbm, vo_ref) = refs[16:20]
    (
        x_v, og_v, mu1, sc1, a1, h2, mu2, sc2, a2, b1, b2, a3, gv, gh, big, c3, g3,
        m1, m2, k1, k2, w_in, w_inT, w_cv, w_cvT, w_out, wps, vecb, sa, ta, ha, pt, nh,
        psg, rx1, rx2, s2, rx3, fo, p8, p4, acc8, acc4, vx, vr, vs, vz,
        lsem, ssem, rsem,
    ) = refs[20:]

    c = lax.axis_index("ctx")
    z = lax.axis_index("wsh")
    k = c % 2
    p = c // 2
    slot_in_order = k * half_chips + p
    sibling = (flip(c, 1), z)
    chips = [(flip(c, 2 * e), z) for e in range(1, half_chips)]
    planes = [(c, flip(z, d)) for d in range(1, W)]
    copies = Copies(ssem, rsem)
    shards = range(W)

    def local(i, source, target):
        copy = pltpu.make_async_copy(source, target, lsem.at[i])
        copy.start()
        return copy

    def loop(count, body):
        lax.fori_loop(0, count, lambda i, carry: (body(i), carry)[1], 0)

    bar = pltpu.get_barrier_semaphore()
    for m in range(1, C):
        pl.semaphore_signal(bar, inc=1, device_id=(flip(c, m), z), device_id_type=MESH)
    for device in planes:
        pl.semaphore_signal(bar, inc=1, device_id=device, device_id_type=MESH)
    x_copy = local(0, x_hbm, x_v)
    og_copy = local(1, og_hbm, og_v)
    sa[pl.ds(pl.multiple_of(c * J, 8), J)] = seg_ref[...]

    def pack(name, take, put, copies_of, dtype):
        form, base = forms[name], bases[name]
        for start, count, inside in form.packed_spans():
            size = chunk_of(count)

            def step(i, start=start, inside=inside, size=size):
                shift = i * size
                to = pl.ds(pl.multiple_of(base + start + shift, 16), size)
                for s in copies_of:
                    parts, lane = [], 0
                    for row, panel, column, columns, at in inside:
                        rows = pl.ds(pl.multiple_of(row + shift, 16), size)
                        parts.append(take(s, panel, rows, slice(column, column + columns)))
                        lane = at + columns
                    if lane < LANES:
                        parts.append(jnp.zeros((size, LANES - lane), dtype))
                    put(s, to, jnp.concatenate(parts, axis=1))

            loop(count // size, step)
        if form.size > form.used:
            for s in copies_of:
                rest = pl.ds(base + form.used, form.size - form.used)
                put(s, rest, jnp.zeros((form.size - form.used, LANES), dtype))

    def moved(columns, by):
        return slice(columns.start + by, columns.stop + by)

    def put_own(s, rows, value):
        wps[0, rows, :] = value

    own_shard = {
        "in": lambda s, panel, rows, columns: w_in[rows, columns],
        "conv": lambda s, panel, rows, columns: wc_ref[panel, rows, columns],
        "out": lambda s, panel, rows, columns: wo_ref[rows, moved(columns, width * panel)],
    }
    def part(name, order):
        share = forms[name].size // C
        return pl.ds(pl.multiple_of(bases[name] + order * share, 16), share)

    def half(name, which):
        share = forms[name].size // 2
        return pl.ds(pl.multiple_of(bases[name] + which * share, 16), share)

    def z_send(name):
        rows = part(name, slot_in_order)
        return [copies.start(wps.at[0, rows], wps.at[d + 1, rows], planes[d]) for d in range(W - 1)]

    def plane_send(name, before):
        for copy in before:
            copy.wait_recv()
        there = wps.at[pl.ds(1, W - 1), part(name, slot_in_order)]
        return [copies.start(there, there, device) for device in chips]

    def sibling_send(name, before):
        for copy in before:
            copy.wait_recv()
        there = wps.at[pl.ds(1, W - 1), half(name, k)]
        return copies.start(there, there, sibling)

    w_in[:, 0:width] = wi_ref[...].T
    pack("in", own_shard["in"], put_own, (0,), BF16)
    rows = []
    for ref in vec_refs:
        row = ref[...].astype(F32).reshape(1, ref.shape[0])
        for h in range(ref.shape[0] // width):
            rows.append(
                jnp.concatenate([row[:, h * width : (h + 1) * width], jnp.zeros((1, LANES - width), F32)], axis=1)
            )
    rows.append(jnp.zeros((16 - len(rows), LANES), F32))
    vecb[0] = jnp.concatenate(rows, axis=0).astype(BF16)
    pl.semaphore_wait(bar, C - 1 + W - 1)
    vec_sends = [copies.start(vecb.at[0], vecb.at[d + 1], planes[d]) for d in range(W - 1)]
    w_z = {"in": z_send("in")}
    for name in ("conv", "out"):
        pack(name, own_shard[name], put_own, (0,), BF16)
        w_z[name] = z_send(name)
    own_seg = sa.at[pl.ds(pl.multiple_of(c * J, 8), J)]
    seg_sends = [copies.start(own_seg, own_seg, (flip(c, m), z)) for m in range(1, C)]
    acc8[...] = jnp.zeros_like(acc8)
    acc4[...] = jnp.zeros_like(acc4)
    vx[...] = jnp.zeros_like(vx)

    def unpack(name, target, stacked=False):
        form, base = forms[name], bases[name]
        for start, count, panels in form.plain_spans():
            size = chunk_of(count)
            groups = [[panel] for panel in panels] if stacked else [panels]
            for g, group in enumerate(groups):

                def step(i, first=g * form.rows + start, group=group, size=size):
                    shift = i * size
                    parts = [
                        wps[flip(z, s), pl.ds(pl.multiple_of(base + row + shift, 16), size), lane : lane + columns]
                        for s in shards
                        for panel in group
                        for row, lane, columns in panel
                    ]
                    target[pl.ds(pl.multiple_of(first + shift, 16), size), :] = jnp.concatenate(parts, axis=1)

                loop(count // size, step)

    def lanes_at(start):
        return pl.ds(pl.multiple_of(start, LG), LG)

    def blocks(n):
        return [slice(f, f + FB) for f in range(0, n, FB)]

    x_copy.wait()
    og_copy.wait()

    def first_stats(i):
        lanes = lanes_at(i * LG)
        acc = jnp.zeros((8, LG), F32)
        for f in blocks(D):
            acc += fold_rows(x_v[f, lanes].astype(F32))
            acc8[2, f] += fold_lanes(og_v[f, lanes].astype(F32))
        mean = total_rows(acc) * (1.0 / D)
        acc = jnp.zeros((8, LG), F32)
        for f in blocks(D):
            centred = x_v[f, lanes].astype(F32) - mean
            acc += fold_rows(centred * centred)
        mu1[:, lanes] = mean
        sc1[:, lanes] = lax.rsqrt(total_rows(acc) * (1.0 / D) + EPS)

    loop(R // LG, first_stats)

    for copy in vec_sends:
        copy.wait_recv()
    vecs = [vecb[flip(z, s)].astype(F32) for s in shards]
    narrow = jnp.concatenate([v[:, :width] for v in vecs], axis=1).T
    for i in range(6):
        scale = 0.5 if i < 4 else 1.0
        p4[i] = jnp.broadcast_to(narrow[:, 4 + i : 5 + i] * scale, (H, LANES))
    broad = jnp.concatenate(
        [
            jnp.concatenate([v[at + h : at + h + 1, :width] for v in vecs for h in range(2)], axis=1)
            for at in (0, 2, 10)
        ]
        + [jnp.zeros((5, D), F32)],
        axis=0,
    ).T
    for i in range(3):
        scale = 0.5 if i < 2 else 1.0
        p8[i] = jnp.broadcast_to(broad[:, i : i + 1] * scale, (D, LANES))

    def first_act(i):
        lanes = lanes_at(i * LG)
        mean, scaled = mu1[:, lanes], sc1[:, lanes]
        for f in blocks(D):
            normed = (x_v[f, lanes].astype(F32) - mean) * scaled
            pre = normed * dup(p8[0, f], LG) + dup(p8[1, f], LG)
            a1[f, lanes] = (pre * jnp.tanh(pre) + pre).astype(BF16)

    w_plane = {"in": plane_send("in", w_z["in"])}
    loop(R // LG // 2, first_act)
    w_plane["conv"] = plane_send("conv", w_z["conv"])
    loop(R // LG // 2, lambda i: first_act(i + R // LG // 2))
    w_plane["out"] = plane_send("out", w_z["out"])
    w_sib = {"in": sibling_send("in", w_plane["in"])}
    w_sib["in"].wait_recv()
    unpack("in", w_in)
    w_inT[...] = w_in[...].T

    def second(chunk):
        here = slice(chunk * CW, (chunk + 1) * CW)
        h2[:, here] = dot(w_inT[...], a1[:, here])

        def step(i):
            lanes = lanes_at(chunk * CW + i * LG)
            acc = jnp.zeros((8, LG), F32)
            for f in blocks(H):
                value = h2[f, lanes] + dup(p4[4, f], LG)
                h2[f, lanes] = value
                acc += fold_rows(value)
            mean = total_rows(acc) * (1.0 / H)
            acc = jnp.zeros((8, LG), F32)
            for f in blocks(H):
                centred = h2[f, lanes] - mean
                acc += fold_rows(centred * centred)
            scaled = lax.rsqrt(total_rows(acc) * (1.0 / H) + EPS)
            mu2[:, lanes] = mean
            sc2[:, lanes] = scaled
            for f in blocks(H):
                normed = (h2[f, lanes] - mean) * scaled
                pre = normed * dup(p4[0, f], LG) + dup(p4[1, f], LG)
                a2[f, lanes] = (pre * jnp.tanh(pre) + pre).astype(BF16)

        loop(CW // LG, step)

    def edge_send(store, source, chunk, first):
        lanes = slice(chunk * EW, (chunk + 1) * EW)
        store[c, :, lanes] = jnp.concatenate(
            [source[:, j * BLK + first : j * BLK + first + EDGE] for j in range(chunk * CJ, (chunk + 1) * CJ)], axis=1
        )
        there = store.at[c, :, lanes]
        return [copies.start(there, there, device) for device in chips], copies.start(there, there, sibling)

    def edge_forward(store, sends, chunk):
        lanes = slice(chunk * EW, (chunk + 1) * EW)
        passed = []
        for e in range(1, half_chips):
            there = store.at[flip(c, 2 * e), :, lanes]
            sends[e - 1].wait_recv()
            passed.append(copies.start(there, there, sibling))
        return passed

    mine = [deal[c * J + j] for j in range(J)]
    edge_lane = lax.broadcasted_iota(jnp.int32, (1, J * EDGE), 1)
    edge_block = jnp.zeros((1, J * EDGE), jnp.int32)
    seg_block = jnp.zeros((J, BLK), jnp.int32)
    for j in range(J):
        inside = jnp.logical_and(edge_lane >= j * EDGE, edge_lane < (j + 1) * EDGE)
        edge_block = jnp.where(inside, mine[j], edge_block)
        seg_block = jnp.where(lax.broadcasted_iota(jnp.int32, (J, BLK), 0) == j, mine[j], seg_block)
    diagonal = jnp.where(
        lax.broadcasted_iota(jnp.int32, (EDGE, J * EDGE), 0)
        == lax.broadcasted_iota(jnp.int32, (EDGE, J * EDGE), 1) % EDGE,
        1.0,
        0.0,
    )

    def edge_take(store, waits, step, target):
        for copy in waits:
            copy.wait_recv()
        wanted = edge_block + step
        total = jnp.zeros((H, J * EDGE), F32)
        for device in range(C):
            chosen = [
                diagonal * jnp.where(wanted == deal[device * J + j], 1.0, 0.0) for j in range(J)
            ]
            total += dot(store[device], jnp.concatenate(chosen, axis=0).astype(BF16))
        target[...] = total.astype(BF16)

    def seg_take(step):
        wanted = seg_block + step
        out = jnp.full((J, BLK), -1, jnp.int32)
        for slot in range(C * J):
            out = jnp.where(wanted == deal[slot], jnp.broadcast_to(sa[slot : slot + 1], (J, BLK)), out)
        return out

    t_first, t_near, t_passed = [], [], []
    for chunk in range(CHUNKS):
        second(chunk)
        sends, near = edge_send(ta, a2, chunk, BLK - EDGE)
        t_first.append(sends)
        t_near.append(near)
    w_sib["conv"] = sibling_send("conv", w_plane["conv"])
    w_sib["out"] = sibling_send("out", w_plane["out"])

    for copy in seg_sends:
        copy.wait_recv()
    own, before, behind = sa[pl.ds(pl.multiple_of(c * J, 8), J)], seg_take(-1), seg_take(1)
    cut = BLK - STEP

    def same(a, b):
        return jnp.where(a == b, 1.0, 0.0)

    keep_1 = same(own, jnp.concatenate([before[:, cut:], own[:, :cut]], axis=1))
    keep_2 = same(own, jnp.concatenate([before[:, BLK - EDGE :], own[:, : BLK - EDGE]], axis=1))
    next_1 = same(behind[:, :EDGE], jnp.concatenate([own[:, cut:], behind[:, :STEP]], axis=1))
    next_2 = same(behind[:, :EDGE], own[:, BLK - EDGE :])
    for target, mask, size in ((m1, keep_1, BLK), (m2, keep_2, BLK), (k1, next_1, EDGE), (k2, next_2, EDGE)):
        for j in range(J):
            target[:, j * size : (j + 1) * size] = jnp.broadcast_to(mask[j : j + 1], (16, size)).astype(BF16)

    def tall(mask):
        return jnp.concatenate([mask] * (H // 16), axis=0)

    w_sib["conv"].wait_recv()
    unpack("conv", w_cv, stacked=True)
    for tap in range(TAPS):
        w_cvT[tap] = w_cv[tap * H : (tap + 1) * H].T
    w_sib["out"].wait_recv()
    unpack("out", w_out)
    for chunk in range(CHUNKS):
        t_passed += edge_forward(ta, t_first[chunk], chunk)
    for chunk in range(CHUNKS):
        here = slice(chunk * CW, (chunk + 1) * CW)
        g3[:, here] = dot(w_out[...], og_v[:, here])
    edge_take(ta, t_near + t_passed, -1, pt)

    def third(chunk):
        here = slice(chunk * CW, (chunk + 1) * CW)
        for j in range(chunk * CJ, (chunk + 1) * CJ):
            tile, edge = slice(j * BLK, (j + 1) * BLK), slice(j * EDGE, (j + 1) * EDGE)
            own, prev = a2[:, tile], pt[:, edge]
            b1[:, tile] = jnp.concatenate([prev[:, STEP:], own[:, :cut]], axis=1) * tall(m1[:, tile])
            b2[:, tile] = jnp.concatenate([prev, own[:, : BLK - EDGE]], axis=1) * tall(m2[:, tile])
        c3[:, here] = dot(w_cvT[0], a2[:, here]) + dot(w_cvT[1], b1[:, here]) + dot(w_cvT[2], b2[:, here])

        def step(i):
            lanes = lanes_at(chunk * CW + i * LG)
            acc = jnp.zeros((8, LG), F32)
            for f in blocks(H):
                value = c3[f, lanes] + dup(p4[5, f], LG)
                c3[f, lanes] = value
                acc += fold_rows(value)
            mean = total_rows(acc) * (1.0 / H)
            acc = jnp.zeros((8, LG), F32)
            for f in blocks(H):
                centred = c3[f, lanes] - mean
                acc += fold_rows(centred * centred)
            scaled = lax.rsqrt(total_rows(acc) * (1.0 / H) + EPS)
            first, second = jnp.zeros((8, LG), F32), jnp.zeros((8, LG), F32)
            for f in blocks(H):
                normed = (c3[f, lanes] - mean) * scaled
                gain = dup(p4[2, f], LG)
                pre = normed * gain + dup(p4[3, f], LG)
                t = jnp.tanh(pre)
                a3[f, lanes] = (pre * t + pre).astype(BF16)
                upstream = g3[f, lanes] * ((1.0 + t) * (1.0 + pre * (1.0 - t)))
                acc4[2, f] += fold_lanes(upstream * normed)
                acc4[3, f] += fold_lanes(upstream)
                upstream = upstream * gain
                g3[f, lanes] = upstream
                first += fold_rows(upstream)
                second += fold_rows(upstream * normed)
            first, second = total_rows(first) * (1.0 / H), total_rows(second) * (1.0 / H)
            for f in blocks(H):
                normed = (c3[f, lanes] - mean) * scaled
                grad = (scaled * (g3[f, lanes] - first - normed * second)).astype(BF16)
                gv[f, lanes] = grad
                acc4[5, f] += fold_lanes(grad.astype(F32))

        loop(CW // LG, step)

    h_first, h_near, h_passed = [], [], []
    for chunk in range(CHUNKS):
        third(chunk)
        sends, near = edge_send(ha, gv, chunk, 0)
        h_first.append(sends)
        h_near.append(near)

    taps_at = (c3, g3, big)
    whole_grad = {
        "in": lambda s, panel, rows, columns: big[rows, moved(columns, width * s)],
        "conv": lambda s, panel, rows, columns: taps_at[panel][rows, moved(columns, width * s)],
        "out": lambda s, panel, rows, columns: big[rows, moved(columns, width * (forms["out"].panels * s + panel))],
    }

    def put_grad(s, rows, value):
        psg[flip(z, s), rows, :] = value.astype(BF16)

    def pack_grad(name):
        pack(name, whole_grad[name], put_grad, shards, F32)

    def halved(name):
        return pl.ds(bases[name] // 2, forms[name].size // 2)

    def shared(name):
        return pl.ds(bases[name] // C, forms[name].size // C)

    def reduce_1(name):
        return copies.start(psg.at[:, half(name, 1 - k)], rx1.at[:, halved(name)], sibling)

    def tiles(rows, body):
        size = chunk_of(rows)
        loop(rows // size, lambda i: body(pl.multiple_of(i * size, 16), size))

    def reduce_2(name, before):
        before.wait_recv()
        form = forms[name]
        first, mine = bases[name] // 2, bases[name] + k * (form.size // 2)

        def add(at, size):
            to = pl.ds(pl.multiple_of(first + at, 16), size)
            here = pl.ds(pl.multiple_of(mine + at, 16), size)
            for d in range(W):
                psg[d, here] = (psg[d, here].astype(F32) + rx1[d, to].astype(F32)).astype(BF16)

        tiles(form.size // 2, add)
        share = form.size // C
        sends = []
        for e, device in enumerate(chips):
            rows = pl.ds(pl.multiple_of(mine + flip(p, e + 1) * share, 16), share)
            sends.append(copies.start(psg.at[:, rows], rx2.at[e, :, shared(name)], device))
        return sends

    def reduce_3(name, before):
        for copy in before:
            copy.wait_recv()
        share = forms[name].size // C
        first, mine = bases[name] // C, bases[name] + slot_in_order * share

        def add(at, size):
            to = pl.ds(pl.multiple_of(first + at, 16), size)
            here = pl.ds(pl.multiple_of(mine + at, 16), size)
            for d in range(W):
                total = psg[d, here].astype(F32)
                for e in range(half_chips - 1):
                    total = total + rx2[e, d, to].astype(F32)
                s2[d, to] = total.astype(BF16)

        tiles(share, add)
        return [copies.start(s2.at[d + 1, shared(name)], rx3.at[d, shared(name)], planes[d]) for d in range(W - 1)]

    def reduce_4(name, before):
        for copy in before:
            copy.wait_recv()
        share = forms[name].size // C
        first, mine = bases[name] // C, bases[name] + slot_in_order * share

        def add(at, size):
            to = pl.ds(pl.multiple_of(first + at, 16), size)
            total = s2[0, to].astype(F32)
            for d in range(W - 1):
                total = total + rx3[d, to].astype(F32)
            fo[pl.ds(pl.multiple_of(mine + at, 16), size)] = total

        tiles(share, add)
        there = fo.at[part(name, slot_in_order)]
        return [copies.start(there, there, device) for device in chips]

    def reduce_5(name, before):
        for copy in before:
            copy.wait_recv()
        there = fo.at[half(name, k)]
        return copies.start(there, there, sibling)

    big[0:H, 0:D] = dot(a3[...], og_v[...], (1, 1))
    pack_grad("out")
    g_out = reduce_1("out")
    for tap, source in enumerate((a2, b1, b2)):
        taps_at[tap][0:H, 0:H] = dot(source[...], gv[...], (1, 1))
    pack_grad("conv")
    g_conv = reduce_1("conv")
    for chunk in range(CHUNKS):
        h_passed += edge_forward(ha, h_first[chunk], chunk)
    g_out = reduce_2("out", g_out)
    g_conv = reduce_2("conv", g_conv)
    edge_take(ha, h_near + h_passed, 1, nh)

    def second_back(chunk):
        here = slice(chunk * CW, (chunk + 1) * CW)
        for j in range(chunk * CJ, (chunk + 1) * CJ):
            tile, edge = slice(j * BLK, (j + 1) * BLK), slice(j * EDGE, (j + 1) * EDGE)
            own, late = gv[:, tile], nh[:, edge]
            shifted = (late * tall(k1[:, edge]))[:, :STEP]
            b1[:, tile] = jnp.concatenate([(own * tall(m1[:, tile]))[:, STEP:], shifted], axis=1)
            shifted = late * tall(k2[:, edge])
            b2[:, tile] = jnp.concatenate([(own * tall(m2[:, tile]))[:, EDGE:], shifted], axis=1)
        c3[:, here] = (
            dot(w_cv[0:H], gv[:, here]) + dot(w_cv[H : 2 * H], b1[:, here]) + dot(w_cv[2 * H : 3 * H], b2[:, here])
        )

        def step(i):
            lanes = lanes_at(chunk * CW + i * LG)
            mean, scaled = mu2[:, lanes], sc2[:, lanes]
            first, second = jnp.zeros((8, LG), F32), jnp.zeros((8, LG), F32)
            for f in blocks(H):
                normed = (h2[f, lanes] - mean) * scaled
                gain = dup(p4[0, f], LG)
                pre = normed * gain + dup(p4[1, f], LG)
                t = jnp.tanh(pre)
                upstream = c3[f, lanes] * ((1.0 + t) * (1.0 + pre * (1.0 - t)))
                acc4[0, f] += fold_lanes(upstream * normed)
                acc4[1, f] += fold_lanes(upstream)
                upstream = upstream * gain
                c3[f, lanes] = upstream
                first += fold_rows(upstream)
                second += fold_rows(upstream * normed)
            first, second = total_rows(first) * (1.0 / H), total_rows(second) * (1.0 / H)
            for f in blocks(H):
                normed = (h2[f, lanes] - mean) * scaled
                grad = (scaled * (c3[f, lanes] - first - normed * second)).astype(BF16)
                gh[f, lanes] = grad
                acc4[4, f] += fold_lanes(grad.astype(F32))

        loop(CW // LG, step)

    for chunk in range(CHUNKS):
        second_back(chunk)
    big[:, 0:H] = dot(a1[...], gh[...], (1, 1))
    pack_grad("in")
    g_in = reduce_1("in")
    g_out = reduce_3("out", g_out)
    for side in range(D // H):
        w_cvT[side] = w_out[:, side * H : (side + 1) * H].T

    def first_back(chunk):
        here = slice(chunk * CW, (chunk + 1) * CW)
        big[:, here] = dot(w_in[...], gh[:, here])

        def step(i):
            lanes = lanes_at(chunk * CW + i * LG)
            mean, scaled = mu1[:, lanes], sc1[:, lanes]
            first, second = jnp.zeros((8, LG), F32), jnp.zeros((8, LG), F32)
            for f in blocks(D):
                normed = (x_v[f, lanes].astype(F32) - mean) * scaled
                gain = dup(p8[0, f], LG)
                pre = normed * gain + dup(p8[1, f], LG)
                t = jnp.tanh(pre)
                upstream = big[f, lanes] * ((1.0 + t) * (1.0 + pre * (1.0 - t)))
                acc8[0, f] += fold_lanes(upstream * normed)
                acc8[1, f] += fold_lanes(upstream)
                upstream = upstream * gain
                big[f, lanes] = upstream
                first += fold_rows(upstream)
                second += fold_rows(upstream * normed)
            first, second = total_rows(first) * (1.0 / D), total_rows(second) * (1.0 / D)
            for f in blocks(D):
                normed = (x_v[f, lanes].astype(F32) - mean) * scaled
                grad = scaled * (big[f, lanes] - first - normed * second)
                big[f, lanes] = og_v[f, lanes].astype(F32) + grad

        loop(CW // LG, step)
        return local(2 + chunk, big.at[:, here], ig_hbm.at[:, here])

    def last(chunk):
        here = slice(chunk * CW, (chunk + 1) * CW)
        for side, store in enumerate((c3, g3)):
            store[:, 0:CW] = dot(w_cvT[side], a3[:, here])

            def step(i, side=side, store=store):
                lanes, at = lanes_at(chunk * CW + i * LG), lanes_at(i * LG)
                for f in blocks(H):
                    to = slice(side * H + f.start, side * H + f.stop)
                    value = store[f, at] + dup(p8[2, to], LG)
                    x_v[to, lanes] = (x_v[to, lanes].astype(F32) + value).astype(BF16)

            loop(CW // LG, step)
        return local(4 + chunk, x_v.at[:, here], bo_hbm.at[:, here])

    out_copies = [first_back(0)]
    g_in = reduce_2("in", g_in)
    g_conv = reduce_3("conv", g_conv)
    out_copies.append(first_back(1))

    def row_sums(group, i, scale):
        return jnp.sum((acc8 if group == 8 else acc4)[i].T, 0, keepdims=True) * scale

    for (group, i, count, scale), at in vec_at:
        value = row_sums(group, i, scale)
        for t in range(-(-count // LANES)):
            size = min(LANES, count - t * LANES)
            vx[at + t : at + t + 1, 0:size] = value[:, t * LANES : t * LANES + size]
    vr[c] = vx[...]
    v_sends = [copies.start(vr.at[c], vr.at[c], (flip(c, m), z)) for m in range(1, C)]
    g_in = reduce_3("in", g_in)
    g_out = reduce_4("out", g_out)
    g_conv = reduce_4("conv", g_conv)
    out_copies.append(last(0))
    for copy in v_sends:
        copy.wait_recv()
    total = vr[0]
    for m in range(1, C):
        total = total + vr[m]
    vs[...] = total
    z_sends = [copies.start(vs, vz.at[d], planes[d]) for d in range(W - 1)]
    g_in = reduce_4("in", g_in)
    out_copies.append(last(1))
    g_out = reduce_5("out", g_out)
    g_conv = reduce_5("conv", g_conv)
    g_in = reduce_5("in", g_in)
    for copy in z_sends:
        copy.wait_recv()
    total = vs[...]
    for d in range(W - 1):
        total = total + vz[d]
    vo_ref[...] = total
    for copy in (g_out, g_conv, g_in):
        copy.wait_recv()
    out_copies.append(local(0, fo, fo_hbm))
    for copy in copies.open:
        copy.wait_send()
    for copy in out_copies:
        copy.wait()


def spread(cfg, *refs):
    W, forms, bases, width, vec_at = (cfg[key] for key in ("W", "forms", "bases", "width", "vec_at"))
    bo_in, ig_in, fo_in, vx, bo_out, ig_out, gi_out, gc_out, go_out = refs[:9]
    vec_out, (ig_v, bo_v, fo, gi, gc, go, sem) = refs[9:18], refs[18:]
    z = lax.axis_index("wsh")
    used = 0

    def copy(source, target):
        nonlocal used
        used += 1
        move = pltpu.make_async_copy(source, target, sem.at[used - 1])
        move.start()
        return move

    grads = copy(fo_in, fo)
    pieces = []
    for source, stage, target in ((ig_in, ig_v, ig_out), (bo_in, bo_v, bo_out)):
        size = source.shape[0] // SPREAD
        for i in range(SPREAD):
            rows = pl.ds(i * size, size)
            pieces.append((copy(source.at[rows], stage.at[rows]), stage.at[rows], target.at[rows]))
    moves = []

    def pass_on(count):
        for come, stage, target in pieces[:count]:
            come.wait()
            moves.append(copy(stage, target))
        del pieces[:count]

    for ((_, _, count, _), at), target in zip(vec_at, vec_out):
        whole = jnp.concatenate([vx[at + t : at + t + 1] for t in range(-(-count // LANES))], axis=1)
        share = count // W
        mine = jnp.zeros((1, share), F32)
        for s in range(W):
            mine = jnp.where(z == s, whole[:, s * share : (s + 1) * share], mine)
        target[...] = mine.reshape(share)
    grads.wait()
    pass_on(2)
    for name, stage, target in (("conv", gc, gc_out), ("out", go, go_out), ("in", gi, gi_out)):
        form, base, parts = forms[name], bases[name], []
        for start, count, panels in form.plain_spans():
            values = [
                [fo[base + row : base + row + count, lane : lane + columns] for row, lane, columns in panel]
                for panel in panels
            ]
            if name == "conv":
                for tap, part in enumerate(values):
                    stage[tap, start : start + count] = jnp.concatenate(part, axis=1)
            else:
                parts.append(jnp.concatenate(sum(values, []), axis=1))
                if name == "out":
                    stage[start : start + count] = parts[-1]
        if name == "in":
            stage[...] = jnp.concatenate(parts, axis=0).T
        moves.append(copy(stage, target))
        pass_on(2)
    pass_on(len(pieces))
    for move in moves:
        move.wait()


def on_device(
    block_in, out_grad, segments, block_deal, weight_in, weight_conv, weight_out,
    gain_first, shift_first, gain_second, shift_second, gain_third, shift_third, bias_first, bias_conv, bias_out,
):
    C, W = lax.axis_size("ctx"), lax.axis_size("wsh")
    _, rows, D = block_in.shape
    width = weight_in.shape[1]
    H = width * W
    panels = weight_out.shape[1] // width
    J = rows // BLK
    forms = {
        "in": Packed(D, 1, width, C),
        "conv": Packed(H, TAPS, width, C),
        "out": Packed(H, panels, width, C),
    }
    bases, total = {}, 0
    for name, form in forms.items():
        bases[name] = total
        total += form.size

    vec_at, at = [], 0
    for item in [(8, 0, D, 0.5), (8, 1, D, 0.5), (8, 2, D, 1.0)] + [
        (4, i, H, 0.5 if i < 4 else 1.0) for i in range(6)
    ]:
        vec_at.append((item, at))
        at += -(-item[2] // LANES)
    v_rows = up(at, 8)
    cfg = {
        "C": C, "W": W, "J": J, "D": D, "H": H, "forms": forms, "bases": bases, "width": width, "vec_at": vec_at,
    }
    R = rows
    others = max(C // 2 - 1, 1)
    n_copies = (
        3 * ((W - 1) + (C // 2 - 1) + 1) + (W - 1) + (C - 1) + 2 * CHUNKS * (2 * (C // 2 - 1) + 1)
        + 3 * (2 * (C // 2 - 1) + (W - 1) + 2) + (C - 1) + (W - 1)
    )
    vmem = pltpu.VMEM
    scratch = [
        vmem((D, R), BF16),
        vmem((D, R), BF16),
        vmem((1, R), F32),
        vmem((1, R), F32),
        vmem((D, R), BF16),
        vmem((H, R), F32),
        vmem((1, R), F32),
        vmem((1, R), F32),
        vmem((H, R), BF16),
        vmem((H, R), BF16),
        vmem((H, R), BF16),
        vmem((H, R), BF16),
        vmem((H, R), BF16),
        vmem((H, R), BF16),
        vmem((D, R), F32),
        vmem((H, R), F32),
        vmem((H, R), F32),
        vmem((16, R), BF16),
        vmem((16, R), BF16),
        vmem((16, J * EDGE), BF16),
        vmem((16, J * EDGE), BF16),
        vmem((D, H), BF16),
        vmem((H, D), BF16),
        vmem((TAPS * H, H), BF16),
        vmem((TAPS, H, H), BF16),
        vmem((H, D), BF16),
        vmem((W, total, LANES), BF16),
        vmem((W, 16, LANES), BF16),
        vmem((J * C, BLK), jnp.int32),
        vmem((C, H, J * EDGE), BF16),
        vmem((C, H, J * EDGE), BF16),
        vmem((H, J * EDGE), BF16),
        vmem((H, J * EDGE), BF16),
        vmem((W, total, LANES), BF16),
        vmem((W, total // 2, LANES), BF16),
        vmem((others, W, total // C, LANES), BF16),
        vmem((W, total // C, LANES), BF16),
        vmem((W - 1, total // C, LANES), BF16),
        vmem((total, LANES), F32),
        vmem((3, D, LANES), F32),
        vmem((6, H, LANES), F32),
        vmem((3, D, LANES), F32),
        vmem((6, H, LANES), F32),
        vmem((v_rows, LANES), F32),
        vmem((C, v_rows, LANES), F32),
        vmem((v_rows, LANES), F32),
        vmem((W - 1, v_rows, LANES), F32),
        pltpu.SemaphoreType.DMA((6,)),
        pltpu.SemaphoreType.DMA((n_copies,)),
        pltpu.SemaphoreType.DMA((n_copies,)),
    ]
    any_spec = pl.BlockSpec(memory_space=pl.ANY)
    vmem_spec = pl.BlockSpec(memory_space=pltpu.VMEM)
    flat, tree = jax.tree.flatten(scratch)

    def run(*refs):
        kernel(cfg, *refs[:20], *jax.tree.unflatten(tree, refs[20:]))

    macs = R * (2 * D * H + TAPS * H * H) * 3
    bo, ig, fo, vo = pl.pallas_call(
        run,
        out_shape=(
            jax.ShapeDtypeStruct((D, R), BF16),
            jax.ShapeDtypeStruct((D, R), F32),
            jax.ShapeDtypeStruct((total, LANES), F32),
            jax.ShapeDtypeStruct((v_rows, LANES), F32),
        ),
        in_specs=[pl.BlockSpec(memory_space=pltpu.SMEM), any_spec, any_spec] + [vmem_spec] * 13,
        out_specs=(any_spec, any_spec, any_spec, vmem_spec),
        scratch_shapes=flat,
        compiler_params=pltpu.CompilerParams(
            collective_id=0, has_side_effects=True, vmem_limit_bytes=62 * 2**20
        ),
        cost_estimate=pl.CostEstimate(
            flops=2 * macs, bytes_accessed=10 * R * D, transcendentals=2 * R * (D + 2 * H)
        ),
        name="block",
    )(
        block_deal,
        block_in[0].T,
        out_grad[0].T,
        segments.reshape(J, BLK),
        weight_in.T,
        weight_conv,
        weight_out,
        gain_first, shift_first, gain_second, shift_second, gain_third, shift_third, bias_first, bias_conv, bias_out,
    )
    results = pl.pallas_call(
        lambda *refs: spread(cfg, *refs),
        out_shape=(
            jax.ShapeDtypeStruct((D, R), BF16),
            jax.ShapeDtypeStruct((D, R), F32),
            jax.ShapeDtypeStruct((width, D), F32),
            jax.ShapeDtypeStruct((TAPS, H, width), F32),
            jax.ShapeDtypeStruct((H, panels * width), F32),
        )
        + tuple(jax.ShapeDtypeStruct((item[2] // W,), F32) for item, _ in vec_at),
        in_specs=[any_spec, any_spec, any_spec, vmem_spec],
        out_specs=(any_spec,) * 5 + (vmem_spec,) * 9,
        scratch_shapes=[
            vmem((D, R), F32), vmem((D, R), BF16), vmem((total, LANES), F32),
            vmem((width, D), F32), vmem((TAPS, H, width), F32), vmem((H, panels * width), F32),
            pltpu.SemaphoreType.DMA((4 * SPREAD + 4,)),
        ],
        compiler_params=pltpu.CompilerParams(vmem_limit_bytes=62 * 2**20),
        cost_estimate=pl.CostEstimate(flops=0, bytes_accessed=14 * R * D, transcendentals=0),
        name="spread",
    )(bo, ig, fo, vo)
    bo, ig, gi, gc, go = results[:5]
    vec = results[5:]
    return (bo.T[None], ig.T[None], gi.T, gc, go, vec[0], vec[1], *vec[3:], vec[2])


def solution(mesh):
    in_specs = (
        P("wsh", "ctx", None), P("wsh", "ctx", None), P("wsh", "ctx"), P(),
        P(None, "wsh"), P(None, None, "wsh"), P(None, "wsh"),
    ) + (P("wsh"),) * 9
    out_specs = (
        P("wsh", "ctx", None), P("wsh", "ctx", None),
        P(None, "wsh"), P(None, None, "wsh"), P(None, "wsh"),
    ) + (P("wsh"),) * 9
    return jax.shard_map(
        on_device, mesh=mesh, in_specs=in_specs, out_specs=out_specs, check_vma=False
    )
```

```python
import jax
import jax.numpy as jnp
from jax import lax
from jax.experimental import pallas as pl
from jax.experimental.pallas import tpu as pltpu
from jax.sharding import PartitionSpec as P

TAPS = 3
STEP = 16
BLK = 128
EDGE = (TAPS - 1) * STEP
EPS = 1e-05
LANES = 128
MESH = pl.DeviceIdType.MESH
F32 = jnp.float32
BF16 = jnp.bfloat16


def up(value, unit):
    return -(-value // unit) * unit


class Packed:
    def __init__(self, rows, panels, width, devices):
        self.rows, self.panels, self.width = rows, panels, width
        total = rows * panels
        if width % 4 == 0 and width > 64 and LANES - width >= width // 4 and total % 80 == 0:
            main, rest, quarter = total * 4 // 5, total // 5, width // 4
            self.parts = [(0, main, 0, width, 0, 0)]
            self.parts += [(main, rest, quarter * i, quarter, rest * i, width) for i in range(4)]
            used = main
        else:
            count = max(LANES // width, 1)
            used = up(-(-total // count), 16)
            self.parts = [
                (used * i, min(used, total - used * i), 0, width, 0, width * i)
                for i in range(count)
                if used * i < total
            ]
        self.used = used
        self.size = up(used, 16 * devices)

    def packed_spans(self):
        cuts = {0, self.used}
        for row, count, _, _, at, _ in self.parts:
            cuts |= {at, at + count}
            cuts |= {at + self.rows * h - row for h in range(self.panels) if row < self.rows * h < row + count}
        cuts = sorted(cuts)
        for start, end in zip(cuts, cuts[1:]):
            inside = []
            for row, count, column, columns, at, lane in self.parts:
                if at <= start and end <= at + count:
                    source = row + start - at
                    inside.append((source % self.rows, source // self.rows, column, columns, lane))
            yield start, end - start, sorted(inside, key=lambda item: item[-1])

    def plain_spans(self):
        cuts = {0, self.rows}
        for row, count, _, _, _, _ in self.parts:
            cuts |= {edge - self.rows * h for edge in (row, row + count) for h in range(self.panels)}
        cuts = sorted(cut for cut in cuts if 0 <= cut <= self.rows)
        for start, end in zip(cuts, cuts[1:]):
            panels = []
            for h in range(self.panels):
                first = self.rows * h + start
                inside = [
                    (column, at + first - row, lane, columns)
                    for row, count, column, columns, at, lane in self.parts
                    if row <= first < row + count
                ]
                panels.append([item[1:] for item in sorted(inside)])
            yield start, end - start, panels


def chunk_of(count):
    return next(size for size in (80, 64, 48, 32, 16) if count % size == 0)


def flip(value, mask):
    bit = 1
    out = value
    while bit <= mask:
        if mask & bit:
            out = out + bit - 2 * bit * ((value // bit) % 2)
        bit *= 2
    return out


def dot(a, b, contract=(1, 0)):
    return lax.dot_general(
        a, b, (((contract[0],), (contract[1],)), ((), ())), preferred_element_type=F32
    )


def dup(v, lanes):
    return jnp.concatenate([v] * (lanes // LANES), axis=1)


def fold_rows(v):
    out = v[0:8]
    for i in range(8, v.shape[0], 8):
        out = out + v[i : i + 8]
    return out


def fold_lanes(v):
    out = v[:, 0:LANES]
    for i in range(LANES, v.shape[1], LANES):
        out = out + v[:, i : i + LANES]
    return out


def total_rows(v):
    return jnp.sum(v, 0, keepdims=True)


class Group:
    def __init__(self, send, recv, moves, size):
        self.send, self.recv, self.size = send, recv, size
        for source, target, device in moves:
            pltpu.make_async_remote_copy(
                src_ref=source,
                dst_ref=target,
                send_sem=send,
                recv_sem=recv,
                device_id=device,
                device_id_type=MESH,
            ).start()

    def wait(self):
        pltpu.make_async_copy(self.size, self.size, self.recv).wait()

    def wait_sent(self):
        pltpu.make_async_copy(self.size, self.size, self.send).wait()


class Copies:
    def __init__(self, send, recv):
        self.send, self.recv, self.groups = send, recv, []

    def start(self, moves, size):
        n = len(self.groups)
        self.groups.append(Group(self.send.at[n], self.recv.at[n], moves, size))
        return self.groups[-1]


LG = 512
FB = 16
CHUNKS = 2
SPREAD = 5


def kernel(cfg, *refs):
    C, W, J, D, H = cfg["C"], cfg["W"], cfg["J"], cfg["D"], cfg["H"]
    forms, bases = cfg["forms"], cfg["bases"]
    width, vec_at = cfg["width"], cfg["vec_at"]
    half_chips = C // 2
    R = J * BLK
    CW = R // CHUNKS
    CJ = J // CHUNKS
    EW = CJ * EDGE
    (deal, x_hbm, og_hbm, seg_hbm, wi_hbm, wc_hbm, wo_hbm) = refs[:7]
    vec_hbm = refs[7:16]
    (bo_hbm, ig_hbm, fo_hbm, vo_ref) = refs[16:20]
    (
        x_v, og_v, mu1, sc1, a1, h2, mu2, sc2, bb, a3, gv, gh, big, c3, g3,
        m1, m2, k1, k2, w_in, w_inT, w_cv, w_cvT, w_out, wps, vecb, sa, ta, ha, pt, nh,
        psg, rx1, rx2, s2, rx3, rz, tz, fo, p8, p4, acc8, acc4, vx, vr, vs, vz,
        wi_ref, wc_ref, wo_ref, *vec_refs, lsem, ssem, rsem,
    ) = refs[20:]

    c = lax.axis_index("ctx")
    z = lax.axis_index("wsh")
    k = c % 2
    p = c // 2
    slot_in_order = k * half_chips + p
    sibling = (flip(c, 1), z)
    chips = [(flip(c, 2 * e), z) for e in range(1, half_chips)]
    planes = [(c, flip(z, d)) for d in range(1, W)]
    copies = Copies(ssem, rsem)
    shards = range(W)

    def local(i, source, target):
        copy = pltpu.make_async_copy(source, target, lsem.at[i])
        copy.start()
        return copy

    def loop(count, body):
        lax.fori_loop(0, count, lambda i, carry: (body(i), carry)[1], 0)

    bar = pltpu.get_barrier_semaphore()
    for m in range(1, C):
        pl.semaphore_signal(bar, inc=1, device_id=(flip(c, m), z), device_id_type=MESH)
    for device in planes:
        pl.semaphore_signal(bar, inc=1, device_id=device, device_id_type=MESH)
    own_seg = sa.at[pl.ds(pl.multiple_of(c * J, 8), J)]
    w_copies = [local(n, *pair) for n, pair in enumerate(((wi_hbm, wi_ref), (wc_hbm, wc_ref), (wo_hbm, wo_ref)))]
    vec_copies = [local(3 + n, *pair) for n, pair in enumerate(zip(vec_hbm, vec_refs))]
    seg_copy = local(12, seg_hbm, own_seg)
    x_copy = local(13, x_hbm, x_v)
    og_copy = local(14, og_hbm, og_v)

    def pack(name, take, put, copies_of, dtype):
        form, base = forms[name], bases[name]
        for start, count, inside in form.packed_spans():
            size = chunk_of(count)

            def step(i, start=start, inside=inside, size=size):
                shift = i * size
                to = pl.ds(pl.multiple_of(base + start + shift, 16), size)
                for s in copies_of:
                    parts, lane = [], 0
                    for row, panel, column, columns, at in inside:
                        rows = pl.ds(pl.multiple_of(row + shift, 16), size)
                        parts.append(take(s, panel, rows, slice(column, column + columns)))
                        lane = at + columns
                    if lane < LANES:
                        parts.append(jnp.zeros((size, LANES - lane), dtype))
                    put(s, to, jnp.concatenate(parts, axis=1))

            loop(count // size, step)
        if form.size > form.used:
            for s in copies_of:
                rest = pl.ds(base + form.used, form.size - form.used)
                put(s, rest, jnp.zeros((form.size - form.used, LANES), dtype))

    def moved(columns, by):
        return slice(columns.start + by, columns.stop + by)

    def put_own(s, rows, value):
        wps[0, rows, :] = value

    own_shard = {
        "in": lambda s, panel, rows, columns: w_in[rows, columns],
        "conv": lambda s, panel, rows, columns: wc_ref[panel, rows, columns],
        "out": lambda s, panel, rows, columns: wo_ref[rows, moved(columns, width * panel)],
    }
    def part(name, order):
        share = forms[name].size // C
        return pl.ds(pl.multiple_of(bases[name] + order * share, 16), share)

    def half(name, which):
        share = forms[name].size // 2
        return pl.ds(pl.multiple_of(bases[name] + which * share, 16), share)

    others = half_chips - 1

    def z_send(name):
        rows = half(name, k) if name in cfg["z_only"] else part(name, slot_in_order)
        moves = [(wps.at[0, rows], wps.at[d + 1, rows], planes[d]) for d in range(W - 1)]
        return copies.start(moves, wps.at[pl.ds(1, W - 1), rows])

    def plane_send(name, before):
        if name in cfg["z_only"]:
            return before
        before.wait()
        there = wps.at[pl.ds(1, W - 1), part(name, slot_in_order)]
        size = wps.at[pl.ds(1, W - 1), pl.ds(bases[name], others * (forms[name].size // C))]
        return copies.start([(there, there, device) for device in chips], size)

    def sibling_send(name, before):
        before.wait()
        there = wps.at[pl.ds(1, W - 1), half(name, k)]
        return copies.start([(there, there, sibling)], there)

    w_copies[0].wait()
    w_in[:, 0:width] = wi_ref[...].T
    pack("in", own_shard["in"], put_own, (0,), BF16)
    rows = []
    for ref, copy in zip(vec_refs, vec_copies):
        copy.wait()
        row = ref[...].astype(F32).reshape(1, ref.shape[0])
        for h in range(ref.shape[0] // width):
            rows.append(
                jnp.concatenate([row[:, h * width : (h + 1) * width], jnp.zeros((1, LANES - width), F32)], axis=1)
            )
    rows.append(jnp.zeros((16 - len(rows), LANES), F32))
    vecb[0] = jnp.concatenate(rows, axis=0).astype(BF16)
    pl.semaphore_wait(bar, C - 1 + W - 1)
    vec_sends = copies.start(
        [(vecb.at[0], vecb.at[d + 1], planes[d]) for d in range(W - 1)], vecb.at[pl.ds(1, W - 1)]
    )
    w_z = {"in": z_send("in")}
    for name, copy in (("conv", w_copies[1]), ("out", w_copies[2])):
        copy.wait()
        pack(name, own_shard[name], put_own, (0,), BF16)
        w_z[name] = z_send(name)
    seg_copy.wait()
    seg_sends = copies.start(
        [(own_seg, own_seg, (flip(c, m), z)) for m in range(1, C)], sa.at[pl.ds(0, (C - 1) * J)]
    )
    acc8[...] = jnp.zeros_like(acc8)
    acc4[...] = jnp.zeros_like(acc4)
    a1[D : D + 16] = jnp.ones((16, R), BF16)
    a3[H : H + 16] = jnp.ones((16, R), BF16)
    bb[TAPS * H : TAPS * H + 16] = jnp.ones((16, R), BF16)
    vx[...] = jnp.zeros_like(vx)

    def unpack(name, target):
        form, base = forms[name], bases[name]
        for start, count, panels in form.plain_spans():
            size = chunk_of(count)
            order = [(s, panel) for s in shards for panel in panels]
            if name == "conv":
                order = [(s, panel) for panel in panels for s in shards]

            def step(i, start=start, order=order, size=size):
                shift = i * size
                parts = [
                    wps[flip(z, s), pl.ds(pl.multiple_of(base + row + shift, 16), size), lane : lane + columns]
                    for s, panel in order
                    for row, lane, columns in panel
                ]
                target[pl.ds(pl.multiple_of(start + shift, 16), size), :] = jnp.concatenate(parts, axis=1)

            loop(count // size, step)

    def lanes_at(start):
        return pl.ds(pl.multiple_of(start, LG), LG)

    def blocks(n):
        return [slice(f, f + FB) for f in range(0, n, FB)]

    x_copy.wait()

    def first_stats(i):
        lanes = lanes_at(i * LG)
        acc = jnp.zeros((8, LG), F32)
        for f in blocks(D):
            acc += fold_rows(x_v[f, lanes].astype(F32))
        mean = total_rows(acc) * (1.0 / D)
        acc = jnp.zeros((8, LG), F32)
        for f in blocks(D):
            centred = x_v[f, lanes].astype(F32) - mean
            acc += fold_rows(centred * centred)
        mu1[:, lanes] = mean
        sc1[:, lanes] = lax.rsqrt(total_rows(acc) * (1.0 / D) + EPS)

    loop(R // LG, first_stats)

    vec_sends.wait()
    vecs = [vecb[flip(z, s)].astype(F32) for s in shards]
    narrow = jnp.concatenate([v[:, :width] for v in vecs], axis=1).T
    for i in range(6):
        scale = 0.5 if i < 4 else 1.0
        p4[i] = jnp.broadcast_to(narrow[:, 4 + i : 5 + i] * scale, (H, LANES))
    broad = jnp.concatenate(
        [
            jnp.concatenate([v[at + h : at + h + 1, :width] for v in vecs for h in range(2)], axis=1)
            for at in (0, 2, 10)
        ]
        + [jnp.zeros((5, D), F32)],
        axis=0,
    ).T
    for i in range(3):
        scale = 0.5 if i < 2 else 1.0
        p8[i] = jnp.broadcast_to(broad[:, i : i + 1] * scale, (D, LANES))

    def first_act(i):
        lanes = lanes_at(i * LG)
        mean, scaled = mu1[:, lanes], sc1[:, lanes]
        for f in blocks(D):
            normed = (x_v[f, lanes].astype(F32) - mean) * scaled
            pre = normed * dup(p8[0, f], LG) + dup(p8[1, f], LG)
            a1[f, lanes] = (pre * jnp.tanh(pre) + pre).astype(BF16)

    w_plane = {"in": plane_send("in", w_z["in"])}
    loop(R // LG, first_act)
    w_sib = {"in": sibling_send("in", w_plane["in"])}
    w_plane["conv"] = plane_send("conv", w_z["conv"])
    w_sib["in"].wait()
    unpack("in", w_in)
    w_inT[...] = w_in[...].T

    def second(chunk):
        here = slice(chunk * CW, (chunk + 1) * CW)
        h2[:, here] = dot(w_inT[...], a1[0:D, here])

        def step(i):
            lanes = lanes_at(chunk * CW + i * LG)
            acc = jnp.zeros((8, LG), F32)
            for f in blocks(H):
                value = h2[f, lanes] + dup(p4[4, f], LG)
                h2[f, lanes] = value
                acc += fold_rows(value)
            mean = total_rows(acc) * (1.0 / H)
            acc = jnp.zeros((8, LG), F32)
            for f in blocks(H):
                centred = h2[f, lanes] - mean
                acc += fold_rows(centred * centred)
            scaled = lax.rsqrt(total_rows(acc) * (1.0 / H) + EPS)
            mu2[:, lanes] = mean
            sc2[:, lanes] = scaled
            for f in blocks(H):
                normed = (h2[f, lanes] - mean) * scaled
                pre = normed * dup(p4[0, f], LG) + dup(p4[1, f], LG)
                bb[f, lanes] = (pre * jnp.tanh(pre) + pre).astype(BF16)

        loop(CW // LG, step)

    def edge_send(store, source, chunk, first):
        lanes = slice(chunk * EW, (chunk + 1) * EW)
        store[k, p, :, lanes] = jnp.concatenate(
            [source[0:H, j * BLK + first : j * BLK + first + EDGE] for j in range(chunk * CJ, (chunk + 1) * CJ)],
            axis=1,
        )
        there = store.at[k, p, :, lanes]
        return copies.start([(there, there, device) for device in chips], store.at[k, pl.ds(0, others), :, lanes])

    def edge_forward(store, before, chunk):
        before.wait()
        there = store.at[k, :, :, slice(chunk * EW, (chunk + 1) * EW)]
        return copies.start([(there, there, sibling)], there)

    mine = [deal[c * J + j] for j in range(J)]
    edge_lane = lax.broadcasted_iota(jnp.int32, (1, J * EDGE), 1)
    edge_block = jnp.zeros((1, J * EDGE), jnp.int32)
    seg_block = jnp.zeros((J, BLK), jnp.int32)
    for j in range(J):
        inside = jnp.logical_and(edge_lane >= j * EDGE, edge_lane < (j + 1) * EDGE)
        edge_block = jnp.where(inside, mine[j], edge_block)
        seg_block = jnp.where(lax.broadcasted_iota(jnp.int32, (J, BLK), 0) == j, mine[j], seg_block)
    diagonal = jnp.where(
        lax.broadcasted_iota(jnp.int32, (EDGE, J * EDGE), 0)
        == lax.broadcasted_iota(jnp.int32, (EDGE, J * EDGE), 1) % EDGE,
        1.0,
        0.0,
    )

    def edge_take(store, waits, step, target):
        for group in waits:
            group.wait()
        wanted = edge_block + step
        total = jnp.zeros((H, J * EDGE), F32)
        for device in range(C):
            chosen = [diagonal * jnp.where(wanted == deal[device * J + j], 1.0, 0.0) for j in range(J)]
            total += dot(store[device % 2, device // 2], jnp.concatenate(chosen, axis=0).astype(BF16))
        target[...] = total.astype(BF16)

    def seg_take(step):
        wanted = seg_block + step
        out = jnp.full((J, BLK), -1, jnp.int32)
        for slot in range(C * J):
            out = jnp.where(wanted == deal[slot], jnp.broadcast_to(sa[slot : slot + 1], (J, BLK)), out)
        return out

    t_first, t_passed = [], []
    for chunk in range(CHUNKS):
        second(chunk)
        t_first.append(edge_send(ta, bb, chunk, BLK - EDGE))
    w_sib["conv"] = sibling_send("conv", w_plane["conv"])
    w_plane["out"] = plane_send("out", w_z["out"])
    w_sib["out"] = sibling_send("out", w_plane["out"])

    seg_sends.wait()
    own, before, behind = sa[pl.ds(pl.multiple_of(c * J, 8), J)], seg_take(-1), seg_take(1)
    cut = BLK - STEP

    def same(a, b):
        return jnp.where(a == b, 1.0, 0.0)

    keep_1 = same(own, jnp.concatenate([before[:, cut:], own[:, :cut]], axis=1))
    keep_2 = same(own, jnp.concatenate([before[:, BLK - EDGE :], own[:, : BLK - EDGE]], axis=1))
    next_1 = same(behind[:, :EDGE], jnp.concatenate([own[:, cut:], behind[:, :STEP]], axis=1))
    next_2 = same(behind[:, :EDGE], own[:, BLK - EDGE :])
    for target, mask, size in ((m1, keep_1, BLK), (m2, keep_2, BLK), (k1, next_1, EDGE), (k2, next_2, EDGE)):
        for j in range(J):
            target[:, j * size : (j + 1) * size] = jnp.broadcast_to(mask[j : j + 1], (16, size)).astype(BF16)

    def tall(mask):
        return jnp.concatenate([mask] * (H // 16), axis=0)

    w_sib["conv"].wait()
    unpack("conv", w_cv)
    w_cvT[:, 0 : TAPS * H] = jnp.concatenate([w_cv[:, tap * H : (tap + 1) * H].T for tap in range(TAPS)], axis=1)
    w_sib["out"].wait()
    unpack("out", w_out)
    for chunk in range(CHUNKS):
        t_passed.append(edge_forward(ta, t_first[chunk], chunk))
    og_copy.wait()
    for chunk in range(CHUNKS):
        here = slice(chunk * CW, (chunk + 1) * CW)
        g3[:, here] = dot(w_out[...], og_v[:, here])
    edge_take(ta, t_passed, -1, pt)

    def third(chunk):
        here = slice(chunk * CW, (chunk + 1) * CW)
        for j in range(chunk * CJ, (chunk + 1) * CJ):
            tile, edge = slice(j * BLK, (j + 1) * BLK), slice(j * EDGE, (j + 1) * EDGE)
            own, prev = bb[0:H, tile], pt[:, edge]
            bb[H : 2 * H, tile] = jnp.concatenate([prev[:, STEP:], own[:, :cut]], axis=1) * tall(m1[:, tile])
            bb[2 * H : 3 * H, tile] = jnp.concatenate([prev, own[:, : BLK - EDGE]], axis=1) * tall(m2[:, tile])
        c3[:, here] = dot(w_cvT[:, 0 : TAPS * H], bb[0 : TAPS * H, here])

        def step(i):
            lanes = lanes_at(chunk * CW + i * LG)
            acc = jnp.zeros((8, LG), F32)
            for f in blocks(H):
                value = c3[f, lanes] + dup(p4[5, f], LG)
                c3[f, lanes] = value
                acc += fold_rows(value)
            mean = total_rows(acc) * (1.0 / H)
            acc = jnp.zeros((8, LG), F32)
            for f in blocks(H):
                centred = c3[f, lanes] - mean
                acc += fold_rows(centred * centred)
            scaled = lax.rsqrt(total_rows(acc) * (1.0 / H) + EPS)
            first, second = jnp.zeros((8, LG), F32), jnp.zeros((8, LG), F32)
            for f in blocks(H):
                normed = (c3[f, lanes] - mean) * scaled
                gain = dup(p4[2, f], LG)
                pre = normed * gain + dup(p4[3, f], LG)
                t = jnp.tanh(pre)
                a3[f, lanes] = (pre * t + pre).astype(BF16)
                upstream = g3[f, lanes] * ((1.0 + t) * (1.0 + pre * (1.0 - t)))
                acc4[2, f] += fold_lanes(upstream * normed)
                acc4[3, f] += fold_lanes(upstream)
                upstream = upstream * gain
                g3[f, lanes] = upstream
                first += fold_rows(upstream)
                second += fold_rows(upstream * normed)
            first, second = total_rows(first) * (1.0 / H), total_rows(second) * (1.0 / H)
            for f in blocks(H):
                normed = (c3[f, lanes] - mean) * scaled
                grad = (scaled * (g3[f, lanes] - first - normed * second)).astype(BF16)
                gv[f, lanes] = grad

        loop(CW // LG, step)

    h_first, h_passed = [], []
    for chunk in range(CHUNKS):
        third(chunk)
        h_first.append(edge_send(ha, gv, chunk, 0))

    taps_at = (c3, g3, big)
    whole_grad = {
        "in": lambda s, panel, rows, columns: big[rows, moved(columns, width * s)],
        "conv": lambda s, panel, rows, columns: taps_at[panel][rows, moved(columns, width * s)],
        "out": lambda s, panel, rows, columns: big[rows, moved(columns, width * (forms["out"].panels * s + panel))],
    }

    def put_grad(s, rows, value):
        psg[flip(z, s), rows, :] = value.astype(BF16)

    def pack_grad(name):
        pack(name, whole_grad[name], put_grad, shards, F32)

    def halved(name):
        return pl.ds(bases[name] // 2, forms[name].size // 2)

    def shared(name):
        return pl.ds(bases[name] // C, forms[name].size // C)

    def keep_row(index, row):
        at, count = vec_at[index][1], row.shape[1]
        for t in range(-(-count // LANES)):
            size = min(LANES, count - t * LANES)
            vx[at + t : at + t + 1, 0:size] = row[:, t * LANES : t * LANES + size]

    def tiles(rows, body):
        size = chunk_of(rows)
        loop(rows // size, lambda i: body(pl.multiple_of(i * size, 16), size))

    def reduce_1(name):
        there = rx1.at[:, halved(name)]
        return copies.start([(psg.at[:, half(name, 1 - k)], there, sibling)], there)

    def add_sibling(name, before):
        before.wait()
        form = forms[name]
        first, mine = bases[name] // 2, bases[name] + k * (form.size // 2)

        def add(at, size):
            to = pl.ds(pl.multiple_of(first + at, 16), size)
            here = pl.ds(pl.multiple_of(mine + at, 16), size)
            for d in range(W):
                psg[d, here] = (psg[d, here].astype(F32) + rx1[d, to].astype(F32)).astype(BF16)

        tiles(form.size // 2, add)
        return mine

    def plane_2(name, before):
        mine = add_sibling(name, before)
        share = forms[name].size // C
        moves = []
        for e, device in enumerate(chips):
            rows = pl.ds(pl.multiple_of(mine + flip(p, e + 1) * share, 16), share)
            moves.append((psg.at[:, rows], rx2.at[e, :, shared(name)], device))
        return copies.start(moves, rx2.at[:, :, shared(name)])

    def plane_3(name, before):
        before.wait()
        share = forms[name].size // C
        first, mine = bases[name] // C, bases[name] + slot_in_order * share

        def add(at, size):
            to = pl.ds(pl.multiple_of(first + at, 16), size)
            here = pl.ds(pl.multiple_of(mine + at, 16), size)
            for d in range(W):
                total = psg[d, here].astype(F32)
                for e in range(others):
                    total = total + rx2[e, d, to].astype(F32)
                s2[d, to] = total.astype(BF16)

        tiles(share, add)
        moves = [(s2.at[d + 1, shared(name)], rx3.at[d, shared(name)], planes[d]) for d in range(W - 1)]
        return copies.start(moves, rx3.at[:, shared(name)])

    def plane_4(name, before):
        before.wait()
        share = forms[name].size // C
        first, mine = bases[name] // C, bases[name] + slot_in_order * share

        def add(at, size):
            to = pl.ds(pl.multiple_of(first + at, 16), size)
            total = s2[0, to].astype(F32)
            for d in range(W - 1):
                total = total + rx3[d, to].astype(F32)
            fo[pl.ds(pl.multiple_of(mine + at, 16), size)] = total.astype(BF16)

        tiles(share, add)
        there = fo.at[part(name, slot_in_order)]
        return copies.start([(there, there, device) for device in chips], fo.at[pl.ds(bases[name], others * share)])

    def plane_5(name, before):
        before.wait()
        there = fo.at[half(name, k)]
        return copies.start([(there, there, sibling)], there)

    def column_2(name, before):
        add_sibling(name, before)
        there = pl.ds(cfg["rz_at"][name], forms[name].size // 2)
        moves = [(psg.at[d + 1, half(name, k)], rz.at[d, there], planes[d]) for d in range(W - 1)]
        return copies.start(moves, rz.at[:, there])

    def column_3(name, before):
        before.wait()
        size_half, base = forms[name].size // 2, cfg["rz_at"][name]
        mine = bases[name] + k * size_half

        def add(at, size):
            total = psg[0, pl.ds(pl.multiple_of(mine + at, 16), size)].astype(F32)
            to = pl.ds(pl.multiple_of(base + at, 16), size)
            for d in range(W - 1):
                total = total + rz[d, to].astype(F32)
            tz[p, to] = total.astype(BF16)

        tiles(size_half, add)
        there = tz.at[p, pl.ds(base, size_half)]
        return copies.start(
            [(there, there, device) for device in chips], tz.at[pl.ds(0, others), pl.ds(base, size_half)]
        )

    def column_4(name, before):
        before.wait()
        size_half, base = forms[name].size // 2, cfg["rz_at"][name]
        mine = bases[name] + k * size_half

        def add(at, size):
            to = pl.ds(pl.multiple_of(base + at, 16), size)
            total = tz[0, to].astype(F32)
            for chip in range(1, half_chips):
                total = total + tz[chip, to].astype(F32)
            fo[pl.ds(pl.multiple_of(mine + at, 16), size)] = total.astype(BF16)

        tiles(size_half, add)
        there = fo.at[half(name, k)]
        return copies.start([(there, there, sibling)], there)

    def same_group(name, before):
        return before

    steps = {}
    for name in forms:
        first = cfg["z_first"]
        steps[name] = (column_2, column_3, column_4, same_group) if name in first else (plane_2, plane_3, plane_4, plane_5)
    going = {}

    def reduce(name, step):
        going[name] = reduce_1(name) if step == 1 else steps[name][step - 2](name, going[name])

    big[0 : H + 16, 0:D] = dot(a3[...], og_v[...], (1, 1))
    keep_row(2, big[H : H + 1, 0:D])
    pack_grad("out")
    reduce("out", 1)
    for tap in range(TAPS):
        rows = H + 16 if tap == TAPS - 1 else H
        value = dot(bb[tap * H : tap * H + rows], gv[...], (1, 1))
        taps_at[tap][0:H, 0:H] = value[0:H]
    keep_row(8, value[H : H + 1])
    reduce("out", 2)
    pack_grad("conv")
    reduce("conv", 1)
    for chunk in range(CHUNKS):
        h_passed.append(edge_forward(ha, h_first[chunk], chunk))
    reduce("conv", 2)
    edge_take(ha, h_passed, 1, nh)

    def second_back(chunk):
        here = slice(chunk * CW, (chunk + 1) * CW)
        for j in range(chunk * CJ, (chunk + 1) * CJ):
            tile, edge = slice(j * BLK, (j + 1) * BLK), slice(j * EDGE, (j + 1) * EDGE)
            own, late = gv[:, tile], nh[:, edge]
            shifted = (late * tall(k1[:, edge]))[:, :STEP]
            bb[0:H, tile] = own
            bb[H : 2 * H, tile] = jnp.concatenate([(own * tall(m1[:, tile]))[:, STEP:], shifted], axis=1)
            shifted = late * tall(k2[:, edge])
            bb[2 * H : 3 * H, tile] = jnp.concatenate([(own * tall(m2[:, tile]))[:, EDGE:], shifted], axis=1)
        c3[:, here] = dot(w_cv[...], bb[0 : TAPS * H, here])

        def step(i):
            lanes = lanes_at(chunk * CW + i * LG)
            mean, scaled = mu2[:, lanes], sc2[:, lanes]
            first, second = jnp.zeros((8, LG), F32), jnp.zeros((8, LG), F32)
            for f in blocks(H):
                normed = (h2[f, lanes] - mean) * scaled
                gain = dup(p4[0, f], LG)
                pre = normed * gain + dup(p4[1, f], LG)
                t = jnp.tanh(pre)
                upstream = c3[f, lanes] * ((1.0 + t) * (1.0 + pre * (1.0 - t)))
                acc4[0, f] += fold_lanes(upstream * normed)
                acc4[1, f] += fold_lanes(upstream)
                upstream = upstream * gain
                c3[f, lanes] = upstream
                first += fold_rows(upstream)
                second += fold_rows(upstream * normed)
            first, second = total_rows(first) * (1.0 / H), total_rows(second) * (1.0 / H)
            for f in blocks(H):
                normed = (h2[f, lanes] - mean) * scaled
                grad = (scaled * (c3[f, lanes] - first - normed * second)).astype(BF16)
                gh[f, lanes] = grad

        loop(CW // LG, step)

    second_back(0)
    second_back(1)
    reduce("out", 3)
    big[0 : D + 16, 0:H] = dot(a1[...], gh[...], (1, 1))
    keep_row(7, big[D : D + 1, 0:H])
    pack_grad("in")
    reduce("in", 1)

    def sums_rows(indices):
        for index in indices:
            (group, i, _, scale), _ = vec_at[index]
            keep_row(index, jnp.sum((acc8 if group == 8 else acc4)[i].T, 0, keepdims=True) * scale)

    def sums_plane(rows):
        vr[c, rows] = vx[rows]
        there = vr.at[c, rows]
        return copies.start([(there, there, (flip(c, m), z)) for m in range(1, C)], vr.at[pl.ds(0, C - 1), rows])

    def sums_column(rows, before):
        before.wait()
        total = vr[0, rows]
        for m in range(1, C):
            total = total + vr[m, rows]
        vs[rows] = total
        return copies.start([(vs.at[rows], vz.at[d, rows], planes[d]) for d in range(W - 1)], vz.at[:, rows])

    def sums_end(rows, before):
        before.wait()
        total = vs[rows]
        for d in range(W - 1):
            total = total + vz[d, rows]
        vo_ref[rows] = total

    late, early = slice(0, cfg["v_late"]), slice(cfg["v_late"], cfg["v_rows"])
    sums_rows((3, 4, 5, 6))
    v_early = sums_plane(early)
    reduce("conv", 3)
    for side in range(D // H):
        w_cvT[:, side * 512 : side * 512 + H] = w_out[:, side * H : (side + 1) * H].T

    def first_back(chunk):
        here = slice(chunk * CW, (chunk + 1) * CW)
        big[0:D, here] = dot(w_in[...], gh[:, here])

        def step(i):
            lanes = lanes_at(chunk * CW + i * LG)
            mean, scaled = mu1[:, lanes], sc1[:, lanes]
            first, second = jnp.zeros((8, LG), F32), jnp.zeros((8, LG), F32)
            for f in blocks(D):
                normed = (x_v[f, lanes].astype(F32) - mean) * scaled
                gain = dup(p8[0, f], LG)
                pre = normed * gain + dup(p8[1, f], LG)
                t = jnp.tanh(pre)
                upstream = big[f, lanes] * ((1.0 + t) * (1.0 + pre * (1.0 - t)))
                acc8[0, f] += fold_lanes(upstream * normed)
                acc8[1, f] += fold_lanes(upstream)
                upstream = upstream * gain
                big[f, lanes] = upstream
                first += fold_rows(upstream)
                second += fold_rows(upstream * normed)
            first, second = total_rows(first) * (1.0 / D), total_rows(second) * (1.0 / D)
            for f in blocks(D):
                normed = (x_v[f, lanes].astype(F32) - mean) * scaled
                grad = scaled * (big[f, lanes] - first - normed * second)
                big[f, lanes] = og_v[f, lanes].astype(F32) + grad

        loop(CW // LG, step)
        return local(chunk, big.at[0:D, here], ig_hbm.at[:, here])

    def last(chunk):
        here = slice(chunk * CW, (chunk + 1) * CW)
        for side, store in enumerate((c3, g3)):
            store[:, 0:CW] = dot(w_cvT[:, side * 512 : side * 512 + H], a3[0:H, here])

            def step(i, side=side, store=store):
                lanes, at = lanes_at(chunk * CW + i * LG), lanes_at(i * LG)
                for f in blocks(H):
                    to = slice(side * H + f.start, side * H + f.stop)
                    value = store[f, at] + dup(p8[2, to], LG)
                    x_v[to, lanes] = (x_v[to, lanes].astype(F32) + value).astype(BF16)

            loop(CW // LG, step)
        return local(2 + chunk, x_v.at[:, here], bo_hbm.at[:, here])

    def leave(n, name):
        rows = pl.ds(bases[name], forms[name].size)
        going[name].wait()
        return local(n, fo.at[rows], fo_hbm.at[rows])

    out_copies = [first_back(0)]
    reduce("in", 2)
    out_copies.append(first_back(1))
    sums_rows((0, 1))
    v_late = sums_plane(late)
    v_early = sums_column(early, v_early)
    reduce("in", 3)
    reduce("conv", 4)
    out_copies.append(last(0))
    v_late = sums_column(late, v_late)
    reduce("out", 4)
    out_copies.append(last(1))
    reduce("in", 4)
    reduce("conv", 5)
    out_copies.append(leave(4, "out"))
    sums_end(early, v_early)
    out_copies.append(leave(5, "conv"))
    reduce("in", 5)
    sums_end(late, v_late)
    out_copies.append(leave(6, "in"))
    for group in copies.groups:
        group.wait_sent()
    for copy in out_copies:
        copy.wait()


def spread(cfg, *refs):
    W, forms, bases, width, vec_at = (cfg[key] for key in ("W", "forms", "bases", "width", "vec_at"))
    bo_in, ig_in, fo_in, vx, bo_out, ig_out, gi_out, gc_out, go_out = refs[:9]
    vec_out, (ig_v, bo_v, fo, gi, gc, go, sem) = refs[9:18], refs[18:]
    z = lax.axis_index("wsh")
    used = 0

    def copy(source, target):
        nonlocal used
        used += 1
        move = pltpu.make_async_copy(source, target, sem.at[used - 1])
        move.start()
        return move

    grads = copy(fo_in, fo)
    pieces = []
    for source, stage, target in ((ig_in, ig_v, ig_out), (bo_in, bo_v, bo_out)):
        size = source.shape[0] // SPREAD
        for i in range(SPREAD):
            rows = pl.ds(i * size, size)
            pieces.append((copy(source.at[rows], stage.at[rows]), stage.at[rows], target.at[rows]))
    moves = []

    def pass_on(count):
        for come, stage, target in pieces[:count]:
            come.wait()
            moves.append(copy(stage, target))
        del pieces[:count]

    for ((_, _, count, _), at), target in zip(vec_at, vec_out):
        whole = jnp.concatenate([vx[at + t : at + t + 1] for t in range(-(-count // LANES))], axis=1)
        share = count // W
        mine = jnp.zeros((1, share), F32)
        for s in range(W):
            mine = jnp.where(z == s, whole[:, s * share : (s + 1) * share], mine)
        target[...] = mine.reshape(share)
    grads.wait()
    pass_on(2)
    for name, stage, target in (("conv", gc, gc_out), ("out", go, go_out), ("in", gi, gi_out)):
        form, base, parts = forms[name], bases[name], []
        for start, count, panels in form.plain_spans():
            values = [
                [
                    fo[base + row : base + row + count, lane : lane + columns].astype(F32)
                    for row, lane, columns in panel
                ]
                for panel in panels
            ]
            if name == "conv":
                for tap, part in enumerate(values):
                    stage[tap, start : start + count] = jnp.concatenate(part, axis=1)
            else:
                parts.append(jnp.concatenate(sum(values, []), axis=1))
                if name == "out":
                    stage[start : start + count] = parts[-1]
        if name == "in":
            stage[...] = jnp.concatenate(parts, axis=0).T
        moves.append(copy(stage, target))
        pass_on(2)
    pass_on(len(pieces))
    for move in moves:
        move.wait()


def on_device(
    block_in, out_grad, segments, block_deal, weight_in, weight_conv, weight_out,
    gain_first, shift_first, gain_second, shift_second, gain_third, shift_third, bias_first, bias_conv, bias_out,
):
    C, W = lax.axis_size("ctx"), lax.axis_size("wsh")
    _, rows, D = block_in.shape
    width = weight_in.shape[1]
    H = width * W
    panels = weight_out.shape[1] // width
    J = rows // BLK
    forms = {
        "in": Packed(D, 1, width, C),
        "conv": Packed(H, TAPS, width, C),
        "out": Packed(H, panels, width, C),
    }
    bases, total = {}, 0
    for name, form in forms.items():
        bases[name] = total
        total += form.size

    items = [(8, 0, D, 0.5), (8, 1, D, 0.5), (None, 0, D, 1.0)]
    items += [(4, i, H, 0.5) if i < 4 else (None, 0, H, 1.0) for i in range(6)]
    vec_at, at = [], 0
    for n, item in enumerate(items):
        if n == 2:
            at = v_late = up(at, 8)
        vec_at.append((item, at))
        at += -(-item[2] // LANES)
    v_rows = up(at, 8)
    cfg = {
        "C": C, "W": W, "J": J, "D": D, "H": H, "forms": forms, "bases": bases, "width": width, "vec_at": vec_at,
    }
    cfg["z_first"] = ("out",) if C <= 8 else ()
    cfg["z_only"] = ("out",)
    cfg["v_late"], cfg["v_rows"] = v_late, v_rows
    cfg["rz_at"], rz_rows = {}, 0
    for name in cfg["z_first"]:
        cfg["rz_at"][name] = rz_rows
        rz_rows += forms[name].size // 2
    rz_rows = max(rz_rows, 16)
    R = rows
    others = max(C // 2 - 1, 1)
    n_groups = 3 * 3 + 2 + 2 * 2 * CHUNKS + 3 * 5 + 4
    vmem = pltpu.VMEM
    scratch = [
        vmem((D, R), BF16),
        vmem((D, R), BF16),
        vmem((1, R), F32),
        vmem((1, R), F32),
        vmem((D + 16, R), BF16),
        vmem((H, R), F32),
        vmem((1, R), F32),
        vmem((1, R), F32),
        vmem((TAPS * H + 16, R), BF16),
        vmem((H + 16, R), BF16),
        vmem((H, R), BF16),
        vmem((H, R), BF16),
        vmem((D + 16, R), F32),
        vmem((H, R), F32),
        vmem((H, R), F32),
        vmem((16, R), BF16),
        vmem((16, R), BF16),
        vmem((16, J * EDGE), BF16),
        vmem((16, J * EDGE), BF16),
        vmem((D, H), BF16),
        vmem((H, D), BF16),
        vmem((H, TAPS * H), BF16),
        vmem((H, max(up(TAPS * H, LANES), 512 * (D // H))), BF16),
        vmem((H, D), BF16),
        vmem((W, total, LANES), BF16),
        vmem((W, 16, LANES), BF16),
        vmem((J * C, BLK), jnp.int32),
        vmem((2, C // 2, H, J * EDGE), BF16),
        vmem((2, C // 2, H, J * EDGE), BF16),
        vmem((H, J * EDGE), BF16),
        vmem((H, J * EDGE), BF16),
        vmem((W, total, LANES), BF16),
        vmem((W, total // 2, LANES), BF16),
        vmem((others, W, total // C, LANES), BF16),
        vmem((W, total // C, LANES), BF16),
        vmem((W - 1, total // C, LANES), BF16),
        vmem((W - 1, rz_rows, LANES), BF16),
        vmem((C // 2 if cfg["z_first"] else 1, rz_rows, LANES), BF16),
        vmem((total, LANES), BF16),
        vmem((3, D, LANES), F32),
        vmem((6, H, LANES), F32),
        vmem((2, D, LANES), F32),
        vmem((4, H, LANES), F32),
        vmem((v_rows, LANES), F32),
        vmem((C, v_rows, LANES), F32),
        vmem((v_rows, LANES), F32),
        vmem((W - 1, v_rows, LANES), F32),
        vmem((width, D), BF16),
        vmem((TAPS, H, width), BF16),
        vmem((H, panels * width), BF16),
        *[vmem((n // W,), BF16) for n in (D, D, H, H, H, H, H, H, D)],
        pltpu.SemaphoreType.DMA((15,)),
        pltpu.SemaphoreType.DMA((n_groups,)),
        pltpu.SemaphoreType.DMA((n_groups,)),
    ]
    any_spec = pl.BlockSpec(memory_space=pl.ANY)
    vmem_spec = pl.BlockSpec(memory_space=pltpu.VMEM)
    flat, tree = jax.tree.flatten(scratch)

    def run(*refs):
        kernel(cfg, *refs[:20], *jax.tree.unflatten(tree, refs[20:]))

    macs = R * (2 * D * H + TAPS * H * H) * 3
    bo, ig, fo, vo = pl.pallas_call(
        run,
        out_shape=(
            jax.ShapeDtypeStruct((D, R), BF16),
            jax.ShapeDtypeStruct((D, R), F32),
            jax.ShapeDtypeStruct((total, LANES), BF16),
            jax.ShapeDtypeStruct((v_rows, LANES), F32),
        ),
        in_specs=[pl.BlockSpec(memory_space=pltpu.SMEM)] + [any_spec] * 15,
        out_specs=(any_spec, any_spec, any_spec, vmem_spec),
        scratch_shapes=flat,
        compiler_params=pltpu.CompilerParams(
            collective_id=0, has_side_effects=True, vmem_limit_bytes=62 * 2**20
        ),
        cost_estimate=pl.CostEstimate(
            flops=2 * macs, bytes_accessed=10 * R * D, transcendentals=2 * R * (D + 2 * H)
        ),
        name="block",
    )(
        block_deal,
        block_in[0].T,
        out_grad[0].T,
        segments.reshape(J, BLK),
        weight_in.T,
        weight_conv,
        weight_out,
        gain_first, shift_first, gain_second, shift_second, gain_third, shift_third, bias_first, bias_conv, bias_out,
    )
    results = pl.pallas_call(
        lambda *refs: spread(cfg, *refs),
        out_shape=(
            jax.ShapeDtypeStruct((D, R), BF16),
            jax.ShapeDtypeStruct((D, R), F32),
            jax.ShapeDtypeStruct((width, D), F32),
            jax.ShapeDtypeStruct((TAPS, H, width), F32),
            jax.ShapeDtypeStruct((H, panels * width), F32),
        )
        + tuple(jax.ShapeDtypeStruct((item[2] // W,), F32) for item, _ in vec_at),
        in_specs=[any_spec, any_spec, any_spec, vmem_spec],
        out_specs=(any_spec,) * 5 + (vmem_spec,) * 9,
        scratch_shapes=[
            vmem((D, R), F32), vmem((D, R), BF16), vmem((total, LANES), BF16),
            vmem((width, D), F32), vmem((TAPS, H, width), F32), vmem((H, panels * width), F32),
            pltpu.SemaphoreType.DMA((4 * SPREAD + 4,)),
        ],
        compiler_params=pltpu.CompilerParams(vmem_limit_bytes=62 * 2**20),
        cost_estimate=pl.CostEstimate(flops=0, bytes_accessed=14 * R * D, transcendentals=0),
        name="spread",
    )(bo, ig, fo, vo)
    bo, ig, gi, gc, go = results[:5]
    vec = results[5:]
    return (bo.T[None], ig.T[None], gi.T, gc, go, vec[0], vec[1], *vec[3:], vec[2])


def solution(mesh):
    in_specs = (
        P("wsh", "ctx", None), P("wsh", "ctx", None), P("wsh", "ctx"), P(),
        P(None, "wsh"), P(None, None, "wsh"), P(None, "wsh"),
    ) + (P("wsh"),) * 9
    out_specs = (
        P("wsh", "ctx", None), P("wsh", "ctx", None),
        P(None, "wsh"), P(None, None, "wsh"), P(None, "wsh"),
    ) + (P("wsh"),) * 9
    return jax.shard_map(
        on_device, mesh=mesh, in_specs=in_specs, out_specs=out_specs, check_vma=False
    )
```

```python
import jax
import jax.numpy as jnp
from jax import lax
from jax.experimental import pallas as pl
from jax.experimental.pallas import tpu as pltpu
from jax.sharding import PartitionSpec as P

TAPS = 3
STEP = 16
BLK = 128
EDGE = (TAPS - 1) * STEP
EPS = 1e-05
LANES = 128
MESH = pl.DeviceIdType.MESH
F32 = jnp.float32
BF16 = jnp.bfloat16


def up(value, unit):
    return -(-value // unit) * unit


class Packed:
    def __init__(self, rows, panels, width, devices):
        self.rows, self.panels, self.width = rows, panels, width
        total = rows * panels
        if width % 4 == 0 and width > 64 and LANES - width >= width // 4 and total % 80 == 0:
            main, rest, quarter = total * 4 // 5, total // 5, width // 4
            self.parts = [(0, main, 0, width, 0, 0)]
            self.parts += [(main, rest, quarter * i, quarter, rest * i, width) for i in range(4)]
            used = main
        else:
            count = max(LANES // width, 1)
            used = up(-(-total // count), 16)
            self.parts = [
                (used * i, min(used, total - used * i), 0, width, 0, width * i)
                for i in range(count)
                if used * i < total
            ]
        self.used = used
        self.size = up(used, 16 * devices)

    def packed_spans(self):
        cuts = {0, self.used}
        for row, count, _, _, at, _ in self.parts:
            cuts |= {at, at + count}
            cuts |= {at + self.rows * h - row for h in range(self.panels) if row < self.rows * h < row + count}
        cuts = sorted(cuts)
        for start, end in zip(cuts, cuts[1:]):
            inside = []
            for row, count, column, columns, at, lane in self.parts:
                if at <= start and end <= at + count:
                    source = row + start - at
                    inside.append((source % self.rows, source // self.rows, column, columns, lane))
            yield start, end - start, sorted(inside, key=lambda item: item[-1])

    def plain_spans(self):
        cuts = {0, self.rows}
        for row, count, _, _, _, _ in self.parts:
            cuts |= {edge - self.rows * h for edge in (row, row + count) for h in range(self.panels)}
        cuts = sorted(cut for cut in cuts if 0 <= cut <= self.rows)
        for start, end in zip(cuts, cuts[1:]):
            panels = []
            for h in range(self.panels):
                first = self.rows * h + start
                inside = [
                    (column, at + first - row, lane, columns)
                    for row, count, column, columns, at, lane in self.parts
                    if row <= first < row + count
                ]
                panels.append([item[1:] for item in sorted(inside)])
            yield start, end - start, panels


def chunk_of(count):
    return next(size for size in (80, 64, 48, 32, 16) if count % size == 0)


def flip(value, mask):
    bit = 1
    out = value
    while bit <= mask:
        if mask & bit:
            out = out + bit - 2 * bit * ((value // bit) % 2)
        bit *= 2
    return out


def dot(a, b, contract=(1, 0)):
    return lax.dot_general(
        a, b, (((contract[0],), (contract[1],)), ((), ())), preferred_element_type=F32
    )


def dup(v, lanes):
    return jnp.concatenate([v] * (lanes // LANES), axis=1)


def fold_rows(v):
    out = v[0:8]
    for i in range(8, v.shape[0], 8):
        out = out + v[i : i + 8]
    return out


def fold_lanes(v):
    out = v[:, 0:LANES]
    for i in range(LANES, v.shape[1], LANES):
        out = out + v[:, i : i + LANES]
    return out


def total_rows(v):
    return jnp.sum(v, 0, keepdims=True)


class Group:
    def __init__(self, send, recv, moves, size):
        self.send, self.recv, self.size = send, recv, size
        for source, target, device in moves:
            pltpu.make_async_remote_copy(
                src_ref=source,
                dst_ref=target,
                send_sem=send,
                recv_sem=recv,
                device_id=device,
                device_id_type=MESH,
            ).start()

    def wait(self):
        pltpu.make_async_copy(self.size, self.size, self.recv).wait()

    def wait_sent(self):
        pltpu.make_async_copy(self.size, self.size, self.send).wait()


class Copies:
    def __init__(self, send, recv):
        self.send, self.recv, self.groups = send, recv, []

    def start(self, moves, size):
        n = len(self.groups)
        self.groups.append(Group(self.send.at[n], self.recv.at[n], moves, size))
        return self.groups[-1]


LG = 512
FB = 16
CHUNKS = 2
SPREAD = 5


def kernel(cfg, *refs):
    C, W, J, D, H = cfg["C"], cfg["W"], cfg["J"], cfg["D"], cfg["H"]
    forms, bases = cfg["forms"], cfg["bases"]
    width, vec_at = cfg["width"], cfg["vec_at"]
    half_chips = C // 2
    R = J * BLK
    CW = R // CHUNKS
    CJ = J // CHUNKS
    EW = CJ * EDGE
    (deal, x_hbm, og_hbm, seg_hbm, wi_hbm, wc_hbm, wo_hbm) = refs[:7]
    vec_hbm = refs[7:16]
    (bo_hbm, ig_hbm, fo_hbm, sm_hbm, vo_ref) = refs[16:21]
    (
        x_v, og_v, mu1, sc1, a1, h2, mu2, sc2, bb, a3, gv, gh, big, c3, g3,
        m1, m2, k1, k2, w_in, w_inT, w_cv, w_cvT, w_out, wps, vecb, sa, ta, ha, pt, nh,
        psg, rx1, rx2, s2, rx3, rz, tz, fo, p8, p4, acc8, acc4, vx, vr, vs, vz,
        wi_ref, wc_ref, wo_ref, *vec_refs, lsem, ssem, rsem,
    ) = refs[21:]

    c = lax.axis_index("ctx")
    z = lax.axis_index("wsh")
    k = c % 2
    p = c // 2
    slot_in_order = k * half_chips + p
    sibling = (flip(c, 1), z)
    chips = [(flip(c, 2 * e), z) for e in range(1, half_chips)]
    planes = [(c, flip(z, d)) for d in range(1, W)]
    copies = Copies(ssem, rsem)
    shards = range(W)

    def local(i, source, target):
        copy = pltpu.make_async_copy(source, target, lsem.at[i])
        copy.start()
        return copy

    def loop(count, body):
        lax.fori_loop(0, count, lambda i, carry: (body(i), carry)[1], 0)

    bar = pltpu.get_barrier_semaphore()
    for m in range(1, C):
        pl.semaphore_signal(bar, inc=1, device_id=(flip(c, m), z), device_id_type=MESH)
    for device in planes:
        pl.semaphore_signal(bar, inc=1, device_id=device, device_id_type=MESH)
    own_seg = sa.at[pl.ds(pl.multiple_of(c * J, 8), J)]
    w_copies = [local(n, *pair) for n, pair in enumerate(((wi_hbm, wi_ref), (wc_hbm, wc_ref), (wo_hbm, wo_ref)))]
    vec_copies = [local(3 + n, *pair) for n, pair in enumerate(zip(vec_hbm, vec_refs))]
    seg_copy = local(12, seg_hbm, own_seg)
    x_copy = local(13, x_hbm, x_v)
    og_copy = local(14, og_hbm, og_v)

    def pack(name, take, put, copies_of, dtype):
        form, base = forms[name], bases[name]
        for start, count, inside in form.packed_spans():
            size = chunk_of(count)

            def step(i, start=start, inside=inside, size=size):
                shift = i * size
                to = pl.ds(pl.multiple_of(base + start + shift, 16), size)
                for s in copies_of:
                    parts, lane = [], 0
                    for row, panel, column, columns, at in inside:
                        rows = pl.ds(pl.multiple_of(row + shift, 16), size)
                        parts.append(take(s, panel, rows, slice(column, column + columns)))
                        lane = at + columns
                    if lane < LANES:
                        parts.append(jnp.zeros((size, LANES - lane), dtype))
                    put(s, to, jnp.concatenate(parts, axis=1))

            loop(count // size, step)
        if form.size > form.used:
            for s in copies_of:
                rest = pl.ds(base + form.used, form.size - form.used)
                put(s, rest, jnp.zeros((form.size - form.used, LANES), dtype))

    def moved(columns, by):
        return slice(columns.start + by, columns.stop + by)

    def put_own(s, rows, value):
        wps[0, rows, :] = value

    own_shard = {
        "in": lambda s, panel, rows, columns: w_in[rows, columns],
        "conv": lambda s, panel, rows, columns: wc_ref[panel, rows, columns],
        "out": lambda s, panel, rows, columns: wo_ref[rows, moved(columns, width * panel)],
    }
    spans = cfg["spans"]

    def part(name, order):
        base, size = spans[name]
        return pl.ds(pl.multiple_of(base + order * (size // C), 16), size // C)

    def half(name, which):
        base, size = spans[name]
        return pl.ds(pl.multiple_of(base + which * (size // 2), 16), size // 2)

    others = half_chips - 1

    def z_send(name):
        rows = half(name, k) if name in cfg["z_only"] else part(name, slot_in_order)
        moves = [(wps.at[0, rows], wps.at[d + 1, rows], planes[d]) for d in range(W - 1)]
        return copies.start(moves, wps.at[pl.ds(1, W - 1), rows])

    def plane_send(name, before):
        if name in cfg["z_only"]:
            return before
        before.wait()
        there = wps.at[pl.ds(1, W - 1), part(name, slot_in_order)]
        base, size = spans[name]
        size = wps.at[pl.ds(1, W - 1), pl.ds(base, others * (size // C))]
        return copies.start([(there, there, device) for device in chips], size)

    def sibling_send(name, before):
        before.wait()
        there = wps.at[pl.ds(1, W - 1), half(name, k)]
        return copies.start([(there, there, sibling)], there)

    w_copies[0].wait()
    w_in[:, 0:width] = wi_ref[...].T
    pack("in", own_shard["in"], put_own, (0,), BF16)
    rows = []
    for ref, copy in zip(vec_refs, vec_copies):
        copy.wait()
        row = ref[...].astype(F32).reshape(1, ref.shape[0])
        for h in range(ref.shape[0] // width):
            rows.append(
                jnp.concatenate([row[:, h * width : (h + 1) * width], jnp.zeros((1, LANES - width), F32)], axis=1)
            )
    rows.append(jnp.zeros((16 - len(rows), LANES), F32))
    vecb[0] = jnp.concatenate(rows, axis=0).astype(BF16)
    pl.semaphore_wait(bar, C - 1 + W - 1)
    vec_sends = copies.start(
        [(vecb.at[0], vecb.at[d + 1], planes[d]) for d in range(W - 1)], vecb.at[pl.ds(1, W - 1)]
    )
    w_z = {name: z_send(name) for name in cfg["in_spans"]}
    for name, copy in (("conv", w_copies[1]), ("out", w_copies[2])):
        copy.wait()
        pack(name, own_shard[name], put_own, (0,), BF16)
        if name == "conv":
            w_z[name] = z_send(name)
    seg_copy.wait()
    seg_sends = copies.start(
        [(own_seg, own_seg, (flip(c, m), z)) for m in range(1, C)], sa.at[pl.ds(0, (C - 1) * J)]
    )
    acc8[...] = jnp.zeros_like(acc8)
    acc4[...] = jnp.zeros_like(acc4)
    a1[D : D + 16] = jnp.ones((16, R), BF16)
    a3[H : H + 16] = jnp.ones((16, R), BF16)
    bb[TAPS * H : TAPS * H + 16] = jnp.ones((16, R), BF16)
    vx[...] = jnp.zeros_like(vx)

    def unpack(name, target):
        form, base = forms[name], bases[name]
        for start, count, panels in form.plain_spans():
            size = chunk_of(count)
            order = [(s, panel) for s in shards for panel in panels]
            if name == "conv":
                order = [(s, panel) for panel in panels for s in shards]

            def step(i, start=start, order=order, size=size):
                shift = i * size
                parts = [
                    wps[flip(z, s), pl.ds(pl.multiple_of(base + row + shift, 16), size), lane : lane + columns]
                    for s, panel in order
                    for row, lane, columns in panel
                ]
                target[pl.ds(pl.multiple_of(start + shift, 16), size), :] = jnp.concatenate(parts, axis=1)

            loop(count // size, step)

    def lanes_at(start):
        return pl.ds(pl.multiple_of(start, LG), LG)

    def blocks(n):
        return [slice(f, f + FB) for f in range(0, n, FB)]

    x_copy.wait()

    def first_stats(i):
        lanes = lanes_at(i * LG)
        acc = jnp.zeros((8, LG), F32)
        for f in blocks(D):
            acc += fold_rows(x_v[f, lanes].astype(F32))
        mean = total_rows(acc) * (1.0 / D)
        acc = jnp.zeros((8, LG), F32)
        for f in blocks(D):
            centred = x_v[f, lanes].astype(F32) - mean
            acc += fold_rows(centred * centred)
        mu1[:, lanes] = mean
        sc1[:, lanes] = lax.rsqrt(total_rows(acc) * (1.0 / D) + EPS)

    loop(R // LG, first_stats)

    vec_sends.wait()
    vecs = [vecb[flip(z, s)].astype(F32) for s in shards]
    narrow = jnp.concatenate([v[:, :width] for v in vecs], axis=1).T
    for i in range(6):
        scale = 0.5 if i < 4 else 1.0
        p4[i] = jnp.broadcast_to(narrow[:, 4 + i : 5 + i] * scale, (H, LANES))
    broad = jnp.concatenate(
        [
            jnp.concatenate([v[at + h : at + h + 1, :width] for v in vecs for h in range(2)], axis=1)
            for at in (0, 2, 10)
        ]
        + [jnp.zeros((5, D), F32)],
        axis=0,
    ).T
    for i in range(3):
        scale = 0.5 if i < 2 else 1.0
        p8[i] = jnp.broadcast_to(broad[:, i : i + 1] * scale, (D, LANES))

    def first_act(i):
        lanes = lanes_at(i * LG)
        mean, scaled = mu1[:, lanes], sc1[:, lanes]
        for f in blocks(D):
            normed = (x_v[f, lanes].astype(F32) - mean) * scaled
            pre = normed * dup(p8[0, f], LG) + dup(p8[1, f], LG)
            a1[f, lanes] = (pre * jnp.tanh(pre) + pre).astype(BF16)

    w_plane = {name: plane_send(name, w_z[name]) for name in cfg["in_spans"]}
    loop(R // LG, first_act)
    w_sib = {name: sibling_send(name, w_plane[name]) for name in cfg["in_spans"]}
    w_plane["conv"] = plane_send("conv", w_z["conv"])
    w_z["out"] = z_send("out")
    for name in cfg["in_spans"]:
        w_sib[name].wait()
    unpack("in", w_in)
    w_inT[...] = w_in[...].T

    def second(chunk):
        here = slice(chunk * CW, (chunk + 1) * CW)
        h2[:, here] = dot(w_inT[...], a1[0:D, here])

        def step(i):
            lanes = lanes_at(chunk * CW + i * LG)
            acc = jnp.zeros((8, LG), F32)
            for f in blocks(H):
                value = h2[f, lanes] + dup(p4[4, f], LG)
                h2[f, lanes] = value
                acc += fold_rows(value)
            mean = total_rows(acc) * (1.0 / H)
            acc = jnp.zeros((8, LG), F32)
            for f in blocks(H):
                centred = h2[f, lanes] - mean
                acc += fold_rows(centred * centred)
            scaled = lax.rsqrt(total_rows(acc) * (1.0 / H) + EPS)
            mu2[:, lanes] = mean
            sc2[:, lanes] = scaled
            for f in blocks(H):
                normed = (h2[f, lanes] - mean) * scaled
                pre = normed * dup(p4[0, f], LG) + dup(p4[1, f], LG)
                bb[f, lanes] = (pre * jnp.tanh(pre) + pre).astype(BF16)

        loop(CW // LG, step)

    relay = half_chips == 4
    upper, lower = slice(0, H // 32 * 16), slice(H // 32 * 16, H)

    def edge_send(store, source, chunk, first):
        lanes = slice(chunk * EW, (chunk + 1) * EW)
        store[k, p, :, lanes] = jnp.concatenate(
            [source[0:H, j * BLK + first : j * BLK + first + EDGE] for j in range(chunk * CJ, (chunk + 1) * CJ)],
            axis=1,
        )
        there = store.at[k, p, :, lanes]
        if relay:
            return [copies.start([(there, there, device)], there) for device in chips[:2]]
        return [copies.start([(there, there, device) for device in chips], store.at[k, pl.ds(0, others), :, lanes])]

    def edge_relay(store, before, chunk):
        if not relay:
            return before
        lanes = slice(chunk * EW, (chunk + 1) * EW)
        before[0].wait()
        one = store.at[k, flip(p, 1), upper, lanes]
        near = store.at[k, pl.ds(p // 2 * 2, 2), :, lanes]
        first = copies.start([(one, one, chips[1])], one)
        near = copies.start([(near, near, sibling)], near)
        before[1].wait()
        two = store.at[k, flip(p, 2), lower, lanes]
        return [first, copies.start([(two, two, chips[0])], two), near]

    def edge_forward(store, before, chunk):
        lanes = slice(chunk * EW, (chunk + 1) * EW)
        for group in before[:2]:
            group.wait()
        there = store.at[k, pl.ds(flip(p, 2) // 2 * 2, 2), :, lanes] if relay else store.at[k, :, :, lanes]
        return before[2:] + [copies.start([(there, there, sibling)], there)]

    mine = [deal[c * J + j] for j in range(J)]
    edge_lane = lax.broadcasted_iota(jnp.int32, (1, J * EDGE), 1)
    edge_block = jnp.zeros((1, J * EDGE), jnp.int32)
    seg_block = jnp.zeros((J, BLK), jnp.int32)
    for j in range(J):
        inside = jnp.logical_and(edge_lane >= j * EDGE, edge_lane < (j + 1) * EDGE)
        edge_block = jnp.where(inside, mine[j], edge_block)
        seg_block = jnp.where(lax.broadcasted_iota(jnp.int32, (J, BLK), 0) == j, mine[j], seg_block)
    diagonal = jnp.where(
        lax.broadcasted_iota(jnp.int32, (EDGE, J * EDGE), 0)
        == lax.broadcasted_iota(jnp.int32, (EDGE, J * EDGE), 1) % EDGE,
        1.0,
        0.0,
    )

    def edge_take(store, waits, step, target):
        wanted = edge_block + step

        def choice(device):
            chosen = [diagonal * jnp.where(wanted == deal[device * J + j], 1.0, 0.0) for j in range(J)]
            return jnp.concatenate(chosen, axis=0).astype(BF16)

        ready = [choice(device) for device in range(C)] if C <= 8 else None
        for group in sum(waits, []):
            group.wait()
        total = jnp.zeros((H, J * EDGE), F32)
        for device in range(C):
            total += dot(store[device % 2, device // 2], ready[device] if ready else choice(device))
        target[...] = total.astype(BF16)

    def seg_take(step):
        wanted = seg_block + step
        out = jnp.full((J, BLK), -1, jnp.int32)
        for slot in range(C * J):
            out = jnp.where(wanted == deal[slot], jnp.broadcast_to(sa[slot : slot + 1], (J, BLK)), out)
        return out

    t_first, t_passed = [], []
    for chunk in range(CHUNKS):
        second(chunk)
        t_first.append(edge_send(ta, bb, chunk, BLK - EDGE))
    w_sib["conv"] = sibling_send("conv", w_plane["conv"])
    w_plane["out"] = plane_send("out", w_z["out"])
    w_sib["out"] = sibling_send("out", w_plane["out"])

    seg_sends.wait()
    own, before, behind = sa[pl.ds(pl.multiple_of(c * J, 8), J)], seg_take(-1), seg_take(1)
    cut = BLK - STEP

    def same(a, b):
        return jnp.where(a == b, 1.0, 0.0)

    keep_1 = same(own, jnp.concatenate([before[:, cut:], own[:, :cut]], axis=1))
    keep_2 = same(own, jnp.concatenate([before[:, BLK - EDGE :], own[:, : BLK - EDGE]], axis=1))
    next_1 = same(behind[:, :EDGE], jnp.concatenate([own[:, cut:], behind[:, :STEP]], axis=1))
    next_2 = same(behind[:, :EDGE], own[:, BLK - EDGE :])
    for target, mask, size in ((m1, keep_1, BLK), (m2, keep_2, BLK), (k1, next_1, EDGE), (k2, next_2, EDGE)):
        for j in range(J):
            target[:, j * size : (j + 1) * size] = jnp.broadcast_to(mask[j : j + 1], (16, size)).astype(BF16)

    def tall(mask):
        return jnp.concatenate([mask] * (H // 16), axis=0)

    w_sib["conv"].wait()
    unpack("conv", w_cv)
    t_first[0] = edge_relay(ta, t_first[0], 0)
    w_cvT[:, 0 : TAPS * H] = jnp.concatenate([w_cv[:, tap * H : (tap + 1) * H].T for tap in range(TAPS)], axis=1)
    w_sib["out"].wait()
    unpack("out", w_out)
    t_first[1] = edge_relay(ta, t_first[1], 1)
    og_copy.wait()
    for chunk in range(CHUNKS):
        here = slice(chunk * CW, (chunk + 1) * CW)
        g3[:, here] = dot(w_out[...], og_v[:, here])
        t_passed.append(edge_forward(ta, t_first[chunk], chunk))
    edge_take(ta, t_passed, -1, pt)

    def third(chunk):
        here = slice(chunk * CW, (chunk + 1) * CW)
        for j in range(chunk * CJ, (chunk + 1) * CJ):
            tile, edge = slice(j * BLK, (j + 1) * BLK), slice(j * EDGE, (j + 1) * EDGE)
            own, prev = bb[0:H, tile], pt[:, edge]
            bb[H : 2 * H, tile] = jnp.concatenate([prev[:, STEP:], own[:, :cut]], axis=1) * tall(m1[:, tile])
            bb[2 * H : 3 * H, tile] = jnp.concatenate([prev, own[:, : BLK - EDGE]], axis=1) * tall(m2[:, tile])
        c3[:, here] = dot(w_cvT[:, 0 : TAPS * H], bb[0 : TAPS * H, here])

        def step(i):
            lanes = lanes_at(chunk * CW + i * LG)
            acc = jnp.zeros((8, LG), F32)
            for f in blocks(H):
                value = c3[f, lanes] + dup(p4[5, f], LG)
                c3[f, lanes] = value
                acc += fold_rows(value)
            mean = total_rows(acc) * (1.0 / H)
            acc = jnp.zeros((8, LG), F32)
            for f in blocks(H):
                centred = c3[f, lanes] - mean
                acc += fold_rows(centred * centred)
            scaled = lax.rsqrt(total_rows(acc) * (1.0 / H) + EPS)
            first, second = jnp.zeros((8, LG), F32), jnp.zeros((8, LG), F32)
            for f in blocks(H):
                normed = (c3[f, lanes] - mean) * scaled
                gain = dup(p4[2, f], LG)
                pre = normed * gain + dup(p4[3, f], LG)
                t = jnp.tanh(pre)
                a3[f, lanes] = (pre * t + pre).astype(BF16)
                upstream = g3[f, lanes] * ((1.0 + t) * (1.0 + pre * (1.0 - t)))
                acc4[2, f] += fold_lanes(upstream * normed)
                acc4[3, f] += fold_lanes(upstream)
                upstream = upstream * gain
                g3[f, lanes] = upstream
                first += fold_rows(upstream)
                second += fold_rows(upstream * normed)
            first, second = total_rows(first) * (1.0 / H), total_rows(second) * (1.0 / H)
            for f in blocks(H):
                normed = (c3[f, lanes] - mean) * scaled
                grad = (scaled * (g3[f, lanes] - first - normed * second)).astype(BF16)
                gv[f, lanes] = grad

        loop(CW // LG, step)

    h_first, h_passed = [], []
    for chunk in range(CHUNKS):
        third(chunk)
        h_first.append(edge_send(ha, gv, chunk, 0))

    taps_at = (c3, g3, big)
    whole_grad = {
        "in": lambda s, panel, rows, columns: big[rows, moved(columns, width * s)],
        "conv": lambda s, panel, rows, columns: taps_at[panel][rows, moved(columns, width * s)],
        "out": lambda s, panel, rows, columns: big[rows, moved(columns, width * (forms["out"].panels * s + panel))],
    }

    def put_grad(s, rows, value):
        psg[flip(z, s), rows, :] = value.astype(BF16)

    def pack_grad(name):
        pack(name, whole_grad[name], put_grad, shards, F32)

    def halved(name):
        return pl.ds(bases[name] // 2, forms[name].size // 2)

    def shared(name):
        return pl.ds(bases[name] // C, forms[name].size // C)

    def keep_row(index, row):
        at, count = vec_at[index][1], row.shape[1]
        for t in range(-(-count // LANES)):
            size = min(LANES, count - t * LANES)
            vx[at + t : at + t + 1, 0:size] = row[:, t * LANES : t * LANES + size]

    def tiles(rows, body):
        size = chunk_of(rows)
        loop(rows // size, lambda i: body(pl.multiple_of(i * size, 16), size))

    def reduce_1(name):
        there = rx1.at[:, halved(name)]
        return copies.start([(psg.at[:, half(name, 1 - k)], there, sibling)], there)

    def add_sibling(name, before):
        before.wait()
        form = forms[name]
        first, mine = bases[name] // 2, bases[name] + k * (form.size // 2)

        def add(at, size):
            to = pl.ds(pl.multiple_of(first + at, 16), size)
            here = pl.ds(pl.multiple_of(mine + at, 16), size)
            for d in range(W):
                psg[d, here] = (psg[d, here].astype(F32) + rx1[d, to].astype(F32)).astype(BF16)

        tiles(form.size // 2, add)
        return mine

    def plane_2(name, before):
        mine = add_sibling(name, before)
        share = forms[name].size // C
        moves = []
        for e, device in enumerate(chips):
            rows = pl.ds(pl.multiple_of(mine + flip(p, e + 1) * share, 16), share)
            moves.append((psg.at[:, rows], rx2.at[e, :, shared(name)], device))
        return copies.start(moves, rx2.at[:, :, shared(name)])

    def plane_3(name, before):
        before.wait()
        share = forms[name].size // C
        first, mine = bases[name] // C, bases[name] + slot_in_order * share

        def add(at, size):
            to = pl.ds(pl.multiple_of(first + at, 16), size)
            here = pl.ds(pl.multiple_of(mine + at, 16), size)
            for d in range(W):
                total = psg[d, here].astype(F32)
                for e in range(others):
                    total = total + rx2[e, d, to].astype(F32)
                s2[d, to] = total.astype(BF16)

        tiles(share, add)
        moves = [(s2.at[d + 1, shared(name)], rx3.at[d, shared(name)], planes[d]) for d in range(W - 1)]
        return copies.start(moves, rx3.at[:, shared(name)])

    def plane_4(name, before):
        before.wait()
        share = forms[name].size // C
        first, mine = bases[name] // C, bases[name] + slot_in_order * share

        def add(at, size):
            to = pl.ds(pl.multiple_of(first + at, 16), size)
            total = s2[0, to].astype(F32)
            for d in range(W - 1):
                total = total + rx3[d, to].astype(F32)
            fo[pl.ds(pl.multiple_of(mine + at, 16), size)] = total.astype(BF16)

        tiles(share, add)
        there = fo.at[part(name, slot_in_order)]
        devices = [(flip(c, m), z) for m in range(1, C)] if name in cfg["direct"] else chips
        return copies.start(
            [(there, there, device) for device in devices], fo.at[pl.ds(bases[name], len(devices) * share)]
        )

    def plane_5(name, before):
        if name in cfg["direct"]:
            return before
        before.wait()
        there = fo.at[half(name, k)]
        return copies.start([(there, there, sibling)], there)

    def column_2(name, before):
        add_sibling(name, before)
        there = pl.ds(cfg["rz_at"][name], forms[name].size // 2)
        moves = [(psg.at[d + 1, half(name, k)], rz.at[d, there], planes[d]) for d in range(W - 1)]
        return copies.start(moves, rz.at[:, there])

    def column_3(name, before):
        before.wait()
        size_half, base = forms[name].size // 2, cfg["rz_at"][name]
        mine = bases[name] + k * size_half

        def add(at, size):
            total = psg[0, pl.ds(pl.multiple_of(mine + at, 16), size)].astype(F32)
            to = pl.ds(pl.multiple_of(base + at, 16), size)
            for d in range(W - 1):
                total = total + rz[d, to].astype(F32)
            tz[p, to] = total.astype(BF16)

        tiles(size_half, add)
        there = tz.at[p, pl.ds(base, size_half)]
        return copies.start(
            [(there, there, device) for device in chips], tz.at[pl.ds(0, others), pl.ds(base, size_half)]
        )

    def column_4(name, before):
        before.wait()
        size_half, base = forms[name].size // 2, cfg["rz_at"][name]
        mine = bases[name] + k * size_half

        def add(at, size):
            to = pl.ds(pl.multiple_of(base + at, 16), size)
            total = tz[0, to].astype(F32)
            for chip in range(1, half_chips):
                total = total + tz[chip, to].astype(F32)
            fo[pl.ds(pl.multiple_of(mine + at, 16), size)] = total.astype(BF16)

        tiles(size_half, add)
        there = fo.at[half(name, k)]
        return copies.start([(there, there, sibling)], there)

    def same_group(name, before):
        return before

    steps = {}
    for name in forms:
        first = cfg["z_first"]
        steps[name] = (column_2, column_3, column_4, same_group) if name in first else (plane_2, plane_3, plane_4, plane_5)
    going = {}

    def reduce(name, step):
        going[name] = reduce_1(name) if step == 1 else steps[name][step - 2](name, going[name])

    big[0 : H + 16, 0:D] = dot(a3[...], og_v[...], (1, 1))
    keep_row(2, big[H : H + 1, 0:D])
    h_first[0] = edge_relay(ha, h_first[0], 0)
    pack_grad("out")
    reduce("out", 1)
    h_first[1] = edge_relay(ha, h_first[1], 1)
    for tap in range(TAPS):
        rows = H + 16 if tap == TAPS - 1 else H
        value = dot(bb[tap * H : tap * H + rows], gv[...], (1, 1))
        taps_at[tap][0:H, 0:H] = value[0:H]
    keep_row(8, value[H : H + 1])
    reduce("out", 2)
    h_passed.append(edge_forward(ha, h_first[0], 0))
    pack_grad("conv")
    reduce("conv", 1)
    h_passed.append(edge_forward(ha, h_first[1], 1))
    edge_take(ha, h_passed, 1, nh)
    reduce("conv", 2)

    def second_back(chunk):
        here = slice(chunk * CW, (chunk + 1) * CW)
        for j in range(chunk * CJ, (chunk + 1) * CJ):
            tile, edge = slice(j * BLK, (j + 1) * BLK), slice(j * EDGE, (j + 1) * EDGE)
            own, late = gv[:, tile], nh[:, edge]
            shifted = (late * tall(k1[:, edge]))[:, :STEP]
            bb[0:H, tile] = own
            bb[H : 2 * H, tile] = jnp.concatenate([(own * tall(m1[:, tile]))[:, STEP:], shifted], axis=1)
            shifted = late * tall(k2[:, edge])
            bb[2 * H : 3 * H, tile] = jnp.concatenate([(own * tall(m2[:, tile]))[:, EDGE:], shifted], axis=1)
        c3[:, here] = dot(w_cv[...], bb[0 : TAPS * H, here])

        def step(i):
            lanes = lanes_at(chunk * CW + i * LG)
            mean, scaled = mu2[:, lanes], sc2[:, lanes]
            first, second = jnp.zeros((8, LG), F32), jnp.zeros((8, LG), F32)
            for f in blocks(H):
                normed = (h2[f, lanes] - mean) * scaled
                gain = dup(p4[0, f], LG)
                pre = normed * gain + dup(p4[1, f], LG)
                t = jnp.tanh(pre)
                upstream = c3[f, lanes] * ((1.0 + t) * (1.0 + pre * (1.0 - t)))
                acc4[0, f] += fold_lanes(upstream * normed)
                acc4[1, f] += fold_lanes(upstream)
                upstream = upstream * gain
                c3[f, lanes] = upstream
                first += fold_rows(upstream)
                second += fold_rows(upstream * normed)
            first, second = total_rows(first) * (1.0 / H), total_rows(second) * (1.0 / H)
            for f in blocks(H):
                normed = (h2[f, lanes] - mean) * scaled
                grad = (scaled * (c3[f, lanes] - first - normed * second)).astype(BF16)
                gh[f, lanes] = grad

        loop(CW // LG, step)

    second_back(0)
    second_back(1)
    big[0 : D + 16, 0:H] = dot(a1[...], gh[...], (1, 1))
    reduce("out", 3)
    keep_row(7, big[D : D + 1, 0:H])
    pack_grad("in")
    reduce("in", 1)

    def sums_rows(indices):
        for index in indices:
            (group, i, _, scale), _ = vec_at[index]
            keep_row(index, jnp.sum((acc8 if group == 8 else acc4)[i].T, 0, keepdims=True) * scale)

    def sums_plane(rows):
        vr[c, rows] = vx[rows]
        there = vr.at[c, rows]
        return copies.start([(there, there, (flip(c, m), z)) for m in range(1, C)], vr.at[pl.ds(0, C - 1), rows])

    def sums_column(rows, before):
        before.wait()
        total = vr[0, rows]
        for m in range(1, C):
            total = total + vr[m, rows]
        vs[rows] = total
        return copies.start([(vs.at[rows], vz.at[d, rows], planes[d]) for d in range(W - 1)], vz.at[:, rows])

    def sums_end(rows, before):
        before.wait()
        total = vs[rows]
        for d in range(W - 1):
            total = total + vz[d, rows]
        vo_ref[rows] = total

    late, early = slice(0, cfg["v_late"]), slice(cfg["v_late"], cfg["v_rows"])
    sums_rows((3, 4, 5, 6))
    v_early = sums_plane(early)
    reduce("conv", 3)
    for side in range(D // H):
        w_cvT[:, side * 512 : side * 512 + H] = w_out[:, side * H : (side + 1) * H].T

    def first_back(chunk):
        here = slice(chunk * CW, (chunk + 1) * CW)
        big[0:D, here] = dot(w_in[...], gh[:, here])

        def step(i):
            lanes = lanes_at(chunk * CW + i * LG)
            mean, scaled = mu1[:, lanes], sc1[:, lanes]
            first, second = jnp.zeros((8, LG), F32), jnp.zeros((8, LG), F32)
            for f in blocks(D):
                normed = (x_v[f, lanes].astype(F32) - mean) * scaled
                gain = dup(p8[0, f], LG)
                pre = normed * gain + dup(p8[1, f], LG)
                t = jnp.tanh(pre)
                upstream = big[f, lanes] * ((1.0 + t) * (1.0 + pre * (1.0 - t)))
                acc8[0, f] += fold_lanes(upstream * normed)
                acc8[1, f] += fold_lanes(upstream)
                upstream = upstream * gain
                big[f, lanes] = upstream
                first += fold_rows(upstream)
                second += fold_rows(upstream * normed)
            first, second = total_rows(first) * (1.0 / D), total_rows(second) * (1.0 / D)
            for f in blocks(D):
                normed = (x_v[f, lanes].astype(F32) - mean) * scaled
                grad = scaled * (big[f, lanes] - first - normed * second)
                big[f, lanes] = og_v[f, lanes].astype(F32) + grad

        loop(CW // LG, step)
        return local(chunk, big.at[0:D, here], ig_hbm.at[:, here])

    def last(chunk):
        here = slice(chunk * CW, (chunk + 1) * CW)
        for side, store in enumerate((c3, g3)):
            store[:, 0:CW] = dot(w_cvT[:, side * 512 : side * 512 + H], a3[0:H, here])

            def step(i, side=side, store=store):
                lanes, at = lanes_at(chunk * CW + i * LG), lanes_at(i * LG)
                for f in blocks(H):
                    to = slice(side * H + f.start, side * H + f.stop)
                    value = store[f, at] + dup(p8[2, to], LG)
                    x_v[to, lanes] = (x_v[to, lanes].astype(F32) + value).astype(BF16)

            loop(CW // LG, step)
        return local(2 + chunk, x_v.at[:, here], bo_hbm.at[:, here])

    def leave(n, name):
        going[name].wait()
        form, base = forms[name], bases[name]
        if name == "in":
            rows = pl.ds(base, form.size)
            return local(n, fo.at[rows], fo_hbm)
        for start, count, panels in form.plain_spans():
            values = [
                [fo[base + row : base + row + count, lane : lane + columns].astype(F32) for row, lane, columns in panel]
                for panel in panels
            ]
            for at, value in zip(cfg["small_at"][name], values if name == "conv" else [sum(values, [])]):
                value = jnp.concatenate(value, axis=1)
                h2[start : start + count, at : at + value.shape[1]] = value
        first, last_lane = cfg["small_at"][name][0], cfg["small_end"][name]
        return local(n, h2.at[:, first:last_lane], sm_hbm.at[:, first:last_lane])

    out_copies = [first_back(0)]
    reduce("in", 2)
    out_copies.append(first_back(1))
    sums_rows((0, 1))
    v_late = sums_plane(late)
    v_early = sums_column(early, v_early)
    reduce("in", 3)
    reduce("conv", 4)
    out_copies.append(last(0))
    v_late = sums_column(late, v_late)
    reduce("out", 4)
    out_copies.append(last(1))
    reduce("in", 4)
    reduce("conv", 5)
    out_copies.append(leave(4, "out"))
    sums_end(early, v_early)
    out_copies.append(leave(5, "conv"))
    reduce("in", 5)
    sums_end(late, v_late)
    out_copies.append(leave(6, "in"))
    for group in copies.groups:
        group.wait_sent()
    for copy in out_copies:
        copy.wait()


def spread(cfg, *refs):
    W, forms, bases, width, vec_at = (cfg[key] for key in ("W", "forms", "bases", "width", "vec_at"))
    bo_in, ig_in, fo_in, sm_in, vx_in, bo_out, ig_out, gi_out, gc_out, go_out = refs[:10]
    vec_out, (ig_v, bo_v, fo, sm, vx, gi, gc, go), vec_v, sem = refs[10:19], refs[19:27], refs[27:36], refs[36]
    z = lax.axis_index("wsh")
    used = 0

    def copy(source, target):
        nonlocal used
        used += 1
        move = pltpu.make_async_copy(source, target, sem.at[used - 1])
        move.start()
        return move

    early, pieces, moves = [], [], []
    for source, stage, target in ((ig_in, ig_v, ig_out), (bo_in, bo_v, bo_out)):
        size = source.shape[0] // SPREAD
        for i in range(SPREAD):
            rows = pl.ds(i * size, size)
            pieces.append((copy(source.at[rows], stage.at[rows]), stage.at[rows], target.at[rows]))
        if not early:
            early = [copy(fo_in, fo), copy(sm_in, sm), copy(vx_in, vx)]

    def pass_on(count):
        for come, stage, target in pieces[:count]:
            come.wait()
            moves.append(copy(stage, target))
        del pieces[:count]

    pass_on(SPREAD)
    early[0].wait()
    form, parts = forms["in"], []
    for _, count, panels in form.plain_spans():
        values = [fo[row : row + count, lane : lane + columns] for panel in panels for row, lane, columns in panel]
        parts.append(jnp.concatenate(values, axis=1))
    gi[...] = jnp.concatenate(parts, axis=0).astype(F32).T
    moves.append(copy(gi, gi_out))
    pass_on(SPREAD)
    early[1].wait()
    for tap, at in enumerate(cfg["small_at"]["conv"]):
        gc[tap] = sm[:, at : at + width]
    at = cfg["small_at"]["out"][0]
    go[...] = sm[:, at : at + go.shape[1]]
    moves += [copy(gc, gc_out), copy(go, go_out)]
    early[2].wait()
    for ((_, _, count, _), at), stage, target in zip(vec_at, vec_v, vec_out):
        whole = jnp.concatenate([vx[at + t : at + t + 1] for t in range(-(-count // LANES))], axis=1)
        share = count // W
        mine = jnp.zeros((1, share), F32)
        for s in range(W):
            mine = jnp.where(z == s, whole[:, s * share : (s + 1) * share], mine)
        stage[...] = mine.reshape(share)
        moves.append(copy(stage, target))
    for move in moves:
        move.wait()


def on_device(
    block_in, out_grad, segments, block_deal, weight_in, weight_conv, weight_out,
    gain_first, shift_first, gain_second, shift_second, gain_third, shift_third, bias_first, bias_conv, bias_out,
):
    C, W = lax.axis_size("ctx"), lax.axis_size("wsh")
    _, rows, D = block_in.shape
    width = weight_in.shape[1]
    H = width * W
    panels = weight_out.shape[1] // width
    J = rows // BLK
    forms = {
        "in": Packed(D, 1, width, C),
        "conv": Packed(H, TAPS, width, C),
        "out": Packed(H, panels, width, C),
    }
    bases, total = {}, 0
    for name, form in forms.items():
        bases[name] = total
        total += form.size

    items = [(8, 0, D, 0.5), (8, 1, D, 0.5), (None, 0, D, 1.0)]
    items += [(4, i, H, 0.5) if i < 4 else (None, 0, H, 1.0) for i in range(6)]
    vec_at, at = [], 0
    for n, item in enumerate(items):
        if n == 2:
            at = v_late = up(at, 8)
        vec_at.append((item, at))
        at += -(-item[2] // LANES)
    v_rows = up(at, 8)
    cfg = {
        "C": C, "W": W, "J": J, "D": D, "H": H, "forms": forms, "bases": bases, "width": width, "vec_at": vec_at,
    }
    cfg["z_first"] = ("out",) if C <= 8 else ()
    cfg["spans"] = {name: (bases[name], form.size) for name, form in forms.items()}
    straight = forms["in"].size * 2 // 5
    if C <= 8 and straight % 32 == 0 and (forms["in"].size - straight) % (16 * C) == 0:
        cfg["in_spans"] = ("in_shared", "in_straight")
        cfg["spans"]["in_straight"] = (bases["in"], straight)
        cfg["spans"]["in_shared"] = (bases["in"] + straight, forms["in"].size - straight)
    else:
        cfg["in_spans"] = ("in",)
    cfg["z_only"] = ("out", "in_straight")
    cfg["small_at"] = {"conv": [tap * up(width, LANES) for tap in range(TAPS)], "out": [TAPS * up(width, LANES)]}
    small = cfg["small_at"]["out"][0] + up(panels * width, LANES)
    cfg["small_end"] = {"conv": cfg["small_at"]["out"][0], "out": small}
    cfg["direct"] = ("in",) if C <= 8 else ()
    cfg["v_late"], cfg["v_rows"] = v_late, v_rows
    cfg["rz_at"], rz_rows = {}, 0
    for name in cfg["z_first"]:
        cfg["rz_at"][name] = rz_rows
        rz_rows += forms[name].size // 2
    rz_rows = max(rz_rows, 16)
    R = rows
    others = max(C // 2 - 1, 1)
    n_groups = 4 * 3 + 2 + 2 * 6 * CHUNKS + 3 * 5 + 4
    vmem = pltpu.VMEM
    scratch = [
        vmem((D, R), BF16),
        vmem((D, R), BF16),
        vmem((1, R), F32),
        vmem((1, R), F32),
        vmem((D + 16, R), BF16),
        vmem((H, R), F32),
        vmem((1, R), F32),
        vmem((1, R), F32),
        vmem((TAPS * H + 16, R), BF16),
        vmem((H + 16, R), BF16),
        vmem((H, R), BF16),
        vmem((H, R), BF16),
        vmem((D + 16, R), F32),
        vmem((H, R), F32),
        vmem((H, R), F32),
        vmem((16, R), BF16),
        vmem((16, R), BF16),
        vmem((16, J * EDGE), BF16),
        vmem((16, J * EDGE), BF16),
        vmem((D, H), BF16),
        vmem((H, D), BF16),
        vmem((H, TAPS * H), BF16),
        vmem((H, max(up(TAPS * H, LANES), 512 * (D // H))), BF16),
        vmem((H, D), BF16),
        vmem((W, total, LANES), BF16),
        vmem((W, 16, LANES), BF16),
        vmem((J * C, BLK), jnp.int32),
        vmem((2, C // 2, H, J * EDGE), BF16),
        vmem((2, C // 2, H, J * EDGE), BF16),
        vmem((H, J * EDGE), BF16),
        vmem((H, J * EDGE), BF16),
        vmem((W, total, LANES), BF16),
        vmem((W, total // 2, LANES), BF16),
        vmem((others, W, total // C, LANES), BF16),
        vmem((W, total // C, LANES), BF16),
        vmem((W - 1, total // C, LANES), BF16),
        vmem((W - 1, rz_rows, LANES), BF16),
        vmem((C // 2 if cfg["z_first"] else 1, rz_rows, LANES), BF16),
        vmem((total, LANES), BF16),
        vmem((3, D, LANES), F32),
        vmem((6, H, LANES), F32),
        vmem((2, D, LANES), F32),
        vmem((4, H, LANES), F32),
        vmem((v_rows, LANES), F32),
        vmem((C, v_rows, LANES), F32),
        vmem((v_rows, LANES), F32),
        vmem((W - 1, v_rows, LANES), F32),
        vmem((width, D), BF16),
        vmem((TAPS, H, width), BF16),
        vmem((H, panels * width), BF16),
        *[vmem((n // W,), BF16) for n in (D, D, H, H, H, H, H, H, D)],
        pltpu.SemaphoreType.DMA((15,)),
        pltpu.SemaphoreType.DMA((n_groups,)),
        pltpu.SemaphoreType.DMA((n_groups,)),
    ]
    any_spec = pl.BlockSpec(memory_space=pl.ANY)
    vmem_spec = pl.BlockSpec(memory_space=pltpu.VMEM)
    flat, tree = jax.tree.flatten(scratch)

    def run(*refs):
        kernel(cfg, *refs[:21], *jax.tree.unflatten(tree, refs[21:]))

    macs = R * (2 * D * H + TAPS * H * H) * 3
    bo, ig, fo, sm, vo = pl.pallas_call(
        run,
        out_shape=(
            jax.ShapeDtypeStruct((D, R), BF16),
            jax.ShapeDtypeStruct((D, R), F32),
            jax.ShapeDtypeStruct((forms["in"].size, LANES), BF16),
            jax.ShapeDtypeStruct((H, small), F32),
            jax.ShapeDtypeStruct((v_rows, LANES), F32),
        ),
        in_specs=[pl.BlockSpec(memory_space=pltpu.SMEM)] + [any_spec] * 15,
        out_specs=(any_spec, any_spec, any_spec, any_spec, vmem_spec),
        scratch_shapes=flat,
        compiler_params=pltpu.CompilerParams(
            collective_id=0, has_side_effects=True, vmem_limit_bytes=62 * 2**20
        ),
        cost_estimate=pl.CostEstimate(
            flops=2 * macs, bytes_accessed=10 * R * D, transcendentals=2 * R * (D + 2 * H)
        ),
        name="block",
    )(
        block_deal,
        block_in[0].T,
        out_grad[0].T,
        segments.reshape(J, BLK),
        weight_in.T,
        weight_conv,
        weight_out,
        gain_first, shift_first, gain_second, shift_second, gain_third, shift_third, bias_first, bias_conv, bias_out,
    )
    results = pl.pallas_call(
        lambda *refs: spread(cfg, *refs),
        out_shape=(
            jax.ShapeDtypeStruct((D, R), BF16),
            jax.ShapeDtypeStruct((D, R), F32),
            jax.ShapeDtypeStruct((width, D), F32),
            jax.ShapeDtypeStruct((TAPS, H, width), F32),
            jax.ShapeDtypeStruct((H, panels * width), F32),
        )
        + tuple(jax.ShapeDtypeStruct((item[2] // W,), F32) for item, _ in vec_at),
        in_specs=[any_spec] * 5,
        out_specs=(any_spec,) * 14,
        scratch_shapes=[
            vmem((D, R), F32), vmem((D, R), BF16), vmem((forms["in"].size, LANES), BF16), vmem((H, small), F32),
            vmem((v_rows, LANES), F32), vmem((width, D), F32), vmem((TAPS, H, width), F32),
            vmem((H, panels * width), F32), *[vmem((item[2] // W,), F32) for item, _ in vec_at],
            pltpu.SemaphoreType.DMA((4 * SPREAD + 15,)),
        ],
        compiler_params=pltpu.CompilerParams(vmem_limit_bytes=62 * 2**20),
        cost_estimate=pl.CostEstimate(flops=0, bytes_accessed=14 * R * D, transcendentals=0),
        name="spread",
    )(bo, ig, fo, sm, vo)
    bo, ig, gi, gc, go = results[:5]
    vec = results[5:]
    return (bo.T[None], ig.T[None], gi.T, gc, go, vec[0], vec[1], *vec[3:], vec[2])


def solution(mesh):
    in_specs = (
        P("wsh", "ctx", None), P("wsh", "ctx", None), P("wsh", "ctx"), P(),
        P(None, "wsh"), P(None, None, "wsh"), P(None, "wsh"),
    ) + (P("wsh"),) * 9
    out_specs = (
        P("wsh", "ctx", None), P("wsh", "ctx", None),
        P(None, "wsh"), P(None, None, "wsh"), P(None, "wsh"),
    ) + (P("wsh"),) * 9
    return jax.shard_map(
        on_device, mesh=mesh, in_specs=in_specs, out_specs=out_specs, check_vma=False
    )
```

```python
import jax
import jax.numpy as jnp
from jax import lax
from jax.experimental import pallas as pl
from jax.experimental.pallas import tpu as pltpu
from jax.sharding import PartitionSpec as P

TAPS = 3
STEP = 16
BLK = 128
EDGE = (TAPS - 1) * STEP
EPS = 1e-05
LANES = 128
MESH = pl.DeviceIdType.MESH
F32 = jnp.float32
BF16 = jnp.bfloat16


def up(value, unit):
    return -(-value // unit) * unit


class Packed:
    def __init__(self, rows, panels, width, devices):
        self.rows, self.panels, self.width = rows, panels, width
        total = rows * panels
        if width % 4 == 0 and width > 64 and LANES - width >= width // 4 and total % 80 == 0:
            main, rest, quarter = total * 4 // 5, total // 5, width // 4
            self.parts = [(0, main, 0, width, 0, 0)]
            self.parts += [(main, rest, quarter * i, quarter, rest * i, width) for i in range(4)]
            used = main
        else:
            count = max(LANES // width, 1)
            used = up(-(-total // count), 16)
            self.parts = [
                (used * i, min(used, total - used * i), 0, width, 0, width * i)
                for i in range(count)
                if used * i < total
            ]
        self.used = used
        self.size = up(used, 16 * devices)

    def packed_spans(self):
        cuts = {0, self.used}
        for row, count, _, _, at, _ in self.parts:
            cuts |= {at, at + count}
            cuts |= {at + self.rows * h - row for h in range(self.panels) if row < self.rows * h < row + count}
        cuts = sorted(cuts)
        for start, end in zip(cuts, cuts[1:]):
            inside = []
            for row, count, column, columns, at, lane in self.parts:
                if at <= start and end <= at + count:
                    source = row + start - at
                    inside.append((source % self.rows, source // self.rows, column, columns, lane))
            yield start, end - start, sorted(inside, key=lambda item: item[-1])

    def plain_spans(self):
        cuts = {0, self.rows}
        for row, count, _, _, _, _ in self.parts:
            cuts |= {edge - self.rows * h for edge in (row, row + count) for h in range(self.panels)}
        cuts = sorted(cut for cut in cuts if 0 <= cut <= self.rows)
        for start, end in zip(cuts, cuts[1:]):
            panels = []
            for h in range(self.panels):
                first = self.rows * h + start
                inside = [
                    (column, at + first - row, lane, columns)
                    for row, count, column, columns, at, lane in self.parts
                    if row <= first < row + count
                ]
                panels.append([item[1:] for item in sorted(inside)])
            yield start, end - start, panels


def chunk_of(count):
    return next(size for size in (80, 64, 48, 32, 16) if count % size == 0)


def flip(value, mask):
    bit = 1
    out = value
    while bit <= mask:
        if mask & bit:
            out = out + bit - 2 * bit * ((value // bit) % 2)
        bit *= 2
    return out


def dot(a, b, contract=(1, 0)):
    return lax.dot_general(
        a, b, (((contract[0],), (contract[1],)), ((), ())), preferred_element_type=F32
    )


def dup(v, lanes):
    return jnp.concatenate([v] * (lanes // LANES), axis=1)


def fold_rows(v):
    out = v[0:8]
    for i in range(8, v.shape[0], 8):
        out = out + v[i : i + 8]
    return out


def fold_lanes(v):
    out = v[:, 0:LANES]
    for i in range(LANES, v.shape[1], LANES):
        out = out + v[:, i : i + LANES]
    return out


def total_rows(v):
    return jnp.sum(v, 0, keepdims=True)


class Group:
    def __init__(self, send, recv, moves, size):
        self.send, self.recv, self.size = send, recv, size
        for source, target, device in moves:
            pltpu.make_async_remote_copy(
                src_ref=source,
                dst_ref=target,
                send_sem=send,
                recv_sem=recv,
                device_id=device,
                device_id_type=MESH,
            ).start()

    def wait(self):
        pltpu.make_async_copy(self.size, self.size, self.recv).wait()

    def wait_sent(self):
        pltpu.make_async_copy(self.size, self.size, self.send).wait()


class Copies:
    def __init__(self, send, recv):
        self.send, self.recv, self.groups = send, recv, []

    def start(self, moves, size):
        n = len(self.groups)
        self.groups.append(Group(self.send.at[n], self.recv.at[n], moves, size))
        return self.groups[-1]


LG = 512
FB = 16
CHUNKS = 2
SPREAD = 5


def kernel(cfg, *refs):
    C, W, J, D, H = cfg["C"], cfg["W"], cfg["J"], cfg["D"], cfg["H"]
    forms, bases = cfg["forms"], cfg["bases"]
    width, vec_at = cfg["width"], cfg["vec_at"]
    half_chips = C // 2
    R = J * BLK
    CW = R // CHUNKS
    CJ = J // CHUNKS
    EW = CJ * EDGE
    (deal, x_hbm, og_hbm, seg_hbm, wi_hbm, wc_hbm, wo_hbm) = refs[:7]
    vec_hbm = refs[7:16]
    (bo_hbm, ig_hbm, fo_hbm, sm_hbm, vo_ref) = refs[16:21]
    (
        x_v, og_v, mu1, sc1, a1, h2, mu2, sc2, bb, a3, gv, gh, big, c3, g3,
        m1, m2, k1, k2, w_in, w_inT, w_cv, w_cvT, w_out, wps, vecb, sa, ta, ha, pt, nh,
        psg, rx1, rx2, s2, rx3, rz, tz, fo, p8, p4, acc8, acc4, vx, vr, vs, vz,
        wi_ref, wc_ref, wo_ref, *vec_refs, lsem, ssem, rsem,
    ) = refs[21:]

    c = lax.axis_index("ctx")
    z = lax.axis_index("wsh")
    k = c % 2
    p = c // 2
    slot_in_order = k * half_chips + p
    sibling = (flip(c, 1), z)
    chips = [(flip(c, 2 * e), z) for e in range(1, half_chips)]
    planes = [(c, flip(z, d)) for d in range(1, W)]
    copies = Copies(ssem, rsem)
    shards = range(W)

    def local(i, source, target):
        copy = pltpu.make_async_copy(source, target, lsem.at[i])
        copy.start()
        return copy

    def loop(count, body):
        lax.fori_loop(0, count, lambda i, carry: (body(i), carry)[1], 0)

    bar = pltpu.get_barrier_semaphore()
    for m in range(1, C):
        pl.semaphore_signal(bar, inc=1, device_id=(flip(c, m), z), device_id_type=MESH)
    for device in planes:
        pl.semaphore_signal(bar, inc=1, device_id=device, device_id_type=MESH)
    own_seg = sa.at[pl.ds(pl.multiple_of(c * J, 8), J)]
    w_copies = [local(n, *pair) for n, pair in enumerate(((wi_hbm, wi_ref), (wc_hbm, wc_ref), (wo_hbm, wo_ref)))]
    vec_copies = [local(3 + n, *pair) for n, pair in enumerate(zip(vec_hbm, vec_refs))]
    seg_copy = local(12, seg_hbm, own_seg)
    x_copy = local(13, x_hbm, x_v)
    og_copy = local(14, og_hbm, og_v)

    def pack(name, take, put, copies_of, dtype):
        form, base = forms[name], bases[name]
        for start, count, inside in form.packed_spans():
            size = chunk_of(count)

            def step(i, start=start, inside=inside, size=size):
                shift = i * size
                to = pl.ds(pl.multiple_of(base + start + shift, 16), size)
                for s in copies_of:
                    parts, lane = [], 0
                    for row, panel, column, columns, at in inside:
                        rows = pl.ds(pl.multiple_of(row + shift, 16), size)
                        parts.append(take(s, panel, rows, slice(column, column + columns)))
                        lane = at + columns
                    if lane < LANES:
                        parts.append(jnp.zeros((size, LANES - lane), dtype))
                    put(s, to, jnp.concatenate(parts, axis=1))

            loop(count // size, step)
        if form.size > form.used:
            for s in copies_of:
                rest = pl.ds(base + form.used, form.size - form.used)
                put(s, rest, jnp.zeros((form.size - form.used, LANES), dtype))

    def moved(columns, by):
        return slice(columns.start + by, columns.stop + by)

    def put_own(s, rows, value):
        wps[0, rows, :] = value

    own_shard = {
        "in": lambda s, panel, rows, columns: w_in[rows, columns],
        "conv": lambda s, panel, rows, columns: wc_ref[panel, rows, columns],
        "out": lambda s, panel, rows, columns: wo_ref[rows, moved(columns, width * panel)],
    }
    spans = cfg["spans"]

    def part(name, order):
        base, size = spans[name]
        return pl.ds(pl.multiple_of(base + order * (size // C), 16), size // C)

    def half(name, which):
        base, size = spans[name]
        return pl.ds(pl.multiple_of(base + which * (size // 2), 16), size // 2)

    others = half_chips - 1

    def z_send(name):
        rows = half(name, k) if name in cfg["z_only"] else part(name, slot_in_order)
        moves = [(wps.at[0, rows], wps.at[d + 1, rows], planes[d]) for d in range(W - 1)]
        return copies.start(moves, wps.at[pl.ds(1, W - 1), rows])

    def plane_send(name, before):
        if name in cfg["z_only"]:
            return before
        before.wait()
        there = wps.at[pl.ds(1, W - 1), part(name, slot_in_order)]
        base, size = spans[name]
        size = wps.at[pl.ds(1, W - 1), pl.ds(base, others * (size // C))]
        return copies.start([(there, there, device) for device in chips], size)

    def sibling_send(name, before):
        before.wait()
        there = wps.at[pl.ds(1, W - 1), half(name, k)]
        return copies.start([(there, there, sibling)], there)

    w_copies[0].wait()
    w_in[:, 0:width] = wi_ref[...].T
    pack("in", own_shard["in"], put_own, (0,), BF16)
    pl.semaphore_wait(bar, C - 1 + W - 1)
    w_z = {name: z_send(name) for name in cfg["in_spans"][:1]}
    rows = []
    for ref, copy in zip(vec_refs, vec_copies):
        copy.wait()
        row = ref[...].astype(F32).reshape(1, ref.shape[0])
        for h in range(ref.shape[0] // width):
            rows.append(
                jnp.concatenate([row[:, h * width : (h + 1) * width], jnp.zeros((1, LANES - width), F32)], axis=1)
            )
    rows.append(jnp.zeros((16 - len(rows), LANES), F32))
    vecb[0] = jnp.concatenate(rows, axis=0).astype(BF16)
    vec_sends = copies.start(
        [(vecb.at[0], vecb.at[d + 1], planes[d]) for d in range(W - 1)], vecb.at[pl.ds(1, W - 1)]
    )
    w_z.update({name: z_send(name) for name in cfg["in_spans"][1:]})
    for name, copy in (("conv", w_copies[1]), ("out", w_copies[2])):
        copy.wait()
        pack(name, own_shard[name], put_own, (0,), BF16)
        if name == "conv":
            w_z[name] = z_send(name)
    seg_copy.wait()
    seg_sends = copies.start(
        [(own_seg, own_seg, (flip(c, m), z)) for m in range(1, C)], sa.at[pl.ds(0, (C - 1) * J)]
    )
    acc8[...] = jnp.zeros_like(acc8)
    acc4[...] = jnp.zeros_like(acc4)
    a1[D : D + 16] = jnp.ones((16, R), BF16)
    a3[H : H + 16] = jnp.ones((16, R), BF16)
    bb[TAPS * H : TAPS * H + 16] = jnp.ones((16, R), BF16)
    vx[...] = jnp.zeros_like(vx)

    def unpack(name, target):
        form, base = forms[name], bases[name]
        for start, count, panels in form.plain_spans():
            size = chunk_of(count)
            order = [(s, panel) for s in shards for panel in panels]
            if name == "conv":
                order = [(s, panel) for panel in panels for s in shards]

            def step(i, start=start, order=order, size=size):
                shift = i * size
                parts = [
                    wps[flip(z, s), pl.ds(pl.multiple_of(base + row + shift, 16), size), lane : lane + columns]
                    for s, panel in order
                    for row, lane, columns in panel
                ]
                target[pl.ds(pl.multiple_of(start + shift, 16), size), :] = jnp.concatenate(parts, axis=1)

            loop(count // size, step)

    def lanes_at(start):
        return pl.ds(pl.multiple_of(start, LG), LG)

    def blocks(n):
        return [slice(f, f + FB) for f in range(0, n, FB)]

    x_copy.wait()

    def first_stats(i):
        lanes = lanes_at(i * LG)
        acc = jnp.zeros((8, LG), F32)
        for f in blocks(D):
            acc += fold_rows(x_v[f, lanes].astype(F32))
        mean = total_rows(acc) * (1.0 / D)
        acc = jnp.zeros((8, LG), F32)
        for f in blocks(D):
            centred = x_v[f, lanes].astype(F32) - mean
            acc += fold_rows(centred * centred)
        mu1[:, lanes] = mean
        sc1[:, lanes] = lax.rsqrt(total_rows(acc) * (1.0 / D) + EPS)

    loop(R // LG, first_stats)
    w_plane = {name: plane_send(name, w_z[name]) for name in cfg["in_spans"]}

    vec_sends.wait()
    vecs = [vecb[flip(z, s)].astype(F32) for s in shards]
    narrow = jnp.concatenate([v[:, :width] for v in vecs], axis=1).T
    for i in range(6):
        scale = 0.5 if i < 4 else 1.0
        p4[i] = jnp.broadcast_to(narrow[:, 4 + i : 5 + i] * scale, (H, LANES))
    broad = jnp.concatenate(
        [
            jnp.concatenate([v[at + h : at + h + 1, :width] for v in vecs for h in range(2)], axis=1)
            for at in (0, 2, 10)
        ]
        + [jnp.zeros((5, D), F32)],
        axis=0,
    ).T
    for i in range(3):
        scale = 0.5 if i < 2 else 1.0
        p8[i] = jnp.broadcast_to(broad[:, i : i + 1] * scale, (D, LANES))

    def first_act(i):
        lanes = lanes_at(i * LG)
        mean, scaled = mu1[:, lanes], sc1[:, lanes]
        for f in blocks(D):
            normed = (x_v[f, lanes].astype(F32) - mean) * scaled
            pre = normed * dup(p8[0, f], LG) + dup(p8[1, f], LG)
            a1[f, lanes] = (pre * jnp.tanh(pre) + pre).astype(BF16)

    loop(R // LG, first_act)
    w_sib = {name: sibling_send(name, w_plane[name]) for name in cfg["in_spans"]}
    w_plane["conv"] = plane_send("conv", w_z["conv"])
    w_z["out"] = z_send("out")
    for name in cfg["in_spans"]:
        w_sib[name].wait()
    unpack("in", w_in)
    w_inT[...] = w_in[...].T

    def second(chunk):
        here = slice(chunk * CW, (chunk + 1) * CW)
        h2[:, here] = dot(w_inT[...], a1[0:D, here])

        def step(i):
            lanes = lanes_at(chunk * CW + i * LG)
            acc = jnp.zeros((8, LG), F32)
            for f in blocks(H):
                value = h2[f, lanes] + dup(p4[4, f], LG)
                h2[f, lanes] = value
                acc += fold_rows(value)
            mean = total_rows(acc) * (1.0 / H)
            acc = jnp.zeros((8, LG), F32)
            for f in blocks(H):
                centred = h2[f, lanes] - mean
                acc += fold_rows(centred * centred)
            scaled = lax.rsqrt(total_rows(acc) * (1.0 / H) + EPS)
            mu2[:, lanes] = mean
            sc2[:, lanes] = scaled
            for f in blocks(H):
                normed = (h2[f, lanes] - mean) * scaled
                pre = normed * dup(p4[0, f], LG) + dup(p4[1, f], LG)
                bb[f, lanes] = (pre * jnp.tanh(pre) + pre).astype(BF16)

        loop(CW // LG, step)

    relay = half_chips == 4
    upper, lower = slice(0, H // 32 * 16), slice(H // 32 * 16, H)

    def edge_send(store, source, chunk, first):
        lanes = slice(chunk * EW, (chunk + 1) * EW)
        store[k, p, :, lanes] = jnp.concatenate(
            [source[0:H, j * BLK + first : j * BLK + first + EDGE] for j in range(chunk * CJ, (chunk + 1) * CJ)],
            axis=1,
        )
        there = store.at[k, p, :, lanes]
        if relay:
            return [copies.start([(there, there, device)], there) for device in chips[:2]]
        return [copies.start([(there, there, device) for device in chips], store.at[k, pl.ds(0, others), :, lanes])]

    def edge_relay(store, before, chunk):
        if not relay:
            return before
        lanes = slice(chunk * EW, (chunk + 1) * EW)
        before[0].wait()
        one = store.at[k, flip(p, 1), upper, lanes]
        near = store.at[k, pl.ds(p // 2 * 2, 2), :, lanes]
        first = copies.start([(one, one, chips[1])], one)
        near = copies.start([(near, near, sibling)], near)
        before[1].wait()
        two = store.at[k, flip(p, 2), lower, lanes]
        return [first, copies.start([(two, two, chips[0])], two), near]

    def edge_forward(store, before, chunk):
        lanes = slice(chunk * EW, (chunk + 1) * EW)
        for group in before[:2]:
            group.wait()
        there = store.at[k, pl.ds(flip(p, 2) // 2 * 2, 2), :, lanes] if relay else store.at[k, :, :, lanes]
        return before[2:] + [copies.start([(there, there, sibling)], there)]

    mine = [deal[c * J + j] for j in range(J)]
    edge_lane = lax.broadcasted_iota(jnp.int32, (1, J * EDGE), 1)
    edge_block = jnp.zeros((1, J * EDGE), jnp.int32)
    seg_block = jnp.zeros((J, BLK), jnp.int32)
    for j in range(J):
        inside = jnp.logical_and(edge_lane >= j * EDGE, edge_lane < (j + 1) * EDGE)
        edge_block = jnp.where(inside, mine[j], edge_block)
        seg_block = jnp.where(lax.broadcasted_iota(jnp.int32, (J, BLK), 0) == j, mine[j], seg_block)
    diagonal = jnp.where(
        lax.broadcasted_iota(jnp.int32, (EDGE, J * EDGE), 0)
        == lax.broadcasted_iota(jnp.int32, (EDGE, J * EDGE), 1) % EDGE,
        1.0,
        0.0,
    )

    def edge_take(store, waits, step, target):
        wanted = edge_block + step

        def choice(device):
            chosen = [diagonal * jnp.where(wanted == deal[device * J + j], 1.0, 0.0) for j in range(J)]
            return jnp.concatenate(chosen, axis=0).astype(BF16)

        ready = [choice(device) for device in range(C)] if C <= 8 else None
        for group in sum(waits, []):
            group.wait()
        total = jnp.zeros((H, J * EDGE), F32)
        for device in range(C):
            total += dot(store[device % 2, device // 2], ready[device] if ready else choice(device))
        target[...] = total.astype(BF16)

    def seg_take(step):
        wanted = seg_block + step
        out = jnp.full((J, BLK), -1, jnp.int32)
        for slot in range(C * J):
            out = jnp.where(wanted == deal[slot], jnp.broadcast_to(sa[slot : slot + 1], (J, BLK)), out)
        return out

    t_first, t_passed = [], []
    for chunk in range(CHUNKS):
        second(chunk)
        t_first.append(edge_send(ta, bb, chunk, BLK - EDGE))
    w_sib["conv"] = sibling_send("conv", w_plane["conv"])
    w_plane["out"] = plane_send("out", w_z["out"])
    w_sib["out"] = sibling_send("out", w_plane["out"])

    seg_sends.wait()
    own, before, behind = sa[pl.ds(pl.multiple_of(c * J, 8), J)], seg_take(-1), seg_take(1)
    cut = BLK - STEP

    def same(a, b):
        return jnp.where(a == b, 1.0, 0.0)

    keep_1 = same(own, jnp.concatenate([before[:, cut:], own[:, :cut]], axis=1))
    keep_2 = same(own, jnp.concatenate([before[:, BLK - EDGE :], own[:, : BLK - EDGE]], axis=1))
    next_1 = same(behind[:, :EDGE], jnp.concatenate([own[:, cut:], behind[:, :STEP]], axis=1))
    next_2 = same(behind[:, :EDGE], own[:, BLK - EDGE :])
    for target, mask, size in ((m1, keep_1, BLK), (m2, keep_2, BLK), (k1, next_1, EDGE), (k2, next_2, EDGE)):
        for j in range(J):
            target[:, j * size : (j + 1) * size] = jnp.broadcast_to(mask[j : j + 1], (16, size)).astype(BF16)

    def tall(mask):
        return jnp.concatenate([mask] * (H // 16), axis=0)

    t_first[0] = edge_relay(ta, t_first[0], 0)
    w_sib["conv"].wait()
    unpack("conv", w_cv)
    t_first[1] = edge_relay(ta, t_first[1], 1)
    w_cvT[:, 0 : TAPS * H] = jnp.concatenate([w_cv[:, tap * H : (tap + 1) * H].T for tap in range(TAPS)], axis=1)
    w_sib["out"].wait()
    unpack("out", w_out)
    t_passed.append(edge_forward(ta, t_first[0], 0))
    og_copy.wait()
    for chunk in range(CHUNKS):
        here = slice(chunk * CW, (chunk + 1) * CW)
        g3[:, here] = dot(w_out[...], og_v[:, here])
        if chunk == 0:
            t_passed.append(edge_forward(ta, t_first[1], 1))
    edge_take(ta, t_passed, -1, pt)

    def third(chunk):
        here = slice(chunk * CW, (chunk + 1) * CW)
        for j in range(chunk * CJ, (chunk + 1) * CJ):
            tile, edge = slice(j * BLK, (j + 1) * BLK), slice(j * EDGE, (j + 1) * EDGE)
            own, prev = bb[0:H, tile], pt[:, edge]
            bb[H : 2 * H, tile] = jnp.concatenate([prev[:, STEP:], own[:, :cut]], axis=1) * tall(m1[:, tile])
            bb[2 * H : 3 * H, tile] = jnp.concatenate([prev, own[:, : BLK - EDGE]], axis=1) * tall(m2[:, tile])
        c3[:, here] = dot(w_cvT[:, 0 : TAPS * H], bb[0 : TAPS * H, here])

        def step(i):
            lanes = lanes_at(chunk * CW + i * LG)
            acc = jnp.zeros((8, LG), F32)
            for f in blocks(H):
                value = c3[f, lanes] + dup(p4[5, f], LG)
                c3[f, lanes] = value
                acc += fold_rows(value)
            mean = total_rows(acc) * (1.0 / H)
            acc = jnp.zeros((8, LG), F32)
            for f in blocks(H):
                centred = c3[f, lanes] - mean
                acc += fold_rows(centred * centred)
            scaled = lax.rsqrt(total_rows(acc) * (1.0 / H) + EPS)
            first, second = jnp.zeros((8, LG), F32), jnp.zeros((8, LG), F32)
            for f in blocks(H):
                normed = (c3[f, lanes] - mean) * scaled
                gain = dup(p4[2, f], LG)
                pre = normed * gain + dup(p4[3, f], LG)
                t = jnp.tanh(pre)
                a3[f, lanes] = (pre * t + pre).astype(BF16)
                upstream = g3[f, lanes] * ((1.0 + t) * (1.0 + pre * (1.0 - t)))
                acc4[2, f] += fold_lanes(upstream * normed)
                acc4[3, f] += fold_lanes(upstream)
                upstream = upstream * gain
                g3[f, lanes] = upstream
                first += fold_rows(upstream)
                second += fold_rows(upstream * normed)
            first, second = total_rows(first) * (1.0 / H), total_rows(second) * (1.0 / H)
            for f in blocks(H):
                normed = (c3[f, lanes] - mean) * scaled
                grad = (scaled * (g3[f, lanes] - first - normed * second)).astype(BF16)
                gv[f, lanes] = grad

        loop(CW // LG, step)

    h_first, h_passed = [], []
    for chunk in range(CHUNKS):
        third(chunk)
        h_first.append(edge_send(ha, gv, chunk, 0))

    taps_at = (c3, g3, big)
    whole_grad = {
        "in": lambda s, panel, rows, columns: big[rows, moved(columns, width * s)],
        "conv": lambda s, panel, rows, columns: taps_at[panel][rows, moved(columns, width * s)],
        "out": lambda s, panel, rows, columns: big[rows, moved(columns, width * (forms["out"].panels * s + panel))],
    }

    def put_grad(s, rows, value):
        psg[flip(z, s), rows, :] = value.astype(BF16)

    def pack_grad(name):
        pack(name, whole_grad[name], put_grad, shards, F32)

    def halved(name):
        return pl.ds(bases[name] // 2, forms[name].size // 2)

    def shared(name):
        return pl.ds(bases[name] // C, forms[name].size // C)

    def keep_row(index, row):
        at, count = vec_at[index][1], row.shape[1]
        for t in range(-(-count // LANES)):
            size = min(LANES, count - t * LANES)
            vx[at + t : at + t + 1, 0:size] = row[:, t * LANES : t * LANES + size]

    def tiles(rows, body):
        size = chunk_of(rows)
        loop(rows // size, lambda i: body(pl.multiple_of(i * size, 16), size))

    def reduce_1(name):
        there = rx1.at[:, halved(name)]
        return copies.start([(psg.at[:, half(name, 1 - k)], there, sibling)], there)

    def add_sibling(name, before):
        before.wait()
        form = forms[name]
        first, mine = bases[name] // 2, bases[name] + k * (form.size // 2)

        def add(at, size):
            to = pl.ds(pl.multiple_of(first + at, 16), size)
            here = pl.ds(pl.multiple_of(mine + at, 16), size)
            for d in range(W):
                psg[d, here] = (psg[d, here].astype(F32) + rx1[d, to].astype(F32)).astype(BF16)

        tiles(form.size // 2, add)
        return mine

    def plane_2(name, before):
        mine = add_sibling(name, before)
        share = forms[name].size // C
        moves = []
        for e, device in enumerate(chips):
            rows = pl.ds(pl.multiple_of(mine + flip(p, e + 1) * share, 16), share)
            moves.append((psg.at[:, rows], rx2.at[e, :, shared(name)], device))
        return copies.start(moves, rx2.at[:, :, shared(name)])

    def plane_3(name, before):
        before.wait()
        share = forms[name].size // C
        first, mine = bases[name] // C, bases[name] + slot_in_order * share

        def add(at, size):
            to = pl.ds(pl.multiple_of(first + at, 16), size)
            here = pl.ds(pl.multiple_of(mine + at, 16), size)
            for d in range(W):
                total = psg[d, here].astype(F32)
                for e in range(others):
                    total = total + rx2[e, d, to].astype(F32)
                s2[d, to] = total.astype(BF16)

        tiles(share, add)
        moves = [(s2.at[d + 1, shared(name)], rx3.at[d, shared(name)], planes[d]) for d in range(W - 1)]
        return copies.start(moves, rx3.at[:, shared(name)])

    def plane_4(name, before):
        before.wait()
        share = forms[name].size // C
        first, mine = bases[name] // C, bases[name] + slot_in_order * share

        def add(at, size):
            to = pl.ds(pl.multiple_of(first + at, 16), size)
            total = s2[0, to].astype(F32)
            for d in range(W - 1):
                total = total + rx3[d, to].astype(F32)
            fo[pl.ds(pl.multiple_of(mine + at, 16), size)] = total.astype(BF16)

        tiles(share, add)
        there = fo.at[part(name, slot_in_order)]
        devices = [(flip(c, m), z) for m in range(1, C)] if name in cfg["direct"] else chips
        return copies.start(
            [(there, there, device) for device in devices], fo.at[pl.ds(bases[name], len(devices) * share)]
        )

    def plane_5(name, before):
        if name in cfg["direct"]:
            return before
        before.wait()
        there = fo.at[half(name, k)]
        return copies.start([(there, there, sibling)], there)

    def column_2(name, before):
        add_sibling(name, before)
        there = pl.ds(cfg["rz_at"][name], forms[name].size // 2)
        moves = [(psg.at[d + 1, half(name, k)], rz.at[d, there], planes[d]) for d in range(W - 1)]
        return copies.start(moves, rz.at[:, there])

    def column_3(name, before):
        before.wait()
        size_half, base = forms[name].size // 2, cfg["rz_at"][name]
        mine = bases[name] + k * size_half

        def add(at, size):
            total = psg[0, pl.ds(pl.multiple_of(mine + at, 16), size)].astype(F32)
            to = pl.ds(pl.multiple_of(base + at, 16), size)
            for d in range(W - 1):
                total = total + rz[d, to].astype(F32)
            tz[p, to] = total.astype(BF16)

        tiles(size_half, add)
        there = tz.at[p, pl.ds(base, size_half)]
        return copies.start(
            [(there, there, device) for device in chips], tz.at[pl.ds(0, others), pl.ds(base, size_half)]
        )

    def column_4(name, before):
        before.wait()
        size_half, base = forms[name].size // 2, cfg["rz_at"][name]
        mine = bases[name] + k * size_half

        def add(at, size):
            to = pl.ds(pl.multiple_of(base + at, 16), size)
            total = tz[0, to].astype(F32)
            for chip in range(1, half_chips):
                total = total + tz[chip, to].astype(F32)
            fo[pl.ds(pl.multiple_of(mine + at, 16), size)] = total.astype(BF16)

        tiles(size_half, add)
        there = fo.at[half(name, k)]
        return copies.start([(there, there, sibling)], there)

    def same_group(name, before):
        return before

    steps = {}
    for name in forms:
        first = cfg["z_first"]
        steps[name] = (column_2, column_3, column_4, same_group) if name in first else (plane_2, plane_3, plane_4, plane_5)
    going = {}

    def reduce(name, step):
        going[name] = reduce_1(name) if step == 1 else steps[name][step - 2](name, going[name])

    big[0 : H + 16, 0:D] = dot(a3[...], og_v[...], (1, 1))
    keep_row(2, big[H : H + 1, 0:D])
    h_first[0] = edge_relay(ha, h_first[0], 0)
    pack_grad("out")
    reduce("out", 1)
    h_first[1] = edge_relay(ha, h_first[1], 1)
    for tap in range(TAPS):
        rows = H + 16 if tap == TAPS - 1 else H
        value = dot(bb[tap * H : tap * H + rows], gv[...], (1, 1))
        taps_at[tap][0:H, 0:H] = value[0:H]
    keep_row(8, value[H : H + 1])
    reduce("out", 2)
    h_passed.append(edge_forward(ha, h_first[0], 0))
    pack_grad("conv")
    reduce("conv", 1)
    h_passed.append(edge_forward(ha, h_first[1], 1))
    reduce("conv", 2)
    edge_take(ha, h_passed, 1, nh)

    def second_back(chunk):
        here = slice(chunk * CW, (chunk + 1) * CW)
        for j in range(chunk * CJ, (chunk + 1) * CJ):
            tile, edge = slice(j * BLK, (j + 1) * BLK), slice(j * EDGE, (j + 1) * EDGE)
            own, late = gv[:, tile], nh[:, edge]
            shifted = (late * tall(k1[:, edge]))[:, :STEP]
            bb[0:H, tile] = own
            bb[H : 2 * H, tile] = jnp.concatenate([(own * tall(m1[:, tile]))[:, STEP:], shifted], axis=1)
            shifted = late * tall(k2[:, edge])
            bb[2 * H : 3 * H, tile] = jnp.concatenate([(own * tall(m2[:, tile]))[:, EDGE:], shifted], axis=1)
        c3[:, here] = dot(w_cv[...], bb[0 : TAPS * H, here])

        def step(i):
            lanes = lanes_at(chunk * CW + i * LG)
            mean, scaled = mu2[:, lanes], sc2[:, lanes]
            first, second = jnp.zeros((8, LG), F32), jnp.zeros((8, LG), F32)
            for f in blocks(H):
                normed = (h2[f, lanes] - mean) * scaled
                gain = dup(p4[0, f], LG)
                pre = normed * gain + dup(p4[1, f], LG)
                t = jnp.tanh(pre)
                upstream = c3[f, lanes] * ((1.0 + t) * (1.0 + pre * (1.0 - t)))
                acc4[0, f] += fold_lanes(upstream * normed)
                acc4[1, f] += fold_lanes(upstream)
                upstream = upstream * gain
                c3[f, lanes] = upstream
                first += fold_rows(upstream)
                second += fold_rows(upstream * normed)
            first, second = total_rows(first) * (1.0 / H), total_rows(second) * (1.0 / H)
            for f in blocks(H):
                normed = (h2[f, lanes] - mean) * scaled
                grad = (scaled * (c3[f, lanes] - first - normed * second)).astype(BF16)
                gh[f, lanes] = grad

        loop(CW // LG, step)

    second_back(0)
    second_back(1)
    big[0 : D + 16, 0:H] = dot(a1[...], gh[...], (1, 1))
    pack_grad("in")
    reduce("in", 1)
    keep_row(7, big[D : D + 1, 0:H])
    reduce("out", 3)

    def sums_rows(indices):
        for index in indices:
            (group, i, _, scale), _ = vec_at[index]
            keep_row(index, jnp.sum((acc8 if group == 8 else acc4)[i].T, 0, keepdims=True) * scale)

    def sums_plane(rows):
        vr[c, rows] = vx[rows]
        there = vr.at[c, rows]
        return copies.start([(there, there, (flip(c, m), z)) for m in range(1, C)], vr.at[pl.ds(0, C - 1), rows])

    def sums_column(rows, before):
        before.wait()
        total = vr[0, rows]
        for m in range(1, C):
            total = total + vr[m, rows]
        vs[rows] = total
        return copies.start([(vs.at[rows], vz.at[d, rows], planes[d]) for d in range(W - 1)], vz.at[:, rows])

    def sums_end(rows, before):
        before.wait()
        total = vs[rows]
        for d in range(W - 1):
            total = total + vz[d, rows]
        vo_ref[rows] = total

    late, early = slice(0, cfg["v_late"]), slice(cfg["v_late"], cfg["v_rows"])
    sums_rows((3, 4, 5, 6))
    v_early = sums_plane(early)
    for side in range(D // H):
        w_cvT[:, side * 512 : side * 512 + H] = w_out[:, side * H : (side + 1) * H].T

    def first_back(chunk):
        here = slice(chunk * CW, (chunk + 1) * CW)
        big[0:D, here] = dot(w_in[...], gh[:, here])

        def step(i):
            lanes = lanes_at(chunk * CW + i * LG)
            mean, scaled = mu1[:, lanes], sc1[:, lanes]
            first, second = jnp.zeros((8, LG), F32), jnp.zeros((8, LG), F32)
            for f in blocks(D):
                normed = (x_v[f, lanes].astype(F32) - mean) * scaled
                gain = dup(p8[0, f], LG)
                pre = normed * gain + dup(p8[1, f], LG)
                t = jnp.tanh(pre)
                upstream = big[f, lanes] * ((1.0 + t) * (1.0 + pre * (1.0 - t)))
                acc8[0, f] += fold_lanes(upstream * normed)
                acc8[1, f] += fold_lanes(upstream)
                upstream = upstream * gain
                big[f, lanes] = upstream
                first += fold_rows(upstream)
                second += fold_rows(upstream * normed)
            first, second = total_rows(first) * (1.0 / D), total_rows(second) * (1.0 / D)
            for f in blocks(D):
                normed = (x_v[f, lanes].astype(F32) - mean) * scaled
                grad = scaled * (big[f, lanes] - first - normed * second)
                big[f, lanes] = og_v[f, lanes].astype(F32) + grad

        loop(CW // LG, step)
        return local(chunk, big.at[0:D, here], ig_hbm.at[:, here])

    def last(chunk):
        here = slice(chunk * CW, (chunk + 1) * CW)
        for side, store in enumerate((c3, g3)):
            store[:, 0:CW] = dot(w_cvT[:, side * 512 : side * 512 + H], a3[0:H, here])

            def step(i, side=side, store=store):
                lanes, at = lanes_at(chunk * CW + i * LG), lanes_at(i * LG)
                for f in blocks(H):
                    to = slice(side * H + f.start, side * H + f.stop)
                    value = store[f, at] + dup(p8[2, to], LG)
                    x_v[to, lanes] = (x_v[to, lanes].astype(F32) + value).astype(BF16)

            loop(CW // LG, step)
        return local(2 + chunk, x_v.at[:, here], bo_hbm.at[:, here])

    def leave(n, name):
        going[name].wait()
        form, base = forms[name], bases[name]
        if name == "in":
            rows = pl.ds(base, form.size)
            return local(n, fo.at[rows], fo_hbm)
        for start, count, panels in form.plain_spans():
            values = [
                [fo[base + row : base + row + count, lane : lane + columns].astype(F32) for row, lane, columns in panel]
                for panel in panels
            ]
            for at, value in zip(cfg["small_at"][name], values if name == "conv" else [sum(values, [])]):
                value = jnp.concatenate(value, axis=1)
                h2[start : start + count, at : at + value.shape[1]] = value
        first, last_lane = cfg["small_at"][name][0], cfg["small_end"][name]
        return local(n, h2.at[:, first:last_lane], sm_hbm.at[:, first:last_lane])

    out_copies = [first_back(0)]
    reduce("in", 2)
    reduce("conv", 3)
    out_copies.append(first_back(1))
    sums_rows((0, 1))
    v_late = sums_plane(late)
    reduce("in", 3)
    v_early = sums_column(early, v_early)
    reduce("conv", 4)
    out_copies.append(last(0))
    v_late = sums_column(late, v_late)
    reduce("out", 4)
    out_copies.append(last(1))
    reduce("in", 4)
    reduce("conv", 5)
    out_copies.append(leave(4, "out"))
    sums_end(early, v_early)
    out_copies.append(leave(5, "conv"))
    reduce("in", 5)
    sums_end(late, v_late)
    out_copies.append(leave(6, "in"))
    for group in copies.groups:
        group.wait_sent()
    for copy in out_copies:
        copy.wait()


def spread(cfg, *refs):
    W, forms, bases, width, vec_at = (cfg[key] for key in ("W", "forms", "bases", "width", "vec_at"))
    bo_in, ig_in, fo_in, sm_in, vx_in, bo_out, ig_out, gi_out, gc_out, go_out = refs[:10]
    vec_out, (ig_v, bo_v, fo, sm, vx, gi, gc, go), vec_v, sem = refs[10:19], refs[19:27], refs[27:36], refs[36]
    z = lax.axis_index("wsh")
    used = 0

    def copy(source, target):
        nonlocal used
        used += 1
        move = pltpu.make_async_copy(source, target, sem.at[used - 1])
        move.start()
        return move

    early, pieces, moves = [], [], []
    for source, stage, target in ((ig_in, ig_v, ig_out), (bo_in, bo_v, bo_out)):
        size = source.shape[0] // SPREAD
        for i in range(SPREAD):
            rows = pl.ds(i * size, size)
            pieces.append((copy(source.at[rows], stage.at[rows]), stage.at[rows], target.at[rows]))
        if not early:
            early = [copy(fo_in, fo), copy(sm_in, sm), copy(vx_in, vx)]

    def pass_on(count):
        for come, stage, target in pieces[:count]:
            come.wait()
            moves.append(copy(stage, target))
        del pieces[:count]

    pass_on(SPREAD)
    early[0].wait()
    form, parts = forms["in"], []
    for _, count, panels in form.plain_spans():
        values = [fo[row : row + count, lane : lane + columns] for panel in panels for row, lane, columns in panel]
        parts.append(jnp.concatenate(values, axis=1))
    gi[...] = jnp.concatenate(parts, axis=0).astype(F32).T
    moves.append(copy(gi, gi_out))
    pass_on(SPREAD)
    early[1].wait()
    for tap, at in enumerate(cfg["small_at"]["conv"]):
        gc[tap] = sm[:, at : at + width]
    at = cfg["small_at"]["out"][0]
    go[...] = sm[:, at : at + go.shape[1]]
    moves += [copy(gc, gc_out), copy(go, go_out)]
    early[2].wait()
    for ((_, _, count, _), at), stage, target in zip(vec_at, vec_v, vec_out):
        whole = jnp.concatenate([vx[at + t : at + t + 1] for t in range(-(-count // LANES))], axis=1)
        share = count // W
        mine = jnp.zeros((1, share), F32)
        for s in range(W):
            mine = jnp.where(z == s, whole[:, s * share : (s + 1) * share], mine)
        stage[...] = mine.reshape(share)
        moves.append(copy(stage, target))
    for move in moves:
        move.wait()


def on_device(
    block_in, out_grad, segments, block_deal, weight_in, weight_conv, weight_out,
    gain_first, shift_first, gain_second, shift_second, gain_third, shift_third, bias_first, bias_conv, bias_out,
):
    C, W = lax.axis_size("ctx"), lax.axis_size("wsh")
    _, rows, D = block_in.shape
    width = weight_in.shape[1]
    H = width * W
    panels = weight_out.shape[1] // width
    J = rows // BLK
    forms = {
        "in": Packed(D, 1, width, C),
        "conv": Packed(H, TAPS, width, C),
        "out": Packed(H, panels, width, C),
    }
    bases, total = {}, 0
    for name, form in forms.items():
        bases[name] = total
        total += form.size

    items = [(8, 0, D, 0.5), (8, 1, D, 0.5), (None, 0, D, 1.0)]
    items += [(4, i, H, 0.5) if i < 4 else (None, 0, H, 1.0) for i in range(6)]
    vec_at, at = [], 0
    for n, item in enumerate(items):
        if n == 2:
            at = v_late = up(at, 8)
        vec_at.append((item, at))
        at += -(-item[2] // LANES)
    v_rows = up(at, 8)
    cfg = {
        "C": C, "W": W, "J": J, "D": D, "H": H, "forms": forms, "bases": bases, "width": width, "vec_at": vec_at,
    }
    cfg["z_first"] = ("out",) if C <= 8 else ()
    cfg["spans"] = {name: (bases[name], form.size) for name, form in forms.items()}
    straight = forms["in"].size * 2 // 5
    if C <= 8 and straight % 32 == 0 and (forms["in"].size - straight) % (16 * C) == 0:
        cfg["in_spans"] = ("in_shared", "in_straight")
        cfg["spans"]["in_straight"] = (bases["in"], straight)
        cfg["spans"]["in_shared"] = (bases["in"] + straight, forms["in"].size - straight)
    else:
        cfg["in_spans"] = ("in",)
    cfg["z_only"] = ("out", "in_straight")
    cfg["small_at"] = {"conv": [tap * up(width, LANES) for tap in range(TAPS)], "out": [TAPS * up(width, LANES)]}
    small = cfg["small_at"]["out"][0] + up(panels * width, LANES)
    cfg["small_end"] = {"conv": cfg["small_at"]["out"][0], "out": small}
    cfg["direct"] = ("in",) if C <= 8 else ()
    cfg["v_late"], cfg["v_rows"] = v_late, v_rows
    cfg["rz_at"], rz_rows = {}, 0
    for name in cfg["z_first"]:
        cfg["rz_at"][name] = rz_rows
        rz_rows += forms[name].size // 2
    rz_rows = max(rz_rows, 16)
    R = rows
    others = max(C // 2 - 1, 1)
    n_groups = 4 * 3 + 2 + 2 * 6 * CHUNKS + 3 * 5 + 4
    vmem = pltpu.VMEM
    scratch = [
        vmem((D, R), BF16),
        vmem((D, R), BF16),
        vmem((1, R), F32),
        vmem((1, R), F32),
        vmem((D + 16, R), BF16),
        vmem((H, R), F32),
        vmem((1, R), F32),
        vmem((1, R), F32),
        vmem((TAPS * H + 16, R), BF16),
        vmem((H + 16, R), BF16),
        vmem((H, R), BF16),
        vmem((H, R), BF16),
        vmem((D + 16, R), F32),
        vmem((H, R), F32),
        vmem((H, R), F32),
        vmem((16, R), BF16),
        vmem((16, R), BF16),
        vmem((16, J * EDGE), BF16),
        vmem((16, J * EDGE), BF16),
        vmem((D, H), BF16),
        vmem((H, D), BF16),
        vmem((H, TAPS * H), BF16),
        vmem((H, max(up(TAPS * H, LANES), 512 * (D // H))), BF16),
        vmem((H, D), BF16),
        vmem((W, total, LANES), BF16),
        vmem((W, 16, LANES), BF16),
        vmem((J * C, BLK), jnp.int32),
        vmem((2, C // 2, H, J * EDGE), BF16),
        vmem((2, C // 2, H, J * EDGE), BF16),
        vmem((H, J * EDGE), BF16),
        vmem((H, J * EDGE), BF16),
        vmem((W, total, LANES), BF16),
        vmem((W, total // 2, LANES), BF16),
        vmem((others, W, total // C, LANES), BF16),
        vmem((W, total // C, LANES), BF16),
        vmem((W - 1, total // C, LANES), BF16),
        vmem((W - 1, rz_rows, LANES), BF16),
        vmem((C // 2 if cfg["z_first"] else 1, rz_rows, LANES), BF16),
        vmem((total, LANES), BF16),
        vmem((3, D, LANES), F32),
        vmem((6, H, LANES), F32),
        vmem((2, D, LANES), F32),
        vmem((4, H, LANES), F32),
        vmem((v_rows, LANES), F32),
        vmem((C, v_rows, LANES), F32),
        vmem((v_rows, LANES), F32),
        vmem((W - 1, v_rows, LANES), F32),
        vmem((width, D), BF16),
        vmem((TAPS, H, width), BF16),
        vmem((H, panels * width), BF16),
        *[vmem((n // W,), BF16) for n in (D, D, H, H, H, H, H, H, D)],
        pltpu.SemaphoreType.DMA((15,)),
        pltpu.SemaphoreType.DMA((n_groups,)),
        pltpu.SemaphoreType.DMA((n_groups,)),
    ]
    any_spec = pl.BlockSpec(memory_space=pl.ANY)
    vmem_spec = pl.BlockSpec(memory_space=pltpu.VMEM)
    flat, tree = jax.tree.flatten(scratch)

    def run(*refs):
        kernel(cfg, *refs[:21], *jax.tree.unflatten(tree, refs[21:]))

    macs = R * (2 * D * H + TAPS * H * H) * 3
    bo, ig, fo, sm, vo = pl.pallas_call(
        run,
        out_shape=(
            jax.ShapeDtypeStruct((D, R), BF16),
            jax.ShapeDtypeStruct((D, R), F32),
            jax.ShapeDtypeStruct((forms["in"].size, LANES), BF16),
            jax.ShapeDtypeStruct((H, small), F32),
            jax.ShapeDtypeStruct((v_rows, LANES), F32),
        ),
        in_specs=[pl.BlockSpec(memory_space=pltpu.SMEM)] + [any_spec] * 15,
        out_specs=(any_spec, any_spec, any_spec, any_spec, vmem_spec),
        scratch_shapes=flat,
        compiler_params=pltpu.CompilerParams(
            collective_id=0, has_side_effects=True, vmem_limit_bytes=62 * 2**20
        ),
        cost_estimate=pl.CostEstimate(
            flops=2 * macs, bytes_accessed=10 * R * D, transcendentals=2 * R * (D + 2 * H)
        ),
        name="block",
    )(
        block_deal,
        block_in[0].T,
        out_grad[0].T,
        segments.reshape(J, BLK),
        weight_in.T,
        weight_conv,
        weight_out,
        gain_first, shift_first, gain_second, shift_second, gain_third, shift_third, bias_first, bias_conv, bias_out,
    )
    results = pl.pallas_call(
        lambda *refs: spread(cfg, *refs),
        out_shape=(
            jax.ShapeDtypeStruct((D, R), BF16),
            jax.ShapeDtypeStruct((D, R), F32),
            jax.ShapeDtypeStruct((width, D), F32),
            jax.ShapeDtypeStruct((TAPS, H, width), F32),
            jax.ShapeDtypeStruct((H, panels * width), F32),
        )
        + tuple(jax.ShapeDtypeStruct((item[2] // W,), F32) for item, _ in vec_at),
        in_specs=[any_spec] * 5,
        out_specs=(any_spec,) * 14,
        scratch_shapes=[
            vmem((D, R), F32), vmem((D, R), BF16), vmem((forms["in"].size, LANES), BF16), vmem((H, small), F32),
            vmem((v_rows, LANES), F32), vmem((width, D), F32), vmem((TAPS, H, width), F32),
            vmem((H, panels * width), F32), *[vmem((item[2] // W,), F32) for item, _ in vec_at],
            pltpu.SemaphoreType.DMA((4 * SPREAD + 15,)),
        ],
        compiler_params=pltpu.CompilerParams(vmem_limit_bytes=62 * 2**20),
        cost_estimate=pl.CostEstimate(flops=0, bytes_accessed=14 * R * D, transcendentals=0),
        name="spread",
    )(bo, ig, fo, sm, vo)
    bo, ig, gi, gc, go = results[:5]
    vec = results[5:]
    return (bo.T[None], ig.T[None], gi.T, gc, go, vec[0], vec[1], *vec[3:], vec[2])


def solution(mesh):
    in_specs = (
        P("wsh", "ctx", None), P("wsh", "ctx", None), P("wsh", "ctx"), P(),
        P(None, "wsh"), P(None, None, "wsh"), P(None, "wsh"),
    ) + (P("wsh"),) * 9
    out_specs = (
        P("wsh", "ctx", None), P("wsh", "ctx", None),
        P(None, "wsh"), P(None, None, "wsh"), P(None, "wsh"),
    ) + (P("wsh"),) * 9
    return jax.shard_map(
        on_device, mesh=mesh, in_specs=in_specs, out_specs=out_specs, check_vma=False
    )
```
